32 devices in a mesh: seq: 4 (over y, x), batch: 8 (over z, core).
Axes of the slice: x: 2, y: 2, z: 4, core: 2. Of those that a mesh axis runs over, the one named last changes fastest.
Arguments:
- tokens: bfloat16 [8, 512, 768], P('batch', 'seq'), may hold values from -6 to 6
- segments: int32 [8, 512], P('batch'), may hold values from 0 to 5, as said below
- ln1_gain: float32 [768], replicated, may hold values from 0.1 to 1.9
- ln1_bias: float32 [768], replicated, may hold values from -3 to 3
- w_qkv: bfloat16 [768, 2304], replicated, may hold values from -0.3125 to 0.3125
- bias_qv: float32 [1536], replicated, may hold values from -3 to 3
- w_out: bfloat16 [768, 768], replicated, may hold values from -0.875 to 0.875
- bias_out: float32 [768], replicated, may hold values from -3 to 3
- ln2_gain: float32 [768], replicated, may hold values from 0.1 to 1.9
- ln2_bias: float32 [768], replicated, may hold values from -3 to 3
- w_in: bfloat16 [768, 3072], replicated, may hold values from -0.21875 to 0.21875
- bias_in: float32 [3072], replicated, may hold values from -3 to 3
- w_down: bfloat16 [3072, 768], replicated, may hold values from -0.109375 to 0.109375
- bias_down: float32 [768], replicated, may hold values from -3 to 3
- cotangent: bfloat16 [8, 512, 768], P('batch', 'seq'), may hold values from -6 to 6
Outputs:
- activations: bfloat16 [8, 512, 768], P('batch', 'seq')
- d_tokens: float32 [8, 512, 768], P('batch', 'seq')
- d_ln1_gain: float32 [768], P('batch')
- d_ln1_bias: float32 [768], P('batch')
- d_w_qkv: float32 [768, 2304], P('batch')
- d_bias_qv: float32 [1536], P('batch')
- d_w_out: float32 [768, 768], P('batch')
- d_bias_out: float32 [768], P('batch')
- d_ln2_gain: float32 [768], P('batch')
- d_ln2_bias: float32 [768], P('batch')
- d_w_in: float32 [768, 3072], P('batch')
- d_bias_in: float32 [3072], P('batch')
- d_w_down: float32 [3072, 768], P('batch')
- d_bias_down: float32 [768], P('batch')
The draws below stay inside these ranges and needn't reach their ends.
Inputs may be any that keep to these rules, and one draw needn't show every extreme that they name: `segments`: each row holds exactly six documents, numbered 0 to 5 in order (ids never fall); document 2 starts in the first quarter of the row and ends in its last quarter.
All inputs are finite; a program needn't handle non-finite values.
Results may differ from the reference program's by a relative error of at most 0.012.
The reference program's roundings to bfloat16 on the way count: a program that leaves them out, or rounds other values in their place, can miss the bound.
Values may be sent and summed in bfloat16 or wider, within the bound.
No kernel may reach another device: no remote copies, remote signals or barrier semaphores. Data moves between devices by JAX's collectives and lax.ppermute only.
A program may use at most 128 MiB of HBM per device.

```python
import math
import jax
import jax.numpy as jnp
from jax import lax

D = 768
HEADS = 12
HEAD_DIM = 64
FF = 3072
SEQLEN = 512
ROWS = 8


def draw_segments(key, part):
    key = jax.random.fold_in(key, 11)
    key_start, key_end, key_first, key_fourth, key_fifth = jax.random.split(key, 5)
    start = jax.random.randint(key_start, (ROWS, 1), 2, SEQLEN // 4)
    finish = jax.random.randint(key_end, (ROWS, 1), 3 * SEQLEN // 4, SEQLEN - 4)
    first_cut = jax.random.randint(key_first, (ROWS, 1), 1, start)
    fourth_cut = jax.random.randint(key_fourth, (ROWS, 1), finish + 2, SEQLEN - 1)
    fifth_cut = jax.random.randint(key_fifth, (ROWS, 1), fourth_cut + 1, SEQLEN)
    places = jnp.arange(SEQLEN, dtype=jnp.int32)[None, :]
    ids = (places >= first_cut).astype(jnp.int32)
    ids = ids + (places >= start).astype(jnp.int32)
    ids = ids + (places >= finish + 1).astype(jnp.int32)
    ids = ids + (places >= fourth_cut).astype(jnp.int32)
    ids = ids + (places >= fifth_cut).astype(jnp.int32)
    return ids.astype(jnp.int32)


def block_scale(key, shape, shards, low, high):
    def one(axis_at, shards_of):
        draws = jax.random.uniform(jax.random.fold_in(jax.random.fold_in(key, 6), axis_at), (shards_of,), jnp.float32, low / len(shards), high / len(shards))
        return jnp.repeat(jnp.exp(draws), shape[axis_at] // shards_of).reshape((-1,) + (1,) * (len(shape) - axis_at - 1))

    level = one(*shards[0])
    for cut in shards[1:]:
        level = level * one(*cut)
    return level


def scatter_about(stream_key, dims, deviation, limit, pieces=(), kind=jnp.bfloat16):
    factor_of = block_scale(stream_key, dims, pieces, -0.22, 0.18) if pieces else 1.0
    entries = jax.random.normal(stream_key, dims, jnp.float32) * deviation * factor_of
    return jnp.minimum(jnp.maximum(entries, -limit), limit).astype(kind)


def setup_inputs(seed: int = 0) -> dict:
    key_of = jax.random.split(jax.random.key(seed), 16)
    return {
        "tokens": scatter_about(key_of[0], (ROWS, SEQLEN, D), 1.0, 6.0, ((0, 8), (1, 4))),
        "segments": draw_segments(jax.random.fold_in(key_of[15], 71), 0),
        "ln1_gain": jnp.clip(1.0 + 0.18 * jax.random.normal(key_of[2], (D,), jnp.float32), 0.1, 1.9),
        "ln1_bias": scatter_about(key_of[3], (D,), 0.5, 3.0, (), jnp.float32),
        "w_qkv": scatter_about(key_of[4], (D, 3 * D), (D // 2) ** -0.5, 0.3125),
        "bias_qv": scatter_about(key_of[5], (2 * D,), 0.5, 3.0, (), jnp.float32),
        "w_out": scatter_about(key_of[6], (D, D), (D // 16) ** -0.5, 0.875),
        "bias_out": scatter_about(key_of[7], (D,), 0.5, 3.0, (), jnp.float32),
        "ln2_gain": jnp.clip(1.0 + 0.18 * jax.random.normal(key_of[8], (D,), jnp.float32), 0.1, 1.9),
        "ln2_bias": scatter_about(key_of[9], (D,), 0.5, 3.0, (), jnp.float32),
        "w_in": scatter_about(key_of[10], (D, FF), D ** -0.5, 0.21875),
        "bias_in": scatter_about(key_of[11], (FF,), 0.5, 3.0, (), jnp.float32),
        "w_down": scatter_about(key_of[12], (FF, D), FF ** -0.5, 0.109375),
        "bias_down": scatter_about(key_of[13], (D,), 0.5, 3.0, (), jnp.float32),
        "cotangent": scatter_about(key_of[14], (ROWS, SEQLEN, D), 1.0, 6.0, ((0, 8), (1, 4))),
    }


@jax.custom_vjp
def low(v):
    return lax.optimization_barrier(v.astype(jnp.bfloat16)).astype(jnp.float32)

@jax.custom_vjp
def low_back(v):
    return v

def low_keep(v):
    return (low(v), None)

def low_pass(kept, grad):
    return (grad,)

def back_keep(v):
    return (v, None)

def back_low(kept, grad):
    return (low(grad),)
low.defvjp(low_keep, low_pass)
low_back.defvjp(back_keep, back_low)
HIGH = lax.Precision.HIGHEST

def layer_norm(values, gain, shift):
    mean = lax.optimization_barrier(jnp.mean(values, axis=-1, keepdims=True))
    centred = values - mean
    var = lax.optimization_barrier(jnp.mean(centred * centred, axis=-1, keepdims=True))
    return centred * lax.rsqrt(var + 1e-06) * gain + shift

def block_forward(x, seg, ln1_gain, ln1_bias, w_qkv, bias_qv, w_out, bias_out, ln2_gain, ln2_bias, w_in, bias_in, w_down, bias_down):
    count, length, width = x.shape
    h1 = low(layer_norm(x, ln1_gain, ln1_bias))
    bias_all = jnp.concatenate([bias_qv[:width], jnp.zeros((width,), bias_qv.dtype), bias_qv[width:]])
    qkv = jnp.einsum('gsd,de->gse', h1, w_qkv, precision=HIGH) + bias_all
    qkv = low(low_back(qkv)).reshape(count, length, 3, HEADS, HEAD_DIM)
    query, keys, values = (qkv[:, :, 0], qkv[:, :, 1], qkv[:, :, 2])
    scores = low_back(jnp.einsum('gqhd,gkhd->ghqk', query, keys, precision=HIGH) * HEAD_DIM ** (-0.5))
    mask = seg[:, None, :, None] == seg[:, None, None, :]
    scores = jnp.where(mask, scores, -1e+30)
    top = lax.optimization_barrier(jnp.max(scores, axis=-1, keepdims=True))
    expo = jnp.exp(scores - top)
    probs = low(expo / lax.optimization_barrier(jnp.sum(expo, axis=-1, keepdims=True)))
    attn = jnp.einsum('ghqk,gkhd->gqhd', probs, values, precision=HIGH).reshape(count, length, width)
    attn = low(low_back(attn))
    branch = low_back(jnp.einsum('gsd,de->gse', attn, w_out, precision=HIGH) + bias_out)
    x1 = x + branch
    h2 = low(layer_norm(x1, ln2_gain, ln2_bias))
    hidden = low_back(jnp.einsum('gsd,df->gsf', h2, w_in, precision=HIGH) + bias_in)
    act = low(jax.nn.gelu(hidden, approximate=True))
    mixed = low_back(jnp.einsum('gsf,fd->gsd', act, w_down, precision=HIGH) + bias_down)
    return x1 + mixed

def reference(tokens, segments, ln1_gain, ln1_bias, w_qkv, bias_qv, w_out, bias_out, ln2_gain, ln2_bias, w_in, bias_in, w_down, bias_down, cotangent):
    params = tuple((p.astype(jnp.float32) for p in (ln1_gain, ln1_bias, w_qkv, bias_qv, w_out, bias_out, ln2_gain, ln2_bias, w_in, bias_in, w_down, bias_down)))
    total_rows = tokens.shape[0]
    per_step = math.gcd(total_rows, max(1, 4096 // SEQLEN))
    steps_count = total_rows // per_step
    xs = tokens.astype(jnp.float32).reshape(steps_count, per_step, SEQLEN, D)
    cots = cotangent.astype(jnp.float32).reshape(steps_count, per_step, SEQLEN, D)
    segs = segments.reshape(steps_count, per_step, SEQLEN)

    def step(carry, inputs):
        x_block, seg_block, cot_block = inputs

        def forward(xx, *ps):
            return block_forward(xx, seg_block, *ps)
        out_block, back = jax.vjp(forward, x_block, *params)
        grads = back(cot_block)
        carry = tuple((c + g for c, g in zip(carry, grads[1:])))
        return (carry, (out_block, grads[0]))
    start = tuple((jnp.zeros(p.shape, jnp.float32) for p in params))
    sums, (outs, dxs) = lax.scan(step, start, (xs, segs, cots))
    activations = outs.reshape(total_rows, SEQLEN, D).astype(jnp.bfloat16)
    d_tokens = dxs.reshape(total_rows, SEQLEN, D)
    return (activations, d_tokens, sums[0], sums[1], sums[2], sums[3], sums[4], sums[5], sums[6], sums[7], sums[8], sums[9], sums[10], sums[11])
```

```python
import jax
import jax.numpy as jnp
from jax import lax
from jax.sharding import PartitionSpec as P

HEADS = 12
HEAD_DIM = 64
BF = jnp.bfloat16
F32 = jnp.float32


def dot(a, b, dims=((1,), (0,))):
    return lax.dot_general(a, b, (dims, ((), ())), preferred_element_type=F32)


def exchange(value, axis, size, step):
    return lax.ppermute(value, axis, [(j, j ^ step) for j in range(size)])


def gather_seq(value, size):
    return [value] + [exchange(value, "seq", size, k) for k in range(1, size)]


def norm_parts(values):
    mean = jnp.mean(values, axis=-1, keepdims=True)
    centred = values - mean
    var = jnp.mean(centred * centred, axis=-1, keepdims=True)
    scale = lax.rsqrt(var + 1e-06)
    return centred * scale, scale


def norm_back(grad, unit, scale, gain):
    grad = grad * gain
    mean = jnp.mean(grad, axis=-1, keepdims=True)
    along = jnp.mean(grad * unit, axis=-1, keepdims=True)
    return (grad - mean - unit * along) * scale


def gelu_both(v):
    c = 0.7978845608028654
    inner = c * (v + 0.044715 * v * v * v)
    t = jnp.tanh(inner)
    value = 0.5 * v * (1.0 + t)
    slope = 0.5 * (1.0 + t) + 0.5 * v * (1.0 - t * t) * c * (1.0 + 3.0 * 0.044715 * v * v)
    return value, slope


def make(S, NB):
    def shards(tokens, segments, ln1_gain, ln1_bias, w_qkv, bias_qv, w_out, bias_out,
               ln2_gain, ln2_bias, w_in, bias_in, w_down, bias_down, cotangent):
        rows, t, D = tokens.shape
        FF = w_in.shape[1]
        L = t * S
        hs = HEADS // S
        cs = hs * HEAD_DIM
        R = D // NB
        FJ = FF // (NB * S)
        scale = HEAD_DIM ** (-0.5)
        s = lax.axis_index("seq")
        b = lax.axis_index("batch")
        rel_s = jnp.arange(S, dtype=jnp.int32) ^ s
        rel_b = jnp.arange(NB, dtype=jnp.int32) ^ b

        x_own = tokens.reshape(t, D)
        cot_own = cotangent.reshape(t, D)
        wq_s = lax.dynamic_slice_in_dim(w_qkv.reshape(D, 3, S, cs), s, 1, 2).reshape(D, 3 * cs)
        bq_s = lax.dynamic_slice_in_dim(bias_qv.reshape(2, S, cs), s, 1, 1).reshape(2, cs)
        bqkv_s = jnp.concatenate([bq_s[0], jnp.zeros((cs,), F32), bq_s[1]])
        win_s = lax.dynamic_slice_in_dim(w_in.reshape(D, NB, S, FJ), s, 1, 2).reshape(D, NB * FJ)
        bin_s = lax.dynamic_slice_in_dim(bias_in.reshape(NB, S, FJ), s, 1, 1).reshape(NB * FJ)
        wdn_s = lax.dynamic_slice_in_dim(w_down.reshape(NB, S, FJ, D), s, 1, 1).reshape(NB * FJ, D)
        wout_rel = jnp.take(w_out.reshape(S, cs, D), rel_s, axis=0).reshape(D, D)
        seg_rel = jnp.take(segments.reshape(S, t), rel_s, axis=0).reshape(L)

        x_all = jnp.concatenate(gather_seq(x_own, S), 0)
        cot_in, x_all = lax.optimization_barrier((cot_own, x_all))
        cot_all = jnp.concatenate(gather_seq(cot_in, S), 0)

        x_f = x_all.astype(F32)
        unit1, scale1 = norm_parts(x_f)
        h1 = (unit1 * ln1_gain + ln1_bias).astype(BF)
        qkv = (dot(h1, wq_s) + bqkv_s).astype(BF)
        q = qkv[:, :cs].reshape(L, hs, HEAD_DIM)
        k = qkv[:, cs:2 * cs].reshape(L, hs, HEAD_DIM)
        v = qkv[:, 2 * cs:].reshape(L, hs, HEAD_DIM)
        mask = seg_rel[:, None] == seg_rel[None, :]
        scores = jnp.einsum("qhd,khd->hqk", q, k, preferred_element_type=F32) * scale
        scores = jnp.where(mask[None], scores, -1e30)
        top = jnp.max(scores, axis=-1, keepdims=True)
        expo = jnp.exp(scores - top)
        total = jnp.sum(expo, axis=-1, keepdims=True)
        probs = expo / total
        probs_low = probs.astype(BF)
        attn = jnp.einsum("hqk,khd->qhd", probs_low, v, preferred_element_type=F32).reshape(L, cs).astype(BF)

        got = gather_seq(attn, S)
        blocks = []
        for m, g in enumerate(got):
            g4 = g.reshape(S, t, cs)
            blocks.append(jnp.concatenate([g4[kk ^ m] for kk in range(S)], 0))
        attn_all = jnp.concatenate(blocks, 1)

        x1 = x_f + dot(attn_all, wout_rel) + bias_out
        unit2, scale2 = norm_parts(x1)
        h2 = (unit2 * ln2_gain + ln2_bias).astype(BF)

        u_s = dot(h2, win_s) + bin_s
        act_s, slope_s = gelu_both(u_s)
        act_s = act_s.astype(BF)
        dact_s = dot(cot_all, wdn_s, ((1,), (1,)))
        du_s = (dact_s * slope_s).astype(BF)
        g_win = dot(h2, du_s, ((0,), (0,)))
        g_wdn = dot(act_s, cot_all, ((0,), (0,)))
        g_bin = jnp.sum(du_s.astype(F32), 0)
        mlp = jnp.concatenate([g_win.reshape(NB, R, NB * FJ), g_wdn.reshape(NB, FJ, D)], 1).astype(BF)

        h2o = h2[:t]
        u = dot(h2o, w_in) + bias_in
        act, slope = gelu_both(u)
        act = act.astype(BF)
        activations = (x1[:t] + dot(act, w_down) + bias_down).astype(BF)
        dy = cot_own.astype(F32)
        du = (dot(cot_own, w_down, ((1,), (1,))) * slope).astype(BF)
        dh2 = dot(du, w_in, ((1,), (1,)))
        g_ln2g = jnp.sum(dh2 * unit2[:t], 0)
        g_ln2b = jnp.sum(dh2, 0)
        dx1 = dy + norm_back(dh2, unit2[:t], scale2[:t], ln2_gain)
        da = dx1.astype(BF)
        g_bout = jnp.sum(da.astype(F32), 0)
        g_bdn = jnp.sum(dy, 0)
        dattn = dot(da, wout_rel, ((1,), (1,))).astype(BF)
        da_rel = jnp.take(da.reshape(t, S, cs), rel_s, axis=1)
        both = [jnp.concatenate([dattn[:, kk * cs:(kk + 1) * cs], da_rel[:, kk]], 1) for kk in range(S)]
        both = jnp.concatenate([both[0]] + [exchange(both[kk], "seq", S, kk) for kk in range(1, S)], 0)
        dattn_all = both[:, :cs].reshape(L, hs, HEAD_DIM)
        da_s = both[:, cs:]

        log_total = top + jnp.log(total)
        p = jnp.exp(scores - log_total)
        p_low = p.astype(BF)
        dp = jnp.einsum("qhd,khd->hqk", dattn_all, v, preferred_element_type=F32)
        inner = jnp.sum(p * dp, axis=-1, keepdims=True)
        ds = (p * (dp - inner)).astype(BF)
        dq = jnp.einsum("hqk,khd->qhd", ds, k, preferred_element_type=F32) * scale
        dk = jnp.einsum("hqk,qhd->khd", ds, q, preferred_element_type=F32) * scale
        dv = jnp.einsum("hqk,qhd->khd", p_low, dattn_all, preferred_element_type=F32)
        dqkv = jnp.concatenate([dq.reshape(L, cs), dk.reshape(L, cs), dv.reshape(L, cs)], 1).astype(BF)

        dh1_part = dot(dqkv, wq_s, ((1,), (1,)))
        g_ln1g = jnp.sum(dh1_part * unit1, 0)
        g_ln1b = jnp.sum(dh1_part, 0)
        dh1_low = dh1_part.astype(BF)
        dh1 = dh1_part[:t]
        for kk in range(1, S):
            dh1 = dh1 + exchange(dh1_low[kk * t:(kk + 1) * t], "seq", S, kk).astype(F32)
        d_tokens = (dx1 + norm_back(dh1, unit1[:t], scale1[:t], ln1_gain)).reshape(tokens.shape)

        g_wqkv = dot(h1, dqkv, ((0,), (0,)))
        g_wout = dot(attn_all, da_s, ((0,), (0,)))
        g_wout = jnp.take(g_wout.reshape(S, cs, cs), rel_s, axis=0).reshape(D, cs)
        bsum = jnp.sum(dqkv.astype(F32), 0)
        g_bqv = jnp.zeros((2, S, cs), F32)
        g_bqv = lax.dynamic_update_slice(g_bqv, jnp.stack([bsum[:cs], bsum[2 * cs:]])[:, None], (0, s, 0))
        small = jnp.concatenate(
            [v_.reshape(NB, -1) for v_ in (g_ln1g, g_ln1b, g_bqv, g_bout, g_ln2g, g_ln2b, g_bdn, g_bin)], 1)
        small_n = small.shape[1]
        small_rows = -(-small_n // D)
        pad_rows = -(-small_rows // 16) * 16
        small = jnp.pad(small, ((0, 0), (0, pad_rows * D - small_n))).reshape(NB, pad_rows, D)
        att = jnp.concatenate(
            [jnp.concatenate([g_wqkv.reshape(NB, R, 3 * cs), g_wout.reshape(NB, R, cs)], 2), small], 1).astype(BF)

        def reduce_batch(buf):
            buf = jnp.take(buf, rel_b, axis=0).reshape((NB // 2, 2) + buf.shape[1:])
            buf = (buf[:, 0].astype(F32) + exchange(buf[:, 1], "batch", NB, 1).astype(F32)).astype(BF)
            n = NB // 2
            while n > 4:
                n //= 2
                buf = (buf[:n].astype(F32) + exchange(buf[n:], "batch", NB, 2 * n).astype(F32)).astype(BF)
            acc = buf[0].astype(F32)
            for m in range(1, n):
                acc = acc + exchange(buf[m], "batch", NB, 2 * m).astype(F32)
            parts = jnp.stack(gather_seq(acc.astype(BF), S))
            return jnp.take(parts, rel_s, axis=0).astype(F32)

        mlp = reduce_batch(mlp)
        att = reduce_batch(att)
        o_win = mlp[:, :R].reshape(S, R, NB, FJ).transpose(1, 2, 0, 3).reshape(R, FF)
        o_wdn = mlp[:, R:].reshape(S * FJ, D)
        o_wqkv = att[:, :R, :3 * cs].reshape(S, R, 3, cs).transpose(1, 2, 0, 3).reshape(R, 3 * D)
        o_wout = att[:, :R, 3 * cs:].transpose(1, 0, 2).reshape(R, D)
        flat = att[:, R:].reshape(S, -1)
        o_bin = flat[:, 8 * R:8 * R + FJ].reshape(S * FJ)
        tot = jnp.sum(flat[:, :8 * R], 0)
        o_ln1g, o_ln1b, o_bqv, o_bout, o_ln2g, o_ln2b, o_bdn = (
            tot[:R], tot[R:2 * R], tot[2 * R:4 * R], tot[4 * R:5 * R], tot[5 * R:6 * R], tot[6 * R:7 * R], tot[7 * R:])
        return (activations.reshape(tokens.shape), d_tokens, o_ln1g, o_ln1b, o_wqkv, o_bqv, o_wout, o_bout,
                o_ln2g, o_ln2b, o_win, o_bin, o_wdn, o_bdn)
    return shards


def solution(mesh):
    rowwise = P("batch", "seq", None)
    placed = (rowwise, P("batch", None)) + (P(),) * 12 + (rowwise,)
    b, bn = P("batch"), P("batch", None)
    return jax.shard_map(
        make(mesh.shape["seq"], mesh.shape["batch"]),
        mesh=mesh,
        in_specs=placed,
        out_specs=(rowwise, rowwise, b, b, bn, b, bn, b, b, b, bn, b, bn, b),
        check_vma=False,
    )
```

```python
import functools

import jax
import jax.numpy as jnp
from jax import lax
from jax.experimental import pallas as pl
from jax.experimental.pallas import tpu as pltpu
from jax.sharding import PartitionSpec as P

HEADS = 12
HEAD_DIM = 64
BLOCK_ROWS = HEADS * HEAD_DIM
BF = jnp.bfloat16
F32 = jnp.float32
MIB = 1 << 20


def dot(a, b, ca=1, cb=0):
    return lax.dot_general(a, b, (((ca,), (cb,)), ((), ())), preferred_element_type=F32)


def exchange(value, axis, size, step):
    return lax.ppermute(value, axis, [(j, j ^ step) for j in range(size)])


def gather_seq(value, size):
    return [value] + [exchange(value, "seq", size, k) for k in range(1, size)]


def gather_steps(value, size, steps):
    arrays, ks = [value], [[0]]
    held = value[None]
    for step in steps:
        got = exchange(held, "seq", size, step)
        ks.append([k ^ step for part in ks for k in part])
        arrays.append(got)
        if step != steps[-1]:
            held = jnp.concatenate([held, got], 0)
    arrays = [a if len(k) > 1 else a.reshape(value.shape) for a, k in zip(arrays, ks)]
    return arrays, ks


def norm_parts(values):
    mean = jnp.mean(values, axis=-1, keepdims=True)
    centred = values - mean
    var = jnp.mean(centred * centred, axis=-1, keepdims=True)
    scale = lax.rsqrt(var + 1e-06)
    return centred * scale, scale


def norm_back(grad, unit, scale, gain):
    grad = grad * gain
    mean = jnp.mean(grad, axis=-1, keepdims=True)
    along = jnp.mean(grad * unit, axis=-1, keepdims=True)
    return (grad - mean - unit * along) * scale


def gelu_both(v):
    c = 0.7978845608028654
    square = v * v
    t = jnp.tanh(c * v * (1.0 + 0.044715 * square))
    half = 0.5 * (1.0 + t)
    slope = half + (0.5 * c) * v * (1.0 - t * t) * (1.0 + 3.0 * 0.044715 * square)
    return v * half, slope


def call(kernel, outs, args, name, flops=0, limit=24):
    size = sum(a.size * a.dtype.itemsize for a in args) + sum(o.size * o.dtype.itemsize for o in outs)
    return pl.pallas_call(
        kernel,
        out_shape=outs,
        name=name,
        cost_estimate=pl.CostEstimate(flops=flops, bytes_accessed=size, transcendentals=0),
        compiler_params=pltpu.CompilerParams(vmem_limit_bytes=limit * MIB),
    )(*args)


def sds(shape, dtype):
    return jax.ShapeDtypeStruct(shape, dtype)


def flat(ref):
    return ref[...].reshape(1, -1)


def make(S, NB):
    def rel_row(row, t):
        s = lax.axis_index("seq")
        parts = [row[:, i * t:(i + 1) * t] for i in range(S)]
        bit = 1
        while bit < S:
            on = (s & bit) != 0
            parts = [jnp.where(on, parts[i ^ bit], parts[i]) for i in range(S)]
            bit *= 2
        return jnp.concatenate(parts, 1)

    def prep_qkv_kernel(wqkv, pack, wq_o, bq_o, row_o, col_o):
        D = wqkv.shape[0]
        cs = D // S
        L = row_o.shape[1]
        s = lax.axis_index("seq")
        row = rel_row(pack[4:5, :L], L // S)
        row_o[...] = jnp.broadcast_to(row, row_o.shape)
        col_o[...] = jnp.transpose(jnp.broadcast_to(row, (128, L)))
        bq_o[0:2, :] = pack[0:2, :]
        for p in range(S):
            @pl.when(s == p)
            def _(p=p):
                for c in range(3):
                    wq_o[:, c * cs:(c + 1) * cs] = wqkv[:, c * D + p * cs:c * D + (p + 1) * cs]
                zero = jnp.zeros((1, cs), F32)
                bq_o[2:3, :] = jnp.concatenate(
                    [pack[2:3, p * cs:(p + 1) * cs], zero, pack[3:4, p * cs:(p + 1) * cs], zero], 1)

    def prep_mlp_kernel(win, wout, wdown, bout, ln2g, ln2b, bin_, bdown, win_o, wout_o, wdn_o, pack_o):
        D = wout.shape[0]
        FF = win.shape[1]
        cs = D // S
        FJ = FF // (NB * S)
        s = lax.axis_index("seq")
        vin = flat(bin_)
        pack_o[3:4, :] = flat(bout)
        pack_o[4:5, :] = flat(ln2g)
        pack_o[5:6, :] = flat(ln2b)
        pack_o[7:8, :] = flat(bdown)
        for c in range(FF // D):
            pack_o[8 + c:9 + c, :] = vin[:, c * D:(c + 1) * D]
        for m in range(S):
            wout_o[m * cs:(m + 1) * cs, :] = wout[pl.ds(pl.multiple_of((s ^ m) * cs, 16), cs), :]
        for i in range(NB):
            wdn_o[i * FJ:(i + 1) * FJ, :] = wdown[pl.ds(pl.multiple_of((i * S + s) * FJ, 16), FJ), :]
        for p in range(S):
            @pl.when(s == p)
            def _(p=p):
                for i in range(NB):
                    at = (i * S + p) * FJ
                    win_o[:, i * FJ:(i + 1) * FJ] = win[:, at:at + FJ]
                pack_o[6:7, :] = jnp.concatenate(
                    [vin[:, (i * S + p) * FJ:(i * S + p + 1) * FJ] for i in range(NB)], 1)

    def attn_fwd_kernel(*refs):
        xs, (row_ref, col_ref, pack, wq_ref, attn_o, qkv_o, lse_o) = refs[:S], refs[S:]
        t, D = xs[0].shape
        L = S * t
        cs = D // S
        for k in range(S):
            unit, _ = norm_parts(xs[k][...].astype(F32))
            h1 = (unit * pack[0:1, :] + pack[1:2, :]).astype(BF)
            qkv_o[k * t:(k + 1) * t, :] = (dot(h1, wq_ref[...]) + pack[2:3, :3 * cs]).astype(BF)
        row = row_ref[0:1, :]
        outs = [[] for _ in range(S)]
        for h in range(cs // HEAD_DIM):
            at = h * HEAD_DIM
            keys = qkv_o[:, cs + at:cs + at + HEAD_DIM]
            vals = qkv_o[:, 2 * cs + at:2 * cs + at + HEAD_DIM]
            for k in range(S):
                q = qkv_o[k * t:(k + 1) * t, at:at + HEAD_DIM]
                sc = dot(q, keys, 1, 1) * (HEAD_DIM ** -0.5)
                sc = jnp.where(col_ref[k * t:(k + 1) * t, :1] == row, sc, -1e30)
                top = jnp.max(sc, axis=-1, keepdims=True)
                ex = jnp.exp(sc - top)
                total = jnp.sum(ex, axis=-1, keepdims=True)
                pr = (ex * (1.0 / total)).astype(BF)
                outs[k].append(dot(pr, vals).astype(BF))
                lse_o[k * t:(k + 1) * t, h:h + 1] = top + jnp.log(total)
        blocks = [jnp.concatenate(o, 1) for o in outs]
        half = S // 2
        for k in range(half):
            attn_o[k * t:(k + 1) * t, :] = jnp.concatenate([blocks[k], blocks[k + half]], 1)

    def order():
        bits = NB.bit_length() - 1
        return [int(format(p, "b").zfill(bits)[::-1], 2) for p in range(NB)]

    def store_blocks(scr, keep_o, send_o, b):
        for p, m in enumerate(order()):
            o, at = (keep_o, p) if p < NB // 2 else (send_o, p - NB // 2)
            o[at] = scr[b ^ m].astype(BF)

    def up_kernel(*refs):
        xs, ats, cots = refs[:S], refs[S:2 * S], refs[2 * S:3 * S]
        (wout, pack, win, attn_all, h2_o, slope_o, keep_o, send_o, act_s, cot_s, gw_s) = refs[3 * S:]
        t, D = xs[0].shape
        cs = D // S
        FJ = win.shape[1] // NB
        half = S // 2
        b = lax.axis_index("batch")
        for k in range(S):
            pieces = []
            for m in range(S):
                j = k ^ m
                lo, hi = (j % half) * t, (j // half) * cs
                pieces.append(ats[m][lo:lo + t, hi:hi + cs])
            attn_all[k * t:(k + 1) * t, :] = jnp.concatenate(pieces, 1)
        for k in range(S):
            rows = slice(k * t, (k + 1) * t)
            x1 = xs[k][...].astype(F32) + dot(attn_all[rows, :], wout[...]) + pack[3:4, :]
            unit, _ = norm_parts(x1)
            h2 = (unit * pack[4:5, :] + pack[5:6, :]).astype(BF)
            h2_o[rows, :] = h2
            u = dot(h2, win[...]) + pack[6:7, :]
            act, slope = gelu_both(u)
            act_s[rows, :] = act.astype(BF)
            slope_o[rows, :] = slope
            cot_s[rows, :] = cots[k][...]
        gw_s[...] = dot(act_s[...], cot_s[...], 0, 0).reshape(NB, FJ, D)
        store_blocks(gw_s, keep_o, send_o, b)

    def down_kernel(*refs):
        cots, boths = refs[:S], refs[S:2 * S]
        h2, slope, wdn, attn_all, vec, keep_o, send_o, du_s, da_s, gw_s = refs[2 * S:]
        t, D = cots[0].shape
        R = D // NB
        cs = D // S
        NF = slope.shape[1]
        s = lax.axis_index("seq")
        b = lax.axis_index("batch")
        gbin = jnp.zeros((1, NF), F32)
        for k in range(S):
            rows = slice(k * t, (k + 1) * t)
            du = (dot(cots[k][...], wdn[...], 1, 1) * slope[rows, :]).astype(BF)
            du_s[rows, :] = du
            da_s[rows, :] = boths[k][:, cs:]
            gbin = gbin + jnp.sum(du.astype(F32), axis=0, keepdims=True)
        gw_s[:, :, :NF] = dot(h2[...], du_s[...], 0, 0).reshape(NB, R, NF)
        go = dot(attn_all[...], da_s[...], 0, 0)
        per = NB // S
        for m in range(S):
            for j in range(per):
                gw_s[(s ^ m) * per + j, :, NF:NF + cs] = go[m * cs + j * R:m * cs + (j + 1) * R, :]
        gw_s[:, :, NF + cs:] = columns([vec[:4, :], gbin], gw_s.shape[2] - NF - cs)
        store_blocks(gw_s, keep_o, send_o, b)

    def columns(rows, width):
        rows = jnp.concatenate(rows, 0)
        D = rows.shape[1]
        rows = jnp.concatenate([rows, jnp.zeros((128 - rows.shape[0], D), F32)], 0)
        return jnp.transpose(rows)[:, :width].reshape(NB, D // NB, width)

    def local_kernel(*refs):
        x_ref, ats, refs = refs[0], refs[1:1 + S], refs[1 + S:]
        cot_ref, wout, pack, win, wdown = refs[:5]
        refs = refs[5:]
        out_o, dx1_o, vec_o = refs[0], refs[1], refs[2]
        both = refs[3:3 + S]
        t, D = x_ref.shape
        FF = win.shape[1]
        cs = D // S
        s = lax.axis_index("seq")
        half = S // 2
        attn = jnp.concatenate(
            [ats[m][(m % half) * t:(m % half + 1) * t, (m // half) * cs:(m // half + 1) * cs] for m in range(S)], 1)
        x1 = x_ref[...].astype(F32) + dot(attn, wout[...]) + pack[3:4, :]
        unit, scale = norm_parts(x1)
        h2 = (unit * pack[4:5, :] + pack[5:6, :]).astype(BF)
        cot = cot_ref[...]
        C = D
        mixed = jnp.zeros((t, D), F32)
        dh2 = jnp.zeros((t, D), F32)
        for c in range(FF // C):
            cols = slice(c * C, (c + 1) * C)
            u = dot(h2, win[:, cols]) + pack[8 + c:9 + c, :]
            act, slope = gelu_both(u)
            mixed = mixed + dot(act.astype(BF), wdown[cols, :])
            du = (dot(cot, wdown[cols, :], 1, 1) * slope).astype(BF)
            dh2 = dh2 + dot(du, win[:, cols], 1, 1)
        out_o[...] = (x1 + mixed + pack[7:8, :]).astype(BF)
        dy = cot.astype(F32)
        dx1 = dy + norm_back(dh2, unit, scale, pack[4:5, :])
        dx1_o[...] = dx1
        da = dx1.astype(BF)
        vec_o[...] = jnp.concatenate([
            jnp.sum(da.astype(F32), axis=0, keepdims=True),
            jnp.sum(dh2 * unit, axis=0, keepdims=True),
            jnp.sum(dh2, axis=0, keepdims=True),
            jnp.sum(dy, axis=0, keepdims=True),
            jnp.zeros((4, D), F32)], 0)
        dattn = dot(da, wout[...], 1, 1).astype(BF)
        parts = [da[:, i * cs:(i + 1) * cs] for i in range(S)]
        bit = 1
        while bit < S:
            on = (s & bit) != 0
            parts = [jnp.where(on, parts[i ^ bit], parts[i]) for i in range(S)]
            bit *= 2
        for k in range(S):
            both[k][...] = jnp.concatenate([dattn[:, k * cs:(k + 1) * cs], parts[k]], 1)

    def attn_bwd_kernel(*refs):
        xs, boths = refs[:S], refs[S:2 * S]
        row_ref, col_ref, pack, wq, qkv, lse = refs[2 * S:2 * S + 6]
        own_o, next_o, away_o, keep_o, send_o, h1_s, dqkv_s, gw_s = refs[2 * S + 6:]
        t, D = xs[0].shape
        L = S * t
        cs = D // S
        R = D // NB
        s = lax.axis_index("seq")
        b = lax.axis_index("batch")
        scale = HEAD_DIM ** -0.5
        row = row_ref[0:1, :]
        dattn = jnp.concatenate([r[:, :cs] for r in boths], 0)
        dattn_t = jnp.transpose(dattn)
        q_t = jnp.transpose(qkv[:, :cs])
        for h in range(cs // HEAD_DIM):
            at = h * HEAD_DIM
            keys = qkv[:, cs + at:cs + at + HEAD_DIM]
            vals = qkv[:, 2 * cs + at:2 * cs + at + HEAD_DIM]
            dk = jnp.zeros((HEAD_DIM, L), F32)
            dv = jnp.zeros((HEAD_DIM, L), F32)
            for k in range(S):
                rows = slice(k * t, (k + 1) * t)
                sc = dot(qkv[rows, at:at + HEAD_DIM], keys, 1, 1) * scale
                sc = jnp.where(col_ref[rows, :1] == row, sc, -1e30)
                p = jnp.exp(sc - lse[rows, h:h + 1])
                dp = dot(dattn[rows, at:at + HEAD_DIM], vals, 1, 1)
                inner = jnp.sum(p * dp, axis=-1, keepdims=True)
                ds = (p * (dp - inner)).astype(BF)
                dqkv_s[rows, at:at + HEAD_DIM] = (dot(ds, keys) * scale).astype(BF)
                dk = dk + dot(q_t[at:at + HEAD_DIM, rows], ds)
                dv = dv + dot(dattn_t[at:at + HEAD_DIM, rows], p.astype(BF))
            dqkv_s[:, cs + at:cs + at + HEAD_DIM] = jnp.transpose((dk * scale).astype(BF))
            dqkv_s[:, 2 * cs + at:2 * cs + at + HEAD_DIM] = jnp.transpose(dv.astype(BF))
        bsum = jnp.sum(dqkv_s[...].astype(F32), axis=0, keepdims=True)
        gg = jnp.zeros((1, D), F32)
        gb = jnp.zeros((1, D), F32)
        for k in range(S):
            rows = slice(k * t, (k + 1) * t)
            unit, _ = norm_parts(xs[k][...].astype(F32))
            h1_s[rows, :] = (unit * pack[0:1, :] + pack[1:2, :]).astype(BF)
            dh1 = dot(dqkv_s[rows, :], wq[...], 1, 1)
            gg = gg + jnp.sum(dh1 * unit, axis=0, keepdims=True)
            gb = gb + jnp.sum(dh1, axis=0, keepdims=True)
            if k == 0:
                own_o[...] = dh1
            elif k == 1:
                next_o[...] = dh1
            else:
                away_o[k - 2] = dh1.astype(BF)
        gw = dot(h1_s[...], dqkv_s[...], 0, 0)
        gw_s[:, :, :3 * cs] = gw.reshape(NB, R, 3 * cs)
        zero = jnp.zeros((1, cs), F32)
        wide_q = jnp.concatenate([jnp.where(s == i, bsum[:, :cs], zero) for i in range(S)], 1)
        wide_v = jnp.concatenate([jnp.where(s == i, bsum[:, 2 * cs:], zero) for i in range(S)], 1)
        wide = jnp.concatenate([wide_q, wide_v], 1)
        first = jnp.concatenate([wide[:, 2 * i * R:(2 * i + 1) * R] for i in range(NB)], 1)
        second = jnp.concatenate([wide[:, (2 * i + 1) * R:(2 * i + 2) * R] for i in range(NB)], 1)
        gw_s[:, :, 3 * cs:] = columns([gg, gb, first, second], gw_s.shape[2] - 3 * cs)
        store_blocks(gw_s, keep_o, send_o, b)

    def down_final_kernel(ks, *refs):
        parts, (wdn_o,) = refs[:-1], refs[-1:]
        FJ = parts[0].shape[0]
        s = lax.axis_index("seq")
        for k, block in order_of(zip(parts, ks)):
            wdn_o[pl.ds(pl.multiple_of((s ^ k) * FJ, 8), FJ), :] = block.astype(F32)

    def order_of(refs):
        out = []
        for ref, ks in refs:
            out += [(k, ref[...] if len(ks) == 1 else ref[i]) for i, k in enumerate(ks)]
        return out

    def up_final_kernel(ks, *refs):
        parts = refs[:len(ks)]
        win_o, wo_o, bo_o, g2_o, b2_o, bd_o, bin_o, scr = refs[len(ks):]
        R, FF = win_o.shape
        D = wo_o.shape[1]
        cs = D // S
        FJ = FF // (NB * S)
        NF = NB * FJ
        s = lax.axis_index("seq")
        for k, block in order_of(zip(parts, ks)):
            scr[s ^ k] = block.astype(F32)
        for i in range(NB):
            win_o[:, i * S * FJ:(i + 1) * S * FJ] = jnp.concatenate(
                [scr[p, :, i * FJ:(i + 1) * FJ] for p in range(S)], 1)
        wo_o[...] = jnp.concatenate([scr[p, :, NF:NF + cs] for p in range(S)], 1)
        vecs = [as_rows(scr[p, :, NF + cs:]) for p in range(S)]
        total = sum(vecs[1:], vecs[0])
        for i, o in enumerate((bo_o, g2_o, b2_o, bd_o)):
            o[...] = total[i:i + 1, :].reshape(R)
        bin_o[...] = jnp.concatenate([v[4:5, :] for v in vecs], 1).reshape(S * FJ)

    def as_rows(cols):
        R, width = cols.shape
        cols = jnp.concatenate([cols, jnp.zeros((R, 128 - width), F32)], 1)
        cols = jnp.concatenate([cols, jnp.zeros((128 - R, 128), F32)], 0)
        return jnp.transpose(cols)[:8, :R]

    def att_final_kernel(ks, *refs):
        parts = refs[:len(ks)]
        wq_o, g1_o, b1_o, bqv_o, scr = refs[len(ks):]
        R = wq_o.shape[0]
        D = wq_o.shape[1] // 3
        cs = D // S
        s = lax.axis_index("seq")
        for k, block in order_of(zip(parts, ks)):
            scr[s ^ k] = block.astype(F32)
        for c in range(3):
            wq_o[:, c * D:(c + 1) * D] = jnp.concatenate(
                [scr[p, :, c * cs:(c + 1) * cs] for p in range(S)], 1)
        total = as_rows(sum([scr[p, :, 3 * cs:] for p in range(1, S)], scr[0, :, 3 * cs:]))
        g1_o[...] = total[0:1, :].reshape(R)
        b1_o[...] = total[1:2, :].reshape(R)
        bqv_o[...] = jnp.concatenate([total[2:3, :], total[3:4, :]], 1).reshape(2 * R)

    def shards(tokens, segments, ln1_gain, ln1_bias, w_qkv, bias_qv, w_out, bias_out,
               ln2_gain, ln2_bias, w_in, bias_in, w_down, bias_down, cotangent):
        _, t, D = tokens.shape
        FF = w_in.shape[1]
        L = t * S
        cs = D // S
        R = D // NB
        FJ = FF // (NB * S)
        NF = NB * FJ
        x_own = tokens.reshape(t, D)
        cot_own = cotangent.reshape(t, D)

        xs = gather_seq(x_own, S)
        at = lax.broadcasted_iota(jnp.int32, (8, D), 0)
        seg_wide = jnp.pad(segments.astype(F32), ((0, 0), (0, D - L)))
        pack1 = seg_wide
        for i, v in enumerate((ln1_gain, ln1_bias, bias_qv[:D], bias_qv[D:])):
            pack1 = jnp.where(at == i, v[None, :], pack1)
        wq_s, pack1, seg_row, seg_col = call(
            prep_qkv_kernel,
            [sds((D, 3 * cs), BF), sds((8, D), F32), sds((8, L), F32), sds((L, 128), F32)],
            [w_qkv, pack1], "prep_qkv")
        cots = gather_seq(cot_own, S)
        attn, qkv, lse = call(
            attn_fwd_kernel,
            [sds((L // 2, 2 * cs), BF), sds((L, 3 * cs), BF), sds((L, 128), F32)],
            [*xs, seg_row, seg_col, pack1, wq_s], "attn_fwd", flops=2 * L * D * 3 * cs)
        attn, *cots = lax.optimization_barrier((attn, *cots))
        ats = gather_seq(attn, S)
        w_in_late, _ = lax.optimization_barrier((w_in, attn))
        win_s, wout_s, wdn_s, pack = call(
            prep_mlp_kernel,
            [sds((D, NF), BF), sds((D, D), BF), sds((NF, D), BF), sds((16, D), F32)],
            [w_in_late, w_out, w_down, bias_out, ln2_gain, ln2_bias, bias_in, bias_down], "prep_mlp")

        def halve(keep, send, step, after=()):
            got = exchange(send, "batch", NB, step)
            got, keep, after = lax.optimization_barrier((got, keep, after))
            n = keep.shape[0]
            total = lambda lo, hi: (keep[lo:hi].astype(F32) + got[lo:hi].astype(F32)).astype(BF)
            if n == 1:
                return total(0, 1)
            return total(0, n // 2), total(n // 2, n)

        out, dx1, vec, *both = pl.pallas_call(
            local_kernel,
            out_shape=[sds((t, D), BF), sds((t, D), F32), sds((8, D), F32)] + [sds((t, 2 * cs), BF)] * S,
            name="local",
            cost_estimate=pl.CostEstimate(flops=2 * t * D * FF * 4, bytes_accessed=10 * MIB, transcendentals=0),
            compiler_params=pltpu.CompilerParams(vmem_limit_bytes=40 * MIB),
        )(x_own, *ats, cot_own, wout_s, pack, w_in, w_down)
        boths = [both[0]] + [exchange(both[k], "seq", S, k) for k in range(1, S)]
        ats = lax.optimization_barrier((*ats, dx1))[:S]
        attn_all, h2, slope, keep_d, send_d = pl.pallas_call(
            up_kernel,
            out_shape=[sds((L, D), BF), sds((L, D), BF), sds((L, NF), F32),
                       sds((NB // 2, FJ, D), BF), sds((NB // 2, FJ, D), BF)],
            scratch_shapes=[pltpu.VMEM((L, NF), BF), pltpu.VMEM((L, D), BF),
                            pltpu.VMEM((NB, FJ, D), F32)],
            name="up",
            compiler_params=pltpu.CompilerParams(vmem_limit_bytes=32 * MIB),
        )(*xs, *ats, *cots, wout_s, pack, win_s)
        send_d, *boths = lax.optimization_barrier((send_d, *boths))
        wide_u, wide_a = -(-(NF + cs + 8) // 128) * 128, -(-(3 * cs + 8) // 128) * 128
        keep_u, send_u = pl.pallas_call(
            down_kernel,
            out_shape=[sds((NB // 2, R, wide_u), BF), sds((NB // 2, R, wide_u), BF)],
            scratch_shapes=[pltpu.VMEM((L, NF), BF), pltpu.VMEM((L, cs), BF), pltpu.VMEM((NB, R, wide_u), F32)],
            name="down",
            compiler_params=pltpu.CompilerParams(vmem_limit_bytes=32 * MIB),
        )(*cots, *boths, h2, slope, wdn_s, attn_all, vec)
        kd, sd = halve(keep_d, send_d, 1)
        kd, sd, send_u = lax.optimization_barrier((kd, sd, send_u))
        ku, su = halve(keep_u, send_u, 1, sd)
        qkv, su = lax.optimization_barrier((qkv, su))
        own, beside, away, keep_a, send_a = pl.pallas_call(
            attn_bwd_kernel,
            out_shape=[sds((t, D), F32), sds((t, D), F32), sds((S - 2, t, D), BF),
                       sds((NB // 2, R, wide_a), BF), sds((NB // 2, R, wide_a), BF)],
            scratch_shapes=[pltpu.VMEM((L, D), BF), pltpu.VMEM((L, 3 * cs), BF), pltpu.VMEM((NB, R, wide_a), F32)],
            name="attn_bwd",
            cost_estimate=pl.CostEstimate(flops=2 * L * D * D * 4, bytes_accessed=10 * MIB, transcendentals=0),
            compiler_params=pltpu.CompilerParams(vmem_limit_bytes=40 * MIB),
        )(*xs, *boths, seg_row, seg_col, pack1, wq_s, qkv, lse)
        kd, sd = halve(kd, sd, 2, keep_a)
        ku, su = halve(ku, su, 2, sd)
        ka, sa = halve(keep_a, send_a, 1, su)
        away, sa = lax.optimization_barrier((away, sa))
        got = exchange(away, "seq", S, 2)
        kd = halve(kd, sd, 4, sa)
        ka, sa = halve(ka, sa, 2, kd)
        got, sa = lax.optimization_barrier((got, sa))
        beside = exchange((beside + got[1].astype(F32)).astype(BF), "seq", S, 1)
        dh1 = own + got[0].astype(F32) + beside.astype(F32)
        kd, sa = lax.optimization_barrier((kd, sa))
        down, ks_d = gather_steps(kd[0], S, (1, 2))
        ku = halve(ku, su, 4, sa)
        up, ks_u = gather_steps(ku[0], S, (2, 1))
        ka = halve(ka, sa, 4, ku)
        att = gather_seq(ka[0], S)
        ks_a = [[k] for k in range(S)]
        unit1, scale1 = norm_parts(x_own.astype(F32))
        d_tokens = (dx1 + norm_back(dh1, unit1, scale1, ln1_gain)).reshape(tokens.shape)

        o_wdn, = pl.pallas_call(
            functools.partial(down_final_kernel, ks_d), out_shape=[sds((S * FJ, D), F32)], name="down_final",
            compiler_params=pltpu.CompilerParams(vmem_limit_bytes=24 * MIB))(*down)
        vec_out = sds((R,), F32)
        o_win, o_wout, o_bout, o_ln2g, o_ln2b, o_bdn, o_bin = pl.pallas_call(
            functools.partial(up_final_kernel, ks_u),
            out_shape=[sds((R, FF), F32), sds((R, D), F32)] + [vec_out] * 4 + [sds((S * FJ,), F32)],
            scratch_shapes=[pltpu.VMEM((S, R, wide_u), F32)], name="up_final",
            compiler_params=pltpu.CompilerParams(vmem_limit_bytes=24 * MIB))(*up)
        o_wqkv, o_ln1g, o_ln1b, o_bqv = pl.pallas_call(
            functools.partial(att_final_kernel, ks_a),
            out_shape=[sds((R, 3 * D), F32), vec_out, vec_out, sds((2 * R,), F32)],
            scratch_shapes=[pltpu.VMEM((S, R, wide_a), F32)], name="att_final",
            compiler_params=pltpu.CompilerParams(vmem_limit_bytes=24 * MIB))(*att)
        return (out.reshape(tokens.shape), d_tokens, o_ln1g, o_ln1b, o_wqkv, o_bqv, o_wout, o_bout,
                o_ln2g, o_ln2b, o_win, o_bin, o_wdn, o_bdn)
    return shards


def make_plain(S, NB):
    def shards(tokens, segments, ln1_gain, ln1_bias, w_qkv, bias_qv, w_out, bias_out,
               ln2_gain, ln2_bias, w_in, bias_in, w_down, bias_down, cotangent):
        rows, t, D = tokens.shape
        FF = w_in.shape[1]
        L = t * S
        hs = HEADS // S
        cs = hs * HEAD_DIM
        R = D // NB
        FJ = FF // (NB * S)
        scale = HEAD_DIM ** (-0.5)
        s = lax.axis_index("seq")
        b = lax.axis_index("batch")
        rel_s = jnp.arange(S, dtype=jnp.int32) ^ s
        rel_b = jnp.arange(NB, dtype=jnp.int32) ^ b

        x_own = tokens.reshape(t, D)
        cot_own = cotangent.reshape(t, D)
        wq_s = lax.dynamic_slice_in_dim(w_qkv.reshape(D, 3, S, cs), s, 1, 2).reshape(D, 3 * cs)
        bq_s = lax.dynamic_slice_in_dim(bias_qv.reshape(2, S, cs), s, 1, 1).reshape(2, cs)
        bqkv_s = jnp.concatenate([bq_s[0], jnp.zeros((cs,), F32), bq_s[1]])
        win_s = lax.dynamic_slice_in_dim(w_in.reshape(D, NB, S, FJ), s, 1, 2).reshape(D, NB * FJ)
        bin_s = lax.dynamic_slice_in_dim(bias_in.reshape(NB, S, FJ), s, 1, 1).reshape(NB * FJ)
        wdn_s = lax.dynamic_slice_in_dim(w_down.reshape(NB, S, FJ, D), s, 1, 1).reshape(NB * FJ, D)
        wout_rel = jnp.take(w_out.reshape(S, cs, D), rel_s, axis=0).reshape(D, D)
        seg_rel = jnp.take(segments.reshape(S, t), rel_s, axis=0).reshape(L)

        x_all = jnp.concatenate(gather_seq(x_own, S), 0)
        cot_in, x_all = lax.optimization_barrier((cot_own, x_all))
        cot_all = jnp.concatenate(gather_seq(cot_in, S), 0)

        x_f = x_all.astype(F32)
        unit1, scale1 = norm_parts(x_f)
        h1 = (unit1 * ln1_gain + ln1_bias).astype(BF)
        qkv = (dot(h1, wq_s) + bqkv_s).astype(BF)
        q = qkv[:, :cs].reshape(L, hs, HEAD_DIM)
        k = qkv[:, cs:2 * cs].reshape(L, hs, HEAD_DIM)
        v = qkv[:, 2 * cs:].reshape(L, hs, HEAD_DIM)
        mask = seg_rel[:, None] == seg_rel[None, :]
        scores = jnp.einsum("qhd,khd->hqk", q, k, preferred_element_type=F32) * scale
        scores = jnp.where(mask[None], scores, -1e30)
        top = jnp.max(scores, axis=-1, keepdims=True)
        expo = jnp.exp(scores - top)
        total = jnp.sum(expo, axis=-1, keepdims=True)
        probs = expo / total
        probs_low = probs.astype(BF)
        attn = jnp.einsum("hqk,khd->qhd", probs_low, v, preferred_element_type=F32).reshape(L, cs).astype(BF)

        got = gather_seq(attn, S)
        blocks = []
        for m, g in enumerate(got):
            g4 = g.reshape(S, t, cs)
            blocks.append(jnp.concatenate([g4[kk ^ m] for kk in range(S)], 0))
        attn_all = jnp.concatenate(blocks, 1)

        x1 = x_f + dot(attn_all, wout_rel) + bias_out
        unit2, scale2 = norm_parts(x1)
        h2 = (unit2 * ln2_gain + ln2_bias).astype(BF)

        u_s = dot(h2, win_s) + bin_s
        act_s, slope_s = gelu_both(u_s)
        act_s = act_s.astype(BF)
        dact_s = dot(cot_all, wdn_s, 1, 1)
        du_s = (dact_s * slope_s).astype(BF)
        g_win = dot(h2, du_s, 0, 0)
        g_wdn = dot(act_s, cot_all, 0, 0)
        g_bin = jnp.sum(du_s.astype(F32), 0)
        mlp = jnp.concatenate([g_win.reshape(NB, R, NB * FJ), g_wdn.reshape(NB, FJ, D)], 1).astype(BF)

        h2o = h2[:t]
        u = dot(h2o, w_in) + bias_in
        act, slope = gelu_both(u)
        act = act.astype(BF)
        activations = (x1[:t] + dot(act, w_down) + bias_down).astype(BF)
        dy = cot_own.astype(F32)
        du = (dot(cot_own, w_down, 1, 1) * slope).astype(BF)
        dh2 = dot(du, w_in, 1, 1)
        g_ln2g = jnp.sum(dh2 * unit2[:t], 0)
        g_ln2b = jnp.sum(dh2, 0)
        dx1 = dy + norm_back(dh2, unit2[:t], scale2[:t], ln2_gain)
        da = dx1.astype(BF)
        g_bout = jnp.sum(da.astype(F32), 0)
        g_bdn = jnp.sum(dy, 0)
        dattn = dot(da, wout_rel, 1, 1).astype(BF)
        da_rel = jnp.take(da.reshape(t, S, cs), rel_s, axis=1)
        both = [jnp.concatenate([dattn[:, kk * cs:(kk + 1) * cs], da_rel[:, kk]], 1) for kk in range(S)]
        both = jnp.concatenate([both[0]] + [exchange(both[kk], "seq", S, kk) for kk in range(1, S)], 0)
        dattn_all = both[:, :cs].reshape(L, hs, HEAD_DIM)
        da_s = both[:, cs:]

        log_total = top + jnp.log(total)
        p = jnp.exp(scores - log_total)
        p_low = p.astype(BF)
        dp = jnp.einsum("qhd,khd->hqk", dattn_all, v, preferred_element_type=F32)
        inner = jnp.sum(p * dp, axis=-1, keepdims=True)
        ds = (p * (dp - inner)).astype(BF)
        dq = jnp.einsum("hqk,khd->qhd", ds, k, preferred_element_type=F32) * scale
        dk = jnp.einsum("hqk,qhd->khd", ds, q, preferred_element_type=F32) * scale
        dv = jnp.einsum("hqk,qhd->khd", p_low, dattn_all, preferred_element_type=F32)
        dqkv = jnp.concatenate([dq.reshape(L, cs), dk.reshape(L, cs), dv.reshape(L, cs)], 1).astype(BF)

        dh1_part = dot(dqkv, wq_s, 1, 1)
        g_ln1g = jnp.sum(dh1_part * unit1, 0)
        g_ln1b = jnp.sum(dh1_part, 0)
        dh1_low = dh1_part.astype(BF)
        dh1 = dh1_part[:t]
        for kk in range(1, S):
            dh1 = dh1 + exchange(dh1_low[kk * t:(kk + 1) * t], "seq", S, kk).astype(F32)
        d_tokens = (dx1 + norm_back(dh1, unit1[:t], scale1[:t], ln1_gain)).reshape(tokens.shape)

        g_wqkv = dot(h1, dqkv, 0, 0)
        g_wout = dot(attn_all, da_s, 0, 0)
        g_wout = jnp.take(g_wout.reshape(S, cs, cs), rel_s, axis=0).reshape(D, cs)
        bsum = jnp.sum(dqkv.astype(F32), 0)
        g_bqv = jnp.zeros((2, S, cs), F32)
        g_bqv = lax.dynamic_update_slice(g_bqv, jnp.stack([bsum[:cs], bsum[2 * cs:]])[:, None], (0, s, 0))
        small = jnp.concatenate(
            [v_.reshape(NB, -1) for v_ in (g_ln1g, g_ln1b, g_bqv, g_bout, g_ln2g, g_ln2b, g_bdn, g_bin)], 1)
        small_n = small.shape[1]
        small_rows = -(-small_n // D)
        pad_rows = -(-small_rows // 16) * 16
        small = jnp.pad(small, ((0, 0), (0, pad_rows * D - small_n))).reshape(NB, pad_rows, D)
        att = jnp.concatenate(
            [jnp.concatenate([g_wqkv.reshape(NB, R, 3 * cs), g_wout.reshape(NB, R, cs)], 2), small], 1).astype(BF)

        def reduce_batch(buf):
            buf = jnp.take(buf, rel_b, axis=0).reshape((NB // 2, 2) + buf.shape[1:])
            buf = (buf[:, 0].astype(F32) + exchange(buf[:, 1], "batch", NB, 1).astype(F32)).astype(BF)
            n = NB // 2
            while n > 4:
                n //= 2
                buf = (buf[:n].astype(F32) + exchange(buf[n:], "batch", NB, 2 * n).astype(F32)).astype(BF)
            acc = buf[0].astype(F32)
            for m in range(1, n):
                acc = acc + exchange(buf[m], "batch", NB, 2 * m).astype(F32)
            parts = jnp.stack(gather_seq(acc.astype(BF), S))
            return jnp.take(parts, rel_s, axis=0).astype(F32)

        mlp = reduce_batch(mlp)
        att = reduce_batch(att)
        o_win = mlp[:, :R].reshape(S, R, NB, FJ).transpose(1, 2, 0, 3).reshape(R, FF)
        o_wdn = mlp[:, R:].reshape(S * FJ, D)
        o_wqkv = att[:, :R, :3 * cs].reshape(S, R, 3, cs).transpose(1, 2, 0, 3).reshape(R, 3 * D)
        o_wout = att[:, :R, 3 * cs:].transpose(1, 0, 2).reshape(R, D)
        flat = att[:, R:].reshape(S, -1)
        o_bin = flat[:, 8 * R:8 * R + FJ].reshape(S * FJ)
        tot = jnp.sum(flat[:, :8 * R], 0)
        o_ln1g, o_ln1b, o_bqv, o_bout, o_ln2g, o_ln2b, o_bdn = (
            tot[:R], tot[R:2 * R], tot[2 * R:4 * R], tot[4 * R:5 * R], tot[5 * R:6 * R], tot[6 * R:7 * R], tot[7 * R:])
        return (activations.reshape(tokens.shape), d_tokens, o_ln1g, o_ln1b, o_wqkv, o_bqv, o_wout, o_bout,
                o_ln2g, o_ln2b, o_win, o_bin, o_wdn, o_bdn)
    return shards


def solution(mesh):
    S, NB = mesh.shape["seq"], mesh.shape["batch"]
    shards = (make if BLOCK_ROWS // NB % 32 == 0 else make_plain)(S, NB)
    rowwise = P("batch", "seq", None)
    placed = (rowwise, P("batch", None)) + (P(),) * 12 + (rowwise,)
    b, bn = P("batch"), P("batch", None)
    return jax.shard_map(
        shards,
        mesh=mesh,
        in_specs=placed,
        out_specs=(rowwise, rowwise, b, b, bn, b, bn, b, b, b, bn, b, bn, b),
        check_vma=False,
    )
```

```python
import functools

import jax
import jax.numpy as jnp
from jax import lax
from jax.experimental import pallas as pl
from jax.experimental.pallas import tpu as pltpu
from jax.sharding import PartitionSpec as P

HEADS = 12
HEAD_DIM = 64
BLOCK_ROWS = HEADS * HEAD_DIM
BF = jnp.bfloat16
F32 = jnp.float32
MIB = 1 << 20


def dot(a, b, ca=1, cb=0):
    return lax.dot_general(a, b, (((ca,), (cb,)), ((), ())), preferred_element_type=F32)


def exchange(value, axis, size, step):
    return lax.ppermute(value, axis, [(j, j ^ step) for j in range(size)])


def gather_seq(value, size):
    return [value] + [exchange(value, "seq", size, k) for k in range(1, size)]


def norm_parts(values):
    mean = jnp.mean(values, axis=-1, keepdims=True)
    centred = values - mean
    var = jnp.mean(centred * centred, axis=-1, keepdims=True)
    scale = lax.rsqrt(var + 1e-06)
    return centred * scale, scale


def norm_back(grad, unit, scale, gain):
    grad = grad * gain
    mean = jnp.mean(grad, axis=-1, keepdims=True)
    along = jnp.mean(grad * unit, axis=-1, keepdims=True)
    return (grad - mean - unit * along) * scale


def gelu_both(v):
    c = 0.7978845608028654
    square = v * v
    t = jnp.tanh(c * v * (1.0 + 0.044715 * square))
    half = 0.5 * (1.0 + t)
    slope = half + (0.5 * c) * v * (1.0 - t * t) * (1.0 + 3.0 * 0.044715 * square)
    return v * half, slope


def call(kernel, outs, args, name, flops=0, limit=24):
    size = sum(a.size * a.dtype.itemsize for a in args) + sum(o.size * o.dtype.itemsize for o in outs)
    return pl.pallas_call(
        kernel,
        out_shape=outs,
        name=name,
        cost_estimate=pl.CostEstimate(flops=flops, bytes_accessed=size, transcendentals=0),
        compiler_params=pltpu.CompilerParams(vmem_limit_bytes=limit * MIB),
    )(*args)


def sds(shape, dtype):
    return jax.ShapeDtypeStruct(shape, dtype)


HOPS = {"d": "far", "u": "near", "a": "near"}
GATHER = {"d": None, "u": None, "a": None}
DH = (1, 2)
ORDER = "pq af c1 c2 c3 lo pm fa up dn d0 u0 bw d1 u1 bo a0 h1 d2 a1 u2 d3 d4 ou a2 h2 u3 u4 a3 a4".split()


def flat(ref):
    return ref[...].reshape(1, -1)


def make(S, NB):
    near_first = [2 ** i for i in range(NB.bit_length() - 1)]
    far_first = near_first[:1] + near_first[:0:-1]
    hops = {k: near_first if v == "near" else far_first for k, v in HOPS.items()}

    def rel_row(row, t):
        s = lax.axis_index("seq")
        parts = [row[:, i * t:(i + 1) * t] for i in range(S)]
        bit = 1
        while bit < S:
            on = (s & bit) != 0
            parts = [jnp.where(on, parts[i ^ bit], parts[i]) for i in range(S)]
            bit *= 2
        return jnp.concatenate(parts, 1)

    def prep_qkv_kernel(wqkv, pack, wq_o, bq_o, row_o, col_o):
        D = wqkv.shape[0]
        cs = D // S
        L = row_o.shape[1]
        s = lax.axis_index("seq")
        row = rel_row(pack[4:5, :L], L // S)
        row_o[...] = jnp.broadcast_to(row, row_o.shape)
        col_o[...] = jnp.transpose(jnp.broadcast_to(row, (128, L)))
        bq_o[0:2, :] = pack[0:2, :]
        for p in range(S):
            @pl.when(s == p)
            def _(p=p):
                for c in range(3):
                    wq_o[:, c * cs:(c + 1) * cs] = wqkv[:, c * D + p * cs:c * D + (p + 1) * cs]
                zero = jnp.zeros((1, cs), F32)
                bq_o[2:3, :] = jnp.concatenate(
                    [pack[2:3, p * cs:(p + 1) * cs], zero, pack[3:4, p * cs:(p + 1) * cs], zero], 1)

    def prep_mlp_kernel(win, wout, wdown, bin_, win_o, wout_o, wdn_o, bin_o):
        D = wout.shape[0]
        FF = win.shape[1]
        cs = D // S
        FJ = FF // (NB * S)
        s = lax.axis_index("seq")
        vin = flat(bin_)
        for m in range(S):
            wout_o[m * cs:(m + 1) * cs, :] = wout[pl.ds(pl.multiple_of((s ^ m) * cs, 16), cs), :]
        for i in range(NB):
            wdn_o[i * FJ:(i + 1) * FJ, :] = wdown[pl.ds(pl.multiple_of((i * S + s) * FJ, 16), FJ), :]
        for p in range(S):
            @pl.when(s == p)
            def _(p=p):
                for i in range(NB):
                    at = (i * S + p) * FJ
                    win_o[:, i * FJ:(i + 1) * FJ] = win[:, at:at + FJ]
                    bin_o[:, i * FJ:(i + 1) * FJ] = vin[:, at:at + FJ]

    def attn_fwd_kernel(*refs):
        xs, (row_ref, col_ref, pack, wq_ref, qkv_o, lse_o, attn_o) = refs[:S], refs[S:S + 7]
        near_o, far_o = refs[S + 7:2 * S + 6], refs[2 * S + 6:]
        t, D = xs[0].shape
        L = S * t
        cs = D // S
        for k in range(S):
            unit, _ = norm_parts(xs[k][...].astype(F32))
            h1 = (unit * pack[0:1, :] + pack[1:2, :]).astype(BF)
            qkv_o[k * t:(k + 1) * t, :] = (dot(h1, wq_ref[...]) + pack[2:3, :3 * cs]).astype(BF)
        row = row_ref[0:1, :]
        heads = cs // HEAD_DIM
        outs = [[None] * heads for _ in range(S)]
        def part(c, h, rows=slice(None)):
            return qkv_o[rows, c * cs + h * HEAD_DIM:c * cs + (h + 1) * HEAD_DIM]
        def soft(sc, rows, h):
            sc = jnp.where(col_ref[rows, :1] == row, sc, -1e30)
            top = jnp.max(sc, axis=-1, keepdims=True)
            ex = jnp.exp(sc - top)
            total = jnp.sum(ex, axis=-1, keepdims=True)
            lse_o[rows, h:h + 1] = top + jnp.log(total)
            return (ex * (1.0 / total)).astype(BF)
        def put(o, h, n):
            o = o.astype(BF)
            for r in range(o.shape[0] // t):
                outs[n + r][h] = o[r * t:(r + 1) * t]
        Q = 256
        todo = [(h, n) for h in range(heads) for n in range(L // Q)]
        def score(h, n):
            return dot(part(0, h, slice(n * Q, (n + 1) * Q)) * BF(HEAD_DIM ** -0.5), part(1, h), 1, 1)
        nxt = score(*todo[0])
        prev = None
        for i, (h, n) in enumerate(todo):
            cur = nxt
            if i + 1 < len(todo):
                nxt = score(*todo[i + 1])
            pr = soft(cur, slice(n * Q, (n + 1) * Q), h)
            if prev is not None:
                put(dot(prev[0], part(2, prev[1])), prev[1], prev[2])
            prev = (pr, h, n * Q // t)
        put(dot(prev[0], part(2, prev[1])), prev[1], prev[2])
        blocks = [jnp.concatenate(o, 1) for o in outs]
        for k in range(S):
            attn_o[k * t:(k + 1) * t, :] = blocks[k]
        for m in range(1, S):
            near_o[m - 1][...] = fold(blocks[m])
            far_o[m - 1][...] = fold(jnp.concatenate([blocks[k ^ m] for k in range(1, S)], 0))

    def fold(block):
        half = block.shape[0] // 2
        return jnp.concatenate([block[:half], block[half:]], 1)

    def unfold(block):
        half = block.shape[1] // 2
        return jnp.concatenate([block[:, :half], block[:, half:]], 0)

    def order(steps):
        ms = [0]
        for step in reversed(steps):
            ms = ms + [m ^ step for m in ms]
        return ms

    def store_blocks(scr, keep_o, send_o, b, steps):
        for p, m in enumerate(order(steps)):
            o, at = (keep_o, p) if p < NB // 2 else (send_o, p - NB // 2)
            o[at] = scr[b ^ m].astype(BF)

    def up_kernel(*refs):
        xs, (own,), nears, fars, cots = refs[:S], refs[S:S + 1], refs[S + 1:2 * S], refs[2 * S:3 * S - 1], refs[3 * S - 1:4 * S - 1]
        (wout, bout, g_ref, b_ref, win, bin_ref, attn_all, h2_o, slope_o, keep_o, send_o,
         act_s, cot_s, gw_s) = refs[4 * S - 1:]
        t, D = xs[0].shape
        cs = D // S
        FJ = win.shape[1] // NB
        b = lax.axis_index("batch")
        attn_all[:t, :] = jnp.concatenate([own[:t, :]] + [unfold(r[...]) for r in nears], 1)
        attn_all[t:, :] = jnp.concatenate([own[t:, :]] + [unfold(r[...]) for r in fars], 1)
        for k in range(S):
            cot_s[k * t:(k + 1) * t, :] = cots[k][...]
        x = jnp.concatenate([x[...].astype(F32) for x in xs], 0)
        x1 = x + dot(attn_all[...], wout[...]) + flat(bout)
        unit, _ = norm_parts(x1)
        h2 = (unit * flat(g_ref) + flat(b_ref)).astype(BF)
        h2_o[...] = h2
        act, slope = gelu_both(dot(h2, win[...]) + bin_ref[...])
        act_s[...] = act.astype(BF)
        slope_o[...] = slope
        gw_s[...] = dot(act_s[...], cot_s[...], 0, 0).reshape(NB, FJ, D)
        store_blocks(gw_s, keep_o, send_o, b, hops["d"])

    def down_kernel(*refs):
        cots, boths = refs[:S], refs[S:2 * S]
        h2, slope, wdn, attn_all, vec, keep_o, send_o, du_s, da_s, gw_s = refs[2 * S:]
        t, D = cots[0].shape
        R = D // NB
        cs = D // S
        NF = slope.shape[1]
        s = lax.axis_index("seq")
        b = lax.axis_index("batch")
        for k in range(S):
            da_s[k * t:(k + 1) * t, :] = boths[k][:, cs:]
        cot = jnp.concatenate([c[...] for c in cots], 0)
        du = (dot(cot, wdn[...], 1, 1) * slope[...]).astype(BF)
        du_s[...] = du
        gbin = jnp.sum(du.astype(F32), axis=0, keepdims=True)
        gw_s[:, :, :NF] = dot(h2[...], du_s[...], 0, 0).reshape(NB, R, NF)
        go = dot(attn_all[...], da_s[...], 0, 0)
        per = NB // S
        for m in range(S):
            for j in range(per):
                gw_s[(s ^ m) * per + j, :, NF:NF + cs] = go[m * cs + j * R:m * cs + (j + 1) * R, :]
        gw_s[:, :, NF + cs:] = columns([vec[:4, :], gbin], gw_s.shape[2] - NF - cs)
        store_blocks(gw_s, keep_o, send_o, b, hops["u"])

    def columns(rows, width):
        rows = jnp.concatenate(rows, 0)
        D = rows.shape[1]
        rows = jnp.concatenate([rows, jnp.zeros((128 - rows.shape[0], D), F32)], 0)
        return jnp.transpose(rows)[:, :width].reshape(NB, D // NB, width)

    def local_kernel(*refs):
        x_ref, own, nears, refs = refs[0], refs[1], refs[2:1 + S], refs[1 + S:]
        cot_ref, wout, bout, g_ref, b_ref, win, bin_ref, wdown = refs[:8]
        act_o, x1_o, dx1_o, vec_o = refs[8:12]
        both = refs[12:]
        t, D = x_ref.shape
        FF = win.shape[1]
        cs = D // S
        s = lax.axis_index("seq")
        heads = [wout[pl.ds(pl.multiple_of((s ^ m) * cs, 16), cs), :] for m in range(S)]
        attn = [own[:t, :]] + [unfold(r[...]) for r in nears]
        x1 = x_ref[...].astype(F32) + flat(bout)
        for m in range(S):
            x1 = x1 + dot(attn[m], heads[m])
        unit, scale = norm_parts(x1)
        h2 = (unit * flat(g_ref) + flat(b_ref)).astype(BF)
        cot = cot_ref[...]
        bias_in = flat(bin_ref)
        x1_o[...] = x1
        dh2 = jnp.zeros((t, D), F32)
        for c in range(FF // D):
            cols = slice(c * D, (c + 1) * D)
            act, slope = gelu_both(dot(h2, win[:, cols]) + bias_in[:, cols])
            act_o[:, cols] = act.astype(BF)
            du = (dot(cot, wdown[cols, :], 1, 1) * slope).astype(BF)
            dh2 = dh2 + dot(du, win[:, cols], 1, 1)
        dy = cot.astype(F32)
        dx1 = dy + norm_back(dh2, unit, scale, flat(g_ref))
        dx1_o[...] = dx1
        da = dx1.astype(BF)
        vec_o[...] = jnp.concatenate([
            jnp.sum(da.astype(F32), axis=0, keepdims=True),
            jnp.sum(dh2 * unit, axis=0, keepdims=True),
            jnp.sum(dh2, axis=0, keepdims=True),
            jnp.sum(dy, axis=0, keepdims=True),
            jnp.zeros((4, D), F32)], 0)
        parts = [da[:, i * cs:(i + 1) * cs] for i in range(S)]
        bit = 1
        while bit < S:
            on = (s & bit) != 0
            parts = [jnp.where(on, parts[i ^ bit], parts[i]) for i in range(S)]
            bit *= 2
        for k in range(S):
            both[k][...] = jnp.concatenate([dot(da, heads[k], 1, 1).astype(BF), parts[k]], 1)

    def out_kernel(x1_ref, act, wdown, bdown, out_o):
        out_o[...] = (x1_ref[...] + dot(act[...], wdown[...]) + flat(bdown)).astype(BF)

    def attn_bwd_kernel(*refs):
        xs, boths = refs[:S], refs[S:2 * S]
        row_ref, col_ref, pack, wq, qkv, lse = refs[2 * S:2 * S + 6]
        own_o, next_o, away_o, keep_o, send_o, h1_s, dqkv_s, gw_s = refs[2 * S + 6:]
        t, D = xs[0].shape
        L = S * t
        cs = D // S
        R = D // NB
        s = lax.axis_index("seq")
        b = lax.axis_index("batch")
        scale = HEAD_DIM ** -0.5
        row = row_ref[0:1, :]
        dattn = jnp.concatenate([r[:, :cs] for r in boths], 0)
        dattn_t = jnp.transpose(dattn)
        q_t = jnp.transpose(qkv[:, :cs] * BF(scale))
        Q = 512
        heads = cs // HEAD_DIM
        todo = [(h, n) for h in range(heads) for n in range(L // Q)]

        def part(c, h, rows=slice(None)):
            return qkv[rows, c * cs + h * HEAD_DIM:c * cs + (h + 1) * HEAD_DIM]

        def products(h, n):
            rows = slice(n * Q, (n + 1) * Q)
            return (dot(part(0, h, rows) * BF(scale), part(1, h), 1, 1),
                    dot(dattn[rows, h * HEAD_DIM:(h + 1) * HEAD_DIM], part(2, h), 1, 1))

        def slopes(sc, dp, h, n):
            rows = slice(n * Q, (n + 1) * Q)
            sc = jnp.where(col_ref[rows, :1] == row, sc, -1e30)
            p = jnp.exp(sc - lse[rows, h:h + 1])
            inner = jnp.sum(p * dp, axis=-1, keepdims=True)
            return p.astype(BF), (p * (dp - inner)).astype(BF)

        dk = [jnp.zeros((HEAD_DIM, L), F32) for _ in range(heads)]
        dv = [jnp.zeros((HEAD_DIM, L), F32) for _ in range(heads)]

        def gradients(p, ds, h, n):
            rows = slice(n * Q, (n + 1) * Q)
            at = h * HEAD_DIM
            dqkv_s[rows, at:at + HEAD_DIM] = dot(ds, part(1, h) * BF(scale)).astype(BF)
            dk[h] = dk[h] + dot(q_t[at:at + HEAD_DIM, rows], ds)
            dv[h] = dv[h] + dot(dattn_t[at:at + HEAD_DIM, rows], p)
            if n == L // Q - 1:
                dqkv_s[:, cs + at:cs + at + HEAD_DIM] = jnp.transpose(dk[h].astype(BF))
                dqkv_s[:, 2 * cs + at:2 * cs + at + HEAD_DIM] = jnp.transpose(dv[h].astype(BF))

        ahead = products(*todo[0])
        behind = None
        for i, at in enumerate(todo):
            now = ahead
            if i + 1 < len(todo):
                ahead = products(*todo[i + 1])
            p, ds = slopes(*now, *at)
            if behind is not None:
                gradients(*behind)
            behind = (p, ds) + at
        gradients(*behind)
        bsum = jnp.sum(dqkv_s[...].astype(F32), axis=0, keepdims=True)
        gg = jnp.zeros((1, D), F32)
        gb = jnp.zeros((1, D), F32)
        for k in range(S):
            rows = slice(k * t, (k + 1) * t)
            unit, _ = norm_parts(xs[k][...].astype(F32))
            h1_s[rows, :] = (unit * pack[0:1, :] + pack[1:2, :]).astype(BF)
            dh1 = dot(dqkv_s[rows, :], wq[...], 1, 1)
            gg = gg + jnp.sum(dh1 * unit, axis=0, keepdims=True)
            gb = gb + jnp.sum(dh1, axis=0, keepdims=True)
            if k == 0:
                own_o[...] = dh1
            elif k == DH[1]:
                next_o[...] = dh1
            else:
                away_o[int(k != DH[0])] = dh1.astype(BF)
        gw = dot(h1_s[...], dqkv_s[...], 0, 0)
        gw_s[:, :, :3 * cs] = gw.reshape(NB, R, 3 * cs)
        zero = jnp.zeros((1, cs), F32)
        wide_q = jnp.concatenate([jnp.where(s == i, bsum[:, :cs], zero) for i in range(S)], 1)
        wide_v = jnp.concatenate([jnp.where(s == i, bsum[:, 2 * cs:], zero) for i in range(S)], 1)
        wide = jnp.concatenate([wide_q, wide_v], 1)
        first = jnp.concatenate([wide[:, 2 * i * R:(2 * i + 1) * R] for i in range(NB)], 1)
        second = jnp.concatenate([wide[:, (2 * i + 1) * R:(2 * i + 2) * R] for i in range(NB)], 1)
        gw_s[:, :, 3 * cs:] = columns([gg, gb, first, second], gw_s.shape[2] - 3 * cs)
        store_blocks(gw_s, keep_o, send_o, b, hops["a"])

    def down_final_kernel(ks, *refs):
        parts, (wdn_o,) = refs[:-1], refs[-1:]
        FJ = parts[0].shape[0]
        s = lax.axis_index("seq")
        for k, block in order_of(zip(parts, ks)):
            wdn_o[pl.ds(pl.multiple_of((s ^ k) * FJ, 8), FJ), :] = block.astype(F32)

    def order_of(refs):
        out = []
        for ref, ks in refs:
            out += [(k, ref[...] if len(ks) == 1 else ref[i]) for i, k in enumerate(ks)]
        return out

    def up_final_kernel(ks, *refs):
        parts = refs[:len(ks)]
        win_o, wo_o, bo_o, g2_o, b2_o, bd_o, bin_o, scr = refs[len(ks):]
        R, FF = win_o.shape
        D = wo_o.shape[1]
        cs = D // S
        FJ = FF // (NB * S)
        NF = NB * FJ
        s = lax.axis_index("seq")
        for k, block in order_of(zip(parts, ks)):
            scr[s ^ k] = block.astype(F32)
        for i in range(NB):
            win_o[:, i * S * FJ:(i + 1) * S * FJ] = jnp.concatenate(
                [scr[p, :, i * FJ:(i + 1) * FJ] for p in range(S)], 1)
        wo_o[...] = jnp.concatenate([scr[p, :, NF:NF + cs] for p in range(S)], 1)
        vecs = [as_rows(scr[p, :, NF + cs:]) for p in range(S)]
        total = sum(vecs[1:], vecs[0])
        for i, o in enumerate((bo_o, g2_o, b2_o, bd_o)):
            o[...] = total[i:i + 1, :].reshape(R)
        bin_o[...] = jnp.concatenate([v[4:5, :] for v in vecs], 1).reshape(S * FJ)

    def as_rows(cols):
        R, width = cols.shape
        cols = jnp.concatenate([cols, jnp.zeros((R, 128 - width), F32)], 1)
        cols = jnp.concatenate([cols, jnp.zeros((128 - R, 128), F32)], 0)
        return jnp.transpose(cols)[:8, :R]

    def att_final_kernel(ks, *refs):
        parts = refs[:len(ks)]
        wq_o, g1_o, b1_o, bqv_o, scr = refs[len(ks):]
        R = wq_o.shape[0]
        D = wq_o.shape[1] // 3
        cs = D // S
        s = lax.axis_index("seq")
        for k, block in order_of(zip(parts, ks)):
            scr[s ^ k] = block.astype(F32)
        for c in range(3):
            wq_o[:, c * D:(c + 1) * D] = jnp.concatenate(
                [scr[p, :, c * cs:(c + 1) * cs] for p in range(S)], 1)
        total = as_rows(sum([scr[p, :, 3 * cs:] for p in range(1, S)], scr[0, :, 3 * cs:]))
        g1_o[...] = total[0:1, :].reshape(R)
        b1_o[...] = total[1:2, :].reshape(R)
        bqv_o[...] = jnp.concatenate([total[2:3, :], total[3:4, :]], 1).reshape(2 * R)

    def shards(tokens, segments, ln1_gain, ln1_bias, w_qkv, bias_qv, w_out, bias_out,
               ln2_gain, ln2_bias, w_in, bias_in, w_down, bias_down, cotangent):
        _, t, D = tokens.shape
        FF = w_in.shape[1]
        L = t * S
        cs = D // S
        R = D // NB
        FJ = FF // (NB * S)
        NF = NB * FJ
        x_own = tokens.reshape(t, D)
        cot_own = cotangent.reshape(t, D)

        wide_u, wide_a = -(-(NF + cs + 8) // 128) * 128, -(-(3 * cs + 8) // 128) * 128
        vec_out = sds((R,), F32)
        v = {}
        token = [None]

        def wait(*names):
            vals = tuple(v[n] for n in names)
            if token[0] is not None:
                vals, _ = lax.optimization_barrier((vals, token[0]))
            return vals

        def kernel(body, outs, args, name, scratch=(), limit=24, us=1):
            return pl.pallas_call(
                body, out_shape=outs, scratch_shapes=list(scratch), name=name,
                cost_estimate=pl.CostEstimate(flops=us * 10**9, bytes_accessed=us * 2 * 10**6, transcendentals=0),
                compiler_params=pltpu.CompilerParams(vmem_limit_bytes=limit * MIB))(*args)

        def prep_qkv():
            at = lax.broadcasted_iota(jnp.int32, (8, D), 0)
            pack1 = jnp.pad(segments.astype(F32), ((0, 0), (0, D - L)))
            for i, vec in enumerate((ln1_gain, ln1_bias, bias_qv[:D], bias_qv[D:])):
                pack1 = jnp.where(at == i, vec[None, :], pack1)
            v["wq"], v["pack1"], v["row"], v["col"] = kernel(
                prep_qkv_kernel, [sds((D, 3 * cs), BF), sds((8, D), F32), sds((8, L), F32), sds((L, 128), F32)],
                [w_qkv, pack1], "prep_qkv")
            cot_late, _ = lax.optimization_barrier((cot_own, v["col"]))
            v["cots"] = tuple(gather_seq(cot_late, S))

        def attn_fwd():
            near, far = sds((t // 2, 2 * cs), BF), sds(((L - t) // 2, 2 * cs), BF)
            v["qkv"], v["lse"], v["attn"], *sends = kernel(
                attn_fwd_kernel,
                [sds((L, 3 * cs), BF), sds((L, 128), F32), sds((L, cs), BF)] + [near] * (S - 1) + [far] * (S - 1),
                v["xs"] + wait("row", "col", "pack1", "wq"), "attn_fwd", us=6)
            v["nears"] = tuple(exchange(sends[m - 1], "seq", S, m) for m in range(1, S))
            far_sends, _ = lax.optimization_barrier((tuple(sends[S - 1:]), sends[0]))
            v["fars"] = tuple(exchange(far_sends[m - 1], "seq", S, m) for m in range(1, S))
            token[0] = v["attn"]

        def cots(*ks):
            def run():
                got = list(v["cots"])
                vals, _ = lax.optimization_barrier((tuple(got[k] for k in ks), token[0]))
                for k, g in zip(ks, vals):
                    got[k] = g
                v["cots"] = tuple(got)
                token[0] = got[ks[-1]]
            return run

        def prep_mlp():
            (w,) = wait("w_in")
            v["win_s"], v["wout_s"], v["wdn_s"], v["bin_s"] = kernel(
                prep_mlp_kernel, [sds((D, NF), BF), sds((D, D), BF), sds((NF, D), BF), sds((1, NF), F32)],
                [w, w_out, w_down, bias_in], "prep_mlp")
            token[0] = v["bin_s"]

        def local():
            (nears,) = wait("nears")
            v["act"], v["x1"], v["dx1"], v["vec"], *both = kernel(
                local_kernel,
                [sds((t, FF), BF), sds((t, D), F32), sds((t, D), F32), sds((8, D), F32)]
                + [sds((t, 2 * cs), BF)] * S,
                (x_own, v["attn"]) + nears + (cot_own, w_out, bias_out, ln2_gain, ln2_bias, w_in, bias_in, w_down),
                "local", limit=20, us=5)
            v["nears"] = nears
            v["boths"] = (both[0],) + tuple(exchange(both[k], "seq", S, k) for k in range(1, S))
            token[0] = v["dx1"]

        def fars():
            (v["fars"],) = wait("fars")
            token[0] = v["fars"][0]

        def up():
            nears, fars, cots = wait("nears", "fars", "cots")
            v["cots"] = cots
            v["attn_all"], v["h2"], v["slope"], v["d_keep"], v["d_send"] = kernel(
                up_kernel,
                [sds((L, D), BF), sds((L, D), BF), sds((L, NF), F32),
                 sds((NB // 2, FJ, D), BF), sds((NB // 2, FJ, D), BF)],
                v["xs"] + (v["attn"],) + nears + fars + cots
                + (v["wout_s"], bias_out, ln2_gain, ln2_bias, v["win_s"], v["bin_s"]), "up",
                [pltpu.VMEM((L, NF), BF), pltpu.VMEM((L, D), BF), pltpu.VMEM((NB, FJ, D), F32)], 32)
            v["d_got"] = exchange(v["d_send"], "batch", NB, 1)
            token[0] = v["d_keep"]

        def both():
            (v["boths"],) = wait("boths")
            token[0] = v["boths"][1]

        def down():
            boths, h2 = wait("boths", "h2")
            v["u_keep"], v["u_send"] = kernel(
                down_kernel, [sds((NB // 2, R, wide_u), BF), sds((NB // 2, R, wide_u), BF)],
                v["cots"] + boths + (h2, v["slope"], v["wdn_s"], v["attn_all"], v["vec"]), "down",
                [pltpu.VMEM((L, NF), BF), pltpu.VMEM((L, cs), BF), pltpu.VMEM((NB, R, wide_u), F32)], 32)
            v["u_got"] = exchange(v["u_send"], "batch", NB, 1)
            token[0] = v["u_keep"]

        def attn_bwd():
            boths, qkv = wait("boths", "qkv")
            v["own"], v["beside"], away, v["a_keep"], v["a_send"] = kernel(
                attn_bwd_kernel,
                [sds((t, D), F32), sds((t, D), F32), sds((S - 2, t, D), BF),
                 sds((NB // 2, R, wide_a), BF), sds((NB // 2, R, wide_a), BF)],
                v["xs"] + boths + (v["row"], v["col"], v["pack1"], v["wq"], qkv, v["lse"]), "attn_bwd",
                [pltpu.VMEM((L, D), BF), pltpu.VMEM((L, 3 * cs), BF), pltpu.VMEM((NB, R, wide_a), F32)], 32)
            v["a_got"] = exchange(v["a_send"], "batch", NB, 1)
            v["h_got"] = exchange(away, "seq", S, DH[0])
            token[0] = v["a_keep"]

        def halve(name, level):
            def run():
                got, keep = wait(name + "_got", name + "_keep")
                n = keep.shape[0]
                total = lambda lo, hi: (keep[lo:hi].astype(F32) + got[lo:hi].astype(F32)).astype(BF)
                if n > 1:
                    v[name + "_keep"], send = total(0, n // 2), total(n // 2, n)
                    v[name + "_got"] = exchange(send, "batch", NB, hops[name][level + 1])
                    token[0] = send
                    return
                mine = total(0, 1)[0]
                token[0] = mine
                if GATHER[name] is None:
                    v[name + "_all"] = gather_seq(mine, S)
                    v[name + "_ks"] = [[k] for k in range(S)]
                else:
                    first, second = GATHER[name]
                    v[name + "_all"] = [mine, exchange(mine, "seq", S, first)]
                    v[name + "_ks"] = [[0], [first], [second, first ^ second]]
            return run

        def spread(name):
            def run():
                if GATHER[name] is None:
                    return
                (parts,) = wait(name + "_all")
                pair = jnp.stack(parts)
                v[name + "_all"] = list(parts) + [exchange(pair, "seq", S, GATHER[name][1])]
                token[0] = pair
            return run

        def d_final():
            (parts,) = wait("d_all")
            v["o_wdn"], = kernel(
                functools.partial(down_final_kernel, v["d_ks"]), [sds((S * FJ, D), F32)], parts, "down_final")
            token[0] = v["o_wdn"]

        def u_final():
            (parts,) = wait("u_all")
            v["o_u"] = kernel(
                functools.partial(up_final_kernel, v["u_ks"]),
                [sds((R, FF), F32), sds((R, D), F32)] + [vec_out] * 4 + [sds((S * FJ,), F32)],
                parts, "up_final", [pltpu.VMEM((S, R, wide_u), F32)])
            token[0] = v["o_u"][0]

        def a_final():
            (parts,) = wait("a_all")
            v["o_a"] = kernel(
                functools.partial(att_final_kernel, v["a_ks"]),
                [sds((R, 3 * D), F32), vec_out, vec_out, sds((2 * R,), F32)],
                parts, "att_final", [pltpu.VMEM((S, R, wide_a), F32)])
            token[0] = v["o_a"][0]

        def h_first():
            (got,) = wait("h_got")
            beside = (v["beside"] + got[1].astype(F32)).astype(BF)
            v["own"] = v["own"] + got[0].astype(F32)
            v["h_got"] = exchange(beside, "seq", S, DH[1])
            token[0] = beside

        def h_last():
            (got,) = wait("h_got")
            unit1, scale1 = norm_parts(x_own.astype(F32))
            dh1 = v["own"] + got.astype(F32)
            v["d_tokens"] = v["dx1"] + norm_back(dh1, unit1, scale1, ln1_gain)
            token[0] = v["d_tokens"]

        def forward_out():
            x1, act = wait("x1", "act")
            v["out"], = kernel(out_kernel, [sds((t, D), BF)], [x1, act, w_down, bias_down], "out")
            token[0] = v["out"]

        v["xs"] = tuple(gather_seq(x_own, S))
        v["w_in"] = w_in
        steps = dict(
            pq=prep_qkv, af=attn_fwd, c1=cots(1), c2=cots(2), c3=cots(3), fa=fars, pm=prep_mlp, lo=local, up=up, bo=both,
            dn=down, bw=attn_bwd, d0=halve("d", 0), d1=halve("d", 1), d2=halve("d", 2), d3=spread("d"), d4=d_final,
            u0=halve("u", 0), u1=halve("u", 1), u2=halve("u", 2), u3=spread("u"), u4=u_final,
            a0=halve("a", 0), a1=halve("a", 1), a2=halve("a", 2), a3=spread("a"), a4=a_final,
            h1=h_first, h2=h_last, ou=forward_out)
        for name in ORDER:
            steps[name]()
        out, d_tokens, o_wdn = v["out"], v["d_tokens"].reshape(tokens.shape), v["o_wdn"]
        o_win, o_wout, o_bout, o_ln2g, o_ln2b, o_bdn, o_bin = v["o_u"]
        o_wqkv, o_ln1g, o_ln1b, o_bqv = v["o_a"]
        return (out.reshape(tokens.shape), d_tokens, o_ln1g, o_ln1b, o_wqkv, o_bqv, o_wout, o_bout,
                o_ln2g, o_ln2b, o_win, o_bin, o_wdn, o_bdn)
    return shards


def make_plain(S, NB):
    def shards(tokens, segments, ln1_gain, ln1_bias, w_qkv, bias_qv, w_out, bias_out,
               ln2_gain, ln2_bias, w_in, bias_in, w_down, bias_down, cotangent):
        rows, t, D = tokens.shape
        FF = w_in.shape[1]
        L = t * S
        hs = HEADS // S
        cs = hs * HEAD_DIM
        R = D // NB
        FJ = FF // (NB * S)
        scale = HEAD_DIM ** (-0.5)
        s = lax.axis_index("seq")
        b = lax.axis_index("batch")
        rel_s = jnp.arange(S, dtype=jnp.int32) ^ s
        rel_b = jnp.arange(NB, dtype=jnp.int32) ^ b

        x_own = tokens.reshape(t, D)
        cot_own = cotangent.reshape(t, D)
        wq_s = lax.dynamic_slice_in_dim(w_qkv.reshape(D, 3, S, cs), s, 1, 2).reshape(D, 3 * cs)
        bq_s = lax.dynamic_slice_in_dim(bias_qv.reshape(2, S, cs), s, 1, 1).reshape(2, cs)
        bqkv_s = jnp.concatenate([bq_s[0], jnp.zeros((cs,), F32), bq_s[1]])
        win_s = lax.dynamic_slice_in_dim(w_in.reshape(D, NB, S, FJ), s, 1, 2).reshape(D, NB * FJ)
        bin_s = lax.dynamic_slice_in_dim(bias_in.reshape(NB, S, FJ), s, 1, 1).reshape(NB * FJ)
        wdn_s = lax.dynamic_slice_in_dim(w_down.reshape(NB, S, FJ, D), s, 1, 1).reshape(NB * FJ, D)
        wout_rel = jnp.take(w_out.reshape(S, cs, D), rel_s, axis=0).reshape(D, D)
        seg_rel = jnp.take(segments.reshape(S, t), rel_s, axis=0).reshape(L)

        x_all = jnp.concatenate(gather_seq(x_own, S), 0)
        cot_in, x_all = lax.optimization_barrier((cot_own, x_all))
        cot_all = jnp.concatenate(gather_seq(cot_in, S), 0)

        x_f = x_all.astype(F32)
        unit1, scale1 = norm_parts(x_f)
        h1 = (unit1 * ln1_gain + ln1_bias).astype(BF)
        qkv = (dot(h1, wq_s) + bqkv_s).astype(BF)
        q = qkv[:, :cs].reshape(L, hs, HEAD_DIM)
        k = qkv[:, cs:2 * cs].reshape(L, hs, HEAD_DIM)
        v = qkv[:, 2 * cs:].reshape(L, hs, HEAD_DIM)
        mask = seg_rel[:, None] == seg_rel[None, :]
        scores = jnp.einsum("qhd,khd->hqk", q, k, preferred_element_type=F32) * scale
        scores = jnp.where(mask[None], scores, -1e30)
        top = jnp.max(scores, axis=-1, keepdims=True)
        expo = jnp.exp(scores - top)
        total = jnp.sum(expo, axis=-1, keepdims=True)
        probs = expo / total
        probs_low = probs.astype(BF)
        attn = jnp.einsum("hqk,khd->qhd", probs_low, v, preferred_element_type=F32).reshape(L, cs).astype(BF)

        got = gather_seq(attn, S)
        blocks = []
        for m, g in enumerate(got):
            g4 = g.reshape(S, t, cs)
            blocks.append(jnp.concatenate([g4[kk ^ m] for kk in range(S)], 0))
        attn_all = jnp.concatenate(blocks, 1)

        x1 = x_f + dot(attn_all, wout_rel) + bias_out
        unit2, scale2 = norm_parts(x1)
        h2 = (unit2 * ln2_gain + ln2_bias).astype(BF)

        u_s = dot(h2, win_s) + bin_s
        act_s, slope_s = gelu_both(u_s)
        act_s = act_s.astype(BF)
        dact_s = dot(cot_all, wdn_s, 1, 1)
        du_s = (dact_s * slope_s).astype(BF)
        g_win = dot(h2, du_s, 0, 0)
        g_wdn = dot(act_s, cot_all, 0, 0)
        g_bin = jnp.sum(du_s.astype(F32), 0)
        mlp = jnp.concatenate([g_win.reshape(NB, R, NB * FJ), g_wdn.reshape(NB, FJ, D)], 1).astype(BF)

        h2o = h2[:t]
        u = dot(h2o, w_in) + bias_in
        act, slope = gelu_both(u)
        act = act.astype(BF)
        activations = (x1[:t] + dot(act, w_down) + bias_down).astype(BF)
        dy = cot_own.astype(F32)
        du = (dot(cot_own, w_down, 1, 1) * slope).astype(BF)
        dh2 = dot(du, w_in, 1, 1)
        g_ln2g = jnp.sum(dh2 * unit2[:t], 0)
        g_ln2b = jnp.sum(dh2, 0)
        dx1 = dy + norm_back(dh2, unit2[:t], scale2[:t], ln2_gain)
        da = dx1.astype(BF)
        g_bout = jnp.sum(da.astype(F32), 0)
        g_bdn = jnp.sum(dy, 0)
        dattn = dot(da, wout_rel, 1, 1).astype(BF)
        da_rel = jnp.take(da.reshape(t, S, cs), rel_s, axis=1)
        both = [jnp.concatenate([dattn[:, kk * cs:(kk + 1) * cs], da_rel[:, kk]], 1) for kk in range(S)]
        both = jnp.concatenate([both[0]] + [exchange(both[kk], "seq", S, kk) for kk in range(1, S)], 0)
        dattn_all = both[:, :cs].reshape(L, hs, HEAD_DIM)
        da_s = both[:, cs:]

        log_total = top + jnp.log(total)
        p = jnp.exp(scores - log_total)
        p_low = p.astype(BF)
        dp = jnp.einsum("qhd,khd->hqk", dattn_all, v, preferred_element_type=F32)
        inner = jnp.sum(p * dp, axis=-1, keepdims=True)
        ds = (p * (dp - inner)).astype(BF)
        dq = jnp.einsum("hqk,khd->qhd", ds, k, preferred_element_type=F32) * scale
        dk = jnp.einsum("hqk,qhd->khd", ds, q, preferred_element_type=F32) * scale
        dv = jnp.einsum("hqk,qhd->khd", p_low, dattn_all, preferred_element_type=F32)
        dqkv = jnp.concatenate([dq.reshape(L, cs), dk.reshape(L, cs), dv.reshape(L, cs)], 1).astype(BF)

        dh1_part = dot(dqkv, wq_s, 1, 1)
        g_ln1g = jnp.sum(dh1_part * unit1, 0)
        g_ln1b = jnp.sum(dh1_part, 0)
        dh1_low = dh1_part.astype(BF)
        dh1 = dh1_part[:t]
        for kk in range(1, S):
            dh1 = dh1 + exchange(dh1_low[kk * t:(kk + 1) * t], "seq", S, kk).astype(F32)
        d_tokens = (dx1 + norm_back(dh1, unit1[:t], scale1[:t], ln1_gain)).reshape(tokens.shape)

        g_wqkv = dot(h1, dqkv, 0, 0)
        g_wout = dot(attn_all, da_s, 0, 0)
        g_wout = jnp.take(g_wout.reshape(S, cs, cs), rel_s, axis=0).reshape(D, cs)
        bsum = jnp.sum(dqkv.astype(F32), 0)
        g_bqv = jnp.zeros((2, S, cs), F32)
        g_bqv = lax.dynamic_update_slice(g_bqv, jnp.stack([bsum[:cs], bsum[2 * cs:]])[:, None], (0, s, 0))
        small = jnp.concatenate(
            [v_.reshape(NB, -1) for v_ in (g_ln1g, g_ln1b, g_bqv, g_bout, g_ln2g, g_ln2b, g_bdn, g_bin)], 1)
        small_n = small.shape[1]
        small_rows = -(-small_n // D)
        pad_rows = -(-small_rows // 16) * 16
        small = jnp.pad(small, ((0, 0), (0, pad_rows * D - small_n))).reshape(NB, pad_rows, D)
        att = jnp.concatenate(
            [jnp.concatenate([g_wqkv.reshape(NB, R, 3 * cs), g_wout.reshape(NB, R, cs)], 2), small], 1).astype(BF)

        def reduce_batch(buf):
            buf = jnp.take(buf, rel_b, axis=0).reshape((NB // 2, 2) + buf.shape[1:])
            buf = (buf[:, 0].astype(F32) + exchange(buf[:, 1], "batch", NB, 1).astype(F32)).astype(BF)
            n = NB // 2
            while n > 4:
                n //= 2
                buf = (buf[:n].astype(F32) + exchange(buf[n:], "batch", NB, 2 * n).astype(F32)).astype(BF)
            acc = buf[0].astype(F32)
            for m in range(1, n):
                acc = acc + exchange(buf[m], "batch", NB, 2 * m).astype(F32)
            parts = jnp.stack(gather_seq(acc.astype(BF), S))
            return jnp.take(parts, rel_s, axis=0).astype(F32)

        mlp = reduce_batch(mlp)
        att = reduce_batch(att)
        o_win = mlp[:, :R].reshape(S, R, NB, FJ).transpose(1, 2, 0, 3).reshape(R, FF)
        o_wdn = mlp[:, R:].reshape(S * FJ, D)
        o_wqkv = att[:, :R, :3 * cs].reshape(S, R, 3, cs).transpose(1, 2, 0, 3).reshape(R, 3 * D)
        o_wout = att[:, :R, 3 * cs:].transpose(1, 0, 2).reshape(R, D)
        flat = att[:, R:].reshape(S, -1)
        o_bin = flat[:, 8 * R:8 * R + FJ].reshape(S * FJ)
        tot = jnp.sum(flat[:, :8 * R], 0)
        o_ln1g, o_ln1b, o_bqv, o_bout, o_ln2g, o_ln2b, o_bdn = (
            tot[:R], tot[R:2 * R], tot[2 * R:4 * R], tot[4 * R:5 * R], tot[5 * R:6 * R], tot[6 * R:7 * R], tot[7 * R:])
        return (activations.reshape(tokens.shape), d_tokens, o_ln1g, o_ln1b, o_wqkv, o_bqv, o_wout, o_bout,
                o_ln2g, o_ln2b, o_win, o_bin, o_wdn, o_bdn)
    return shards


def solution(mesh):
    S, NB = mesh.shape["seq"], mesh.shape["batch"]
    shards = (make if BLOCK_ROWS // NB % 32 == 0 else make_plain)(S, NB)
    rowwise = P("batch", "seq", None)
    placed = (rowwise, P("batch", None)) + (P(),) * 12 + (rowwise,)
    b, bn = P("batch"), P("batch", None)
    return jax.shard_map(
        shards,
        mesh=mesh,
        in_specs=placed,
        out_specs=(rowwise, rowwise, b, b, bn, b, bn, b, b, b, bn, b, bn, b),
        check_vma=False,
    )
```

```python
import functools

import jax
import jax.numpy as jnp
from jax import lax
from jax.experimental import pallas as pl
from jax.experimental.pallas import tpu as pltpu
from jax.sharding import PartitionSpec as P

HEADS = 12
HEAD_DIM = 64
BLOCK_ROWS = HEADS * HEAD_DIM
BF = jnp.bfloat16
F32 = jnp.float32
MIB = 1 << 20


def dot(a, b, ca=1, cb=0):
    return lax.dot_general(a, b, (((ca,), (cb,)), ((), ())), preferred_element_type=F32)


def exchange(value, axis, size, step):
    return lax.ppermute(value, axis, [(j, j ^ step) for j in range(size)])


def gather_seq(value, size):
    return [value] + [exchange(value, "seq", size, k) for k in range(1, size)]


def norm_parts(values):
    mean = jnp.mean(values, axis=-1, keepdims=True)
    centred = values - mean
    var = jnp.mean(centred * centred, axis=-1, keepdims=True)
    scale = lax.rsqrt(var + 1e-06)
    return centred * scale, scale


def norm_back(grad, unit, scale, gain):
    grad = grad * gain
    mean = jnp.mean(grad, axis=-1, keepdims=True)
    along = jnp.mean(grad * unit, axis=-1, keepdims=True)
    return (grad - mean - unit * along) * scale


def gelu_both(v):
    c = 0.7978845608028654
    square = v * v
    t = jnp.tanh(c * v * (1.0 + 0.044715 * square))
    half = 0.5 * (1.0 + t)
    slope = half + (0.5 * c) * v * (1.0 - t * t) * (1.0 + 3.0 * 0.044715 * square)
    return v * half, slope


def call(kernel, outs, args, name, flops=0, limit=24):
    size = sum(a.size * a.dtype.itemsize for a in args) + sum(o.size * o.dtype.itemsize for o in outs)
    return pl.pallas_call(
        kernel,
        out_shape=outs,
        name=name,
        cost_estimate=pl.CostEstimate(flops=flops, bytes_accessed=size, transcendentals=0),
        compiler_params=pltpu.CompilerParams(vmem_limit_bytes=limit * MIB),
    )(*args)


def sds(shape, dtype):
    return jax.ShapeDtypeStruct(shape, dtype)


HOPS = {"d": "far", "u": "near", "a": "near"}
GATHER = {"d": None, "u": None, "a": None}
DH = (1, 2)
ORDER = "pq cs t2 t1 af fs c1 pm c2 c3 lo fa up dn d0 u0 bw ou d1 u1 a0 h1 d2 h2 a1 u2 d3 d4 a2 u3 u4 a3 a4".split()


def flat(ref):
    return ref[...].reshape(1, -1)


def make(S, NB):
    near_first = [2 ** i for i in range(NB.bit_length() - 1)]
    far_first = near_first[:1] + near_first[:0:-1]
    hops = {k: near_first if v == "near" else far_first for k, v in HOPS.items()}

    def rel_row(row, t):
        s = lax.axis_index("seq")
        parts = [row[:, i * t:(i + 1) * t] for i in range(S)]
        bit = 1
        while bit < S:
            on = (s & bit) != 0
            parts = [jnp.where(on, parts[i ^ bit], parts[i]) for i in range(S)]
            bit *= 2
        return jnp.concatenate(parts, 1)

    def prep_qkv_kernel(wqkv, wq_o):
        D = wqkv.shape[0]
        cs = D // S
        s = lax.axis_index("seq")
        for p in range(S):
            @pl.when(s == p)
            def _(p=p):
                for c in range(3):
                    wq_o[:, c * cs:(c + 1) * cs] = wqkv[:, c * D + p * cs:c * D + (p + 1) * cs]

    def prep_mlp_kernel(win, wout, wdown, bin_, win_o, wout_o, wdn_o, bin_o):
        D = wout.shape[0]
        FF = win.shape[1]
        cs = D // S
        FJ = FF // (NB * S)
        s = lax.axis_index("seq")
        vin = flat(bin_)
        for m in range(S):
            wout_o[m * cs:(m + 1) * cs, :] = wout[pl.ds(pl.multiple_of((s ^ m) * cs, 16), cs), :]
        for i in range(NB):
            wdn_o[i * FJ:(i + 1) * FJ, :] = wdown[pl.ds(pl.multiple_of((i * S + s) * FJ, 16), FJ), :]
        for p in range(S):
            @pl.when(s == p)
            def _(p=p):
                for i in range(NB):
                    at = (i * S + p) * FJ
                    win_o[:, i * FJ:(i + 1) * FJ] = win[:, at:at + FJ]
                    bin_o[:, i * FJ:(i + 1) * FJ] = vin[:, at:at + FJ]

    def turn_kernel(w, o):
        rows, cols = w.shape
        step = min(rows, cols)
        for i in range(0, rows, step):
            for j in range(0, cols, step):
                o[j:j + step, i:i + step] = jnp.transpose(w[i:i + step, j:j + step])

    def attn_fwd_kernel(*refs):
        xs, (seg_ref, g_ref, b_ref, bqv, wq_ref) = refs[:S], refs[S:S + 5]
        qkv_o, lse_o, row_o, col_o, attn_o = refs[S + 5:S + 10]
        near_o, far_o, bias_s = refs[S + 10:2 * S + 9], refs[2 * S + 9:3 * S + 8], refs[3 * S + 8]
        t, D = xs[0].shape
        L = S * t
        cs = D // S
        s = lax.axis_index("seq")
        gain, shift, bias = flat(g_ref), flat(b_ref), flat(bqv)
        for p in range(S):
            @pl.when(s == p)
            def _(p=p):
                zero = jnp.zeros((1, cs), F32)
                bias_s[...] = jnp.concatenate(
                    [bias[:, p * cs:(p + 1) * cs], zero, bias[:, D + p * cs:D + (p + 1) * cs]], 1)
        row = rel_row(seg_ref[...], t).astype(F32)
        row_o[...] = jnp.broadcast_to(row, row_o.shape)
        col_o[...] = jnp.transpose(jnp.broadcast_to(row, (128, L)))
        for k in range(S):
            unit, _ = norm_parts(xs[k][...].astype(F32))
            h1 = (unit * gain + shift).astype(BF)
            qkv_o[k * t:(k + 1) * t, :] = (dot(h1, wq_ref[...]) + bias_s[...]).astype(BF)
        heads = cs // HEAD_DIM
        outs = [[None] * heads for _ in range(S)]
        def part(c, h, rows=slice(None)):
            return qkv_o[rows, c * cs + h * HEAD_DIM:c * cs + (h + 1) * HEAD_DIM]
        def soft(sc, rows, h):
            sc = jnp.where(col_o[rows, :1] == row, sc, -1e30)
            top = jnp.max(sc, axis=-1, keepdims=True)
            ex = jnp.exp(sc - top)
            total = jnp.sum(ex, axis=-1, keepdims=True)
            lse_o[rows, h:h + 1] = top + jnp.log(total)
            return (ex * (1.0 / total)).astype(BF)
        def put(o, h, n):
            o = o.astype(BF)
            for r in range(o.shape[0] // t):
                outs[n + r][h] = o[r * t:(r + 1) * t]
        Q = 256
        todo = [(h, n) for h in range(heads) for n in range(L // Q)]
        def score(h, n):
            return dot(part(0, h, slice(n * Q, (n + 1) * Q)) * BF(HEAD_DIM ** -0.5), part(1, h), 1, 1)
        nxt = score(*todo[0])
        prev = None
        for i, (h, n) in enumerate(todo):
            cur = nxt
            if i + 1 < len(todo):
                nxt = score(*todo[i + 1])
            pr = soft(cur, slice(n * Q, (n + 1) * Q), h)
            if prev is not None:
                put(dot(prev[0], part(2, prev[1])), prev[1], prev[2])
            prev = (pr, h, n * Q // t)
        put(dot(prev[0], part(2, prev[1])), prev[1], prev[2])
        blocks = [jnp.concatenate(o, 1) for o in outs]
        for k in range(S):
            attn_o[k * t:(k + 1) * t, :] = blocks[k]
        for m in range(1, S):
            near_o[m - 1][...] = fold(blocks[m])
            far_o[m - 1][...] = fold(jnp.concatenate([blocks[k ^ m] for k in range(1, S)], 0))

    def fold(block):
        half = block.shape[0] // 2
        return jnp.concatenate([block[:half], block[half:]], 1)

    def unfold(block):
        half = block.shape[1] // 2
        return jnp.concatenate([block[:, :half], block[:, half:]], 0)

    def order(steps):
        ms = [0]
        for step in reversed(steps):
            ms = ms + [m ^ step for m in ms]
        return ms

    def store_blocks(scr, keep_o, send_o, b, steps):
        for p, m in enumerate(order(steps)):
            o, at = (keep_o, p) if p < NB // 2 else (send_o, p - NB // 2)
            o[at] = scr[b ^ m].astype(BF)

    def up_kernel(*refs):
        xs, (own,), nears, fars, cots = refs[:S], refs[S:S + 1], refs[S + 1:2 * S], refs[2 * S:3 * S - 1], refs[3 * S - 1:4 * S - 1]
        (wout, bout, g_ref, b_ref, win, bin_ref, attn_all, h2_o, slope_o, keep_o, send_o,
         act_s, cot_s, gw_s) = refs[4 * S - 1:]
        t, D = xs[0].shape
        cs = D // S
        FJ = win.shape[1] // NB
        b = lax.axis_index("batch")
        attn_all[:t, :] = jnp.concatenate([own[:t, :]] + [unfold(r[...]) for r in nears], 1)
        attn_all[t:, :] = jnp.concatenate([own[t:, :]] + [unfold(r[...]) for r in fars], 1)
        for k in range(S):
            cot_s[k * t:(k + 1) * t, :] = cots[k][...]
        x = jnp.concatenate([x[...].astype(F32) for x in xs], 0)
        x1 = x + dot(attn_all[...], wout[...]) + flat(bout)
        unit, _ = norm_parts(x1)
        h2 = (unit * flat(g_ref) + flat(b_ref)).astype(BF)
        h2_o[...] = h2
        act, slope = gelu_both(dot(h2, win[...]) + bin_ref[...])
        act_s[...] = act.astype(BF)
        slope_o[...] = slope
        gw_s[...] = dot(act_s[...], cot_s[...], 0, 0).reshape(NB, FJ, D)
        store_blocks(gw_s, keep_o, send_o, b, hops["d"])

    def down_kernel(*refs):
        cots, boths = refs[:S], refs[S:2 * S]
        h2, slope, wdn, attn_all, vec, keep_o, send_o, du_s, da_s, gw_s = refs[2 * S:]
        t, D = cots[0].shape
        R = D // NB
        cs = D // S
        NF = slope.shape[1]
        s = lax.axis_index("seq")
        b = lax.axis_index("batch")
        for k in range(S):
            da_s[k * t:(k + 1) * t, :] = boths[k][:, cs:]
        cot = jnp.concatenate([c[...] for c in cots], 0)
        du = (dot(cot, wdn[...], 1, 1) * slope[...]).astype(BF)
        du_s[...] = du
        gbin = jnp.sum(du.astype(F32), axis=0, keepdims=True)
        gw_s[:, :, :NF] = dot(h2[...], du_s[...], 0, 0).reshape(NB, R, NF)
        go = dot(attn_all[...], da_s[...], 0, 0)
        per = NB // S
        for m in range(S):
            for j in range(per):
                gw_s[(s ^ m) * per + j, :, NF:NF + cs] = go[m * cs + j * R:m * cs + (j + 1) * R, :]
        gw_s[:, :, NF + cs:] = columns([vec[:4, :], gbin], gw_s.shape[2] - NF - cs)
        store_blocks(gw_s, keep_o, send_o, b, hops["u"])

    def columns(rows, width):
        rows = jnp.concatenate(rows, 0)
        D = rows.shape[1]
        rows = jnp.concatenate([rows, jnp.zeros((128 - rows.shape[0], D), F32)], 0)
        return jnp.transpose(rows)[:, :width].reshape(NB, D // NB, width)

    def local_kernel(*refs):
        x_ref, own, nears, refs = refs[0], refs[1], refs[2:1 + S], refs[1 + S:]
        cot_ref, wout, bout, g_ref, b_ref, win, bin_ref, win_t, wdown_t = refs[:9]
        act_o, x1_o, dx1_o, vec_o = refs[9:13]
        both = refs[13:]
        t, D = x_ref.shape
        FF = win.shape[1]
        cs = D // S
        s = lax.axis_index("seq")
        heads = [wout[pl.ds(pl.multiple_of((s ^ m) * cs, 16), cs), :] for m in range(S)]
        attn = [own[:t, :]] + [unfold(r[...]) for r in nears]
        x1 = x_ref[...].astype(F32) + flat(bout)
        for m in range(S):
            x1 = x1 + dot(attn[m], heads[m])
        unit, scale = norm_parts(x1)
        h2 = (unit * flat(g_ref) + flat(b_ref)).astype(BF)
        cot = cot_ref[...]
        bias_in = flat(bin_ref)
        x1_o[...] = x1
        dh2 = jnp.zeros((t, D), F32)
        for c in range(FF // D):
            cols = slice(c * D, (c + 1) * D)
            act, slope = gelu_both(dot(h2, win[:, cols]) + bias_in[:, cols])
            act_o[:, cols] = act.astype(BF)
            du = (dot(cot, wdown_t[:, cols]) * slope).astype(BF)
            dh2 = dh2 + dot(du, win_t[cols, :])
        dy = cot.astype(F32)
        dx1 = dy + norm_back(dh2, unit, scale, flat(g_ref))
        dx1_o[...] = dx1
        da = dx1.astype(BF)
        vec_o[...] = jnp.concatenate([
            jnp.sum(da.astype(F32), axis=0, keepdims=True),
            jnp.sum(dh2 * unit, axis=0, keepdims=True),
            jnp.sum(dh2, axis=0, keepdims=True),
            jnp.sum(dy, axis=0, keepdims=True),
            jnp.zeros((4, D), F32)], 0)
        parts = [da[:, i * cs:(i + 1) * cs] for i in range(S)]
        bit = 1
        while bit < S:
            on = (s & bit) != 0
            parts = [jnp.where(on, parts[i ^ bit], parts[i]) for i in range(S)]
            bit *= 2
        for k in range(S):
            both[k][...] = jnp.concatenate([dot(da, heads[k], 1, 1).astype(BF), parts[k]], 1)

    def out_kernel(x1_ref, act, wdown, bdown, out_o):
        out_o[...] = (x1_ref[...] + dot(act[...], wdown[...]) + flat(bdown)).astype(BF)

    def attn_bwd_kernel(*refs):
        xs, boths = refs[:S], refs[S:2 * S]
        row_ref, col_ref, g_ref, b_ref, wq, qkv, lse = refs[2 * S:2 * S + 7]
        own_o, next_o, away_o, keep_o, send_o, h1_s, dqkv_s, gw_s = refs[2 * S + 7:]
        t, D = xs[0].shape
        L = S * t
        cs = D // S
        R = D // NB
        s = lax.axis_index("seq")
        b = lax.axis_index("batch")
        scale = HEAD_DIM ** -0.5
        row = row_ref[0:1, :]
        dattn = jnp.concatenate([r[:, :cs] for r in boths], 0)
        dattn_t = jnp.transpose(dattn)
        q_t = jnp.transpose(qkv[:, :cs] * BF(scale))
        Q = 512
        heads = cs // HEAD_DIM
        todo = [(h, n) for h in range(heads) for n in range(L // Q)]

        def part(c, h, rows=slice(None)):
            return qkv[rows, c * cs + h * HEAD_DIM:c * cs + (h + 1) * HEAD_DIM]

        def products(h, n):
            rows = slice(n * Q, (n + 1) * Q)
            return (dot(part(0, h, rows) * BF(scale), part(1, h), 1, 1),
                    dot(dattn[rows, h * HEAD_DIM:(h + 1) * HEAD_DIM], part(2, h), 1, 1))

        def slopes(sc, dp, h, n):
            rows = slice(n * Q, (n + 1) * Q)
            sc = jnp.where(col_ref[rows, :1] == row, sc, -1e30)
            p = jnp.exp(sc - lse[rows, h:h + 1])
            inner = jnp.sum(p * dp, axis=-1, keepdims=True)
            return p.astype(BF), (p * (dp - inner)).astype(BF)

        dk = [jnp.zeros((HEAD_DIM, L), F32) for _ in range(heads)]
        dv = [jnp.zeros((HEAD_DIM, L), F32) for _ in range(heads)]

        def gradients(p, ds, h, n):
            rows = slice(n * Q, (n + 1) * Q)
            at = h * HEAD_DIM
            dqkv_s[rows, at:at + HEAD_DIM] = dot(ds, part(1, h) * BF(scale)).astype(BF)
            dk[h] = dk[h] + dot(q_t[at:at + HEAD_DIM, rows], ds)
            dv[h] = dv[h] + dot(dattn_t[at:at + HEAD_DIM, rows], p)
            if n == L // Q - 1:
                dqkv_s[:, cs + at:cs + at + HEAD_DIM] = jnp.transpose(dk[h].astype(BF))
                dqkv_s[:, 2 * cs + at:2 * cs + at + HEAD_DIM] = jnp.transpose(dv[h].astype(BF))

        ahead = products(*todo[0])
        behind = None
        for i, at in enumerate(todo):
            now = ahead
            if i + 1 < len(todo):
                ahead = products(*todo[i + 1])
            p, ds = slopes(*now, *at)
            if behind is not None:
                gradients(*behind)
            behind = (p, ds) + at
        gradients(*behind)
        bsum = jnp.sum(dqkv_s[...].astype(F32), axis=0, keepdims=True)
        gg = jnp.zeros((1, D), F32)
        gb = jnp.zeros((1, D), F32)
        for k in range(S):
            rows = slice(k * t, (k + 1) * t)
            unit, _ = norm_parts(xs[k][...].astype(F32))
            h1_s[rows, :] = (unit * flat(g_ref) + flat(b_ref)).astype(BF)
            dh1 = dot(dqkv_s[rows, :], wq[...], 1, 1)
            gg = gg + jnp.sum(dh1 * unit, axis=0, keepdims=True)
            gb = gb + jnp.sum(dh1, axis=0, keepdims=True)
            if k == 0:
                own_o[...] = dh1
            elif k == DH[1]:
                next_o[...] = dh1
            else:
                away_o[int(k != DH[0])] = dh1.astype(BF)
        gw = dot(h1_s[...], dqkv_s[...], 0, 0)
        gw_s[:, :, :3 * cs] = gw.reshape(NB, R, 3 * cs)
        zero = jnp.zeros((1, cs), F32)
        wide_q = jnp.concatenate([jnp.where(s == i, bsum[:, :cs], zero) for i in range(S)], 1)
        wide_v = jnp.concatenate([jnp.where(s == i, bsum[:, 2 * cs:], zero) for i in range(S)], 1)
        wide = jnp.concatenate([wide_q, wide_v], 1)
        first = jnp.concatenate([wide[:, 2 * i * R:(2 * i + 1) * R] for i in range(NB)], 1)
        second = jnp.concatenate([wide[:, (2 * i + 1) * R:(2 * i + 2) * R] for i in range(NB)], 1)
        gw_s[:, :, 3 * cs:] = columns([gg, gb, first, second], gw_s.shape[2] - 3 * cs)
        store_blocks(gw_s, keep_o, send_o, b, hops["a"])

    def down_final_kernel(ks, *refs):
        parts, (wdn_o,) = refs[:-1], refs[-1:]
        FJ = parts[0].shape[0]
        s = lax.axis_index("seq")
        for k, block in order_of(zip(parts, ks)):
            wdn_o[pl.ds(pl.multiple_of((s ^ k) * FJ, 8), FJ), :] = block.astype(F32)

    def order_of(refs):
        out = []
        for ref, ks in refs:
            out += [(k, ref[...] if len(ks) == 1 else ref[i]) for i, k in enumerate(ks)]
        return out

    def up_final_kernel(ks, *refs):
        parts = refs[:len(ks)]
        win_o, wo_o, bo_o, g2_o, b2_o, bd_o, bin_o, scr = refs[len(ks):]
        R, FF = win_o.shape
        D = wo_o.shape[1]
        cs = D // S
        FJ = FF // (NB * S)
        NF = NB * FJ
        s = lax.axis_index("seq")
        for k, block in order_of(zip(parts, ks)):
            scr[s ^ k] = block.astype(F32)
        for i in range(NB):
            win_o[:, i * S * FJ:(i + 1) * S * FJ] = jnp.concatenate(
                [scr[p, :, i * FJ:(i + 1) * FJ] for p in range(S)], 1)
        wo_o[...] = jnp.concatenate([scr[p, :, NF:NF + cs] for p in range(S)], 1)
        vecs = [as_rows(scr[p, :, NF + cs:]) for p in range(S)]
        total = sum(vecs[1:], vecs[0])
        for i, o in enumerate((bo_o, g2_o, b2_o, bd_o)):
            o[...] = total[i:i + 1, :].reshape(R)
        bin_o[...] = jnp.concatenate([v[4:5, :] for v in vecs], 1).reshape(S * FJ)

    def as_rows(cols):
        R, width = cols.shape
        cols = jnp.concatenate([cols, jnp.zeros((R, 128 - width), F32)], 1)
        cols = jnp.concatenate([cols, jnp.zeros((128 - R, 128), F32)], 0)
        return jnp.transpose(cols)[:8, :R]

    def att_final_kernel(ks, *refs):
        parts = refs[:len(ks)]
        wq_o, g1_o, b1_o, bqv_o, scr = refs[len(ks):]
        R = wq_o.shape[0]
        D = wq_o.shape[1] // 3
        cs = D // S
        s = lax.axis_index("seq")
        for k, block in order_of(zip(parts, ks)):
            scr[s ^ k] = block.astype(F32)
        for c in range(3):
            wq_o[:, c * D:(c + 1) * D] = jnp.concatenate(
                [scr[p, :, c * cs:(c + 1) * cs] for p in range(S)], 1)
        total = as_rows(sum([scr[p, :, 3 * cs:] for p in range(1, S)], scr[0, :, 3 * cs:]))
        g1_o[...] = total[0:1, :].reshape(R)
        b1_o[...] = total[1:2, :].reshape(R)
        bqv_o[...] = jnp.concatenate([total[2:3, :], total[3:4, :]], 1).reshape(2 * R)

    def shards(tokens, segments, ln1_gain, ln1_bias, w_qkv, bias_qv, w_out, bias_out,
               ln2_gain, ln2_bias, w_in, bias_in, w_down, bias_down, cotangent):
        _, t, D = tokens.shape
        FF = w_in.shape[1]
        L = t * S
        cs = D // S
        R = D // NB
        FJ = FF // (NB * S)
        NF = NB * FJ
        x_own = tokens.reshape(t, D)
        cot_own = cotangent.reshape(t, D)

        wide_u, wide_a = -(-(NF + cs + 8) // 128) * 128, -(-(3 * cs + 8) // 128) * 128
        vec_out = sds((R,), F32)
        v = {}
        token = [None]

        def wait(*names):
            vals = tuple(v[n] for n in names)
            if token[0] is not None:
                vals, _ = lax.optimization_barrier((vals, token[0]))
            return vals

        def kernel(body, outs, args, name, scratch=(), limit=24, us=1):
            return pl.pallas_call(
                body, out_shape=outs, scratch_shapes=list(scratch), name=name,
                cost_estimate=pl.CostEstimate(flops=us * 10**9, bytes_accessed=us * 2 * 10**6, transcendentals=0),
                compiler_params=pltpu.CompilerParams(vmem_limit_bytes=limit * MIB))(*args)

        def prep_qkv():
            v["wq"], = kernel(prep_qkv_kernel, [sds((D, 3 * cs), BF)], [w_qkv], "prep_qkv", us=8)
            token[0] = v["wq"]

        def attn_fwd():
            near, far = sds((t // 2, 2 * cs), BF), sds(((L - t) // 2, 2 * cs), BF)
            v["qkv"], v["lse"], v["row"], v["col"], v["attn"], *sends = kernel(
                attn_fwd_kernel,
                [sds((L, 3 * cs), BF), sds((L, 128), F32), sds((8, L), F32), sds((L, 128), F32), sds((L, cs), BF)]
                + [near] * (S - 1) + [far] * (S - 1),
                v["xs"] + (segments, ln1_gain, ln1_bias, bias_qv) + wait("wq"), "attn_fwd",
                [pltpu.VMEM((1, 3 * cs), F32)], us=6)
            v["nears"] = tuple(exchange(sends[m - 1], "seq", S, m) for m in range(1, S))
            v["far_sends"] = tuple(sends[S - 1:])
            token[0] = v["attn"]

        def cots_send():
            (cot,) = wait("cot")
            v["cots"] = tuple(gather_seq(cot, S))

        def fars_send():
            (sends,) = wait("far_sends")
            v["fars"] = tuple(exchange(sends[m - 1], "seq", S, m) for m in range(1, S))

        def cots(*ks):
            def run():
                got = list(v["cots"])
                vals, _ = lax.optimization_barrier((tuple(got[k] for k in ks), token[0]))
                for k, g in zip(ks, vals):
                    got[k] = g
                v["cots"] = tuple(got)
                token[0] = got[ks[-1]]
            return run

        def turn(name, source):
            def run():
                w = v[source]
                if token[0] is not None:
                    w, _ = lax.optimization_barrier((w, token[0]))
                v[name], = kernel(turn_kernel, [sds(w.shape[::-1], BF)], [w], name, us=2)
                token[0] = v[name]
            return run

        def prep_mlp():
            (w,) = wait("w_in")
            v["win_s"], v["wout_s"], v["wdn_s"], v["bin_s"] = kernel(
                prep_mlp_kernel, [sds((D, NF), BF), sds((D, D), BF), sds((NF, D), BF), sds((1, NF), F32)],
                [w, w_out, w_down, bias_in], "prep_mlp")
            token[0] = v["bin_s"]

        def local():
            (nears,) = wait("nears")
            v["act"], v["x1"], v["dx1"], v["vec"], *both = kernel(
                local_kernel,
                [sds((t, FF), BF), sds((t, D), F32), sds((t, D), F32), sds((8, D), F32)]
                + [sds((t, 2 * cs), BF)] * S,
                (x_own, v["attn"]) + nears + (cot_own, w_out, bias_out, ln2_gain, ln2_bias, w_in, bias_in, v["win_t"], v["wdown_t"]),
                "local", limit=20, us=5)
            v["nears"] = nears
            v["boths"] = (both[0],) + tuple(exchange(both[k], "seq", S, k) for k in range(1, S))
            token[0] = v["dx1"]

        def fars():
            (v["fars"],) = wait("fars")
            token[0] = v["fars"][0]

        def up():
            nears, fars, cots = wait("nears", "fars", "cots")
            v["cots"] = cots
            v["attn_all"], v["h2"], v["slope"], v["d_keep"], v["d_send"] = kernel(
                up_kernel,
                [sds((L, D), BF), sds((L, D), BF), sds((L, NF), F32),
                 sds((NB // 2, FJ, D), BF), sds((NB // 2, FJ, D), BF)],
                v["xs"] + (v["attn"],) + nears + fars + cots
                + (v["wout_s"], bias_out, ln2_gain, ln2_bias, v["win_s"], v["bin_s"]), "up",
                [pltpu.VMEM((L, NF), BF), pltpu.VMEM((L, D), BF), pltpu.VMEM((NB, FJ, D), F32)], 32)
            v["d_got"] = exchange(v["d_send"], "batch", NB, 1)
            token[0] = v["d_keep"]

        def both():
            (v["boths"],) = wait("boths")
            token[0] = v["boths"][1]

        def down():
            boths, h2 = wait("boths", "h2")
            v["u_keep"], v["u_send"] = kernel(
                down_kernel, [sds((NB // 2, R, wide_u), BF), sds((NB // 2, R, wide_u), BF)],
                v["cots"] + boths + (h2, v["slope"], v["wdn_s"], v["attn_all"], v["vec"]), "down",
                [pltpu.VMEM((L, NF), BF), pltpu.VMEM((L, cs), BF), pltpu.VMEM((NB, R, wide_u), F32)], 32)
            v["u_got"] = exchange(v["u_send"], "batch", NB, 1)
            token[0] = v["u_keep"]

        def attn_bwd():
            boths, qkv = wait("boths", "qkv")
            v["own"], v["beside"], away, v["a_keep"], v["a_send"] = kernel(
                attn_bwd_kernel,
                [sds((t, D), F32), sds((t, D), F32), sds((S - 2, t, D), BF),
                 sds((NB // 2, R, wide_a), BF), sds((NB // 2, R, wide_a), BF)],
                v["xs"] + boths + (v["row"], v["col"], ln1_gain, ln1_bias, v["wq"], qkv, v["lse"]), "attn_bwd",
                [pltpu.VMEM((L, D), BF), pltpu.VMEM((L, 3 * cs), BF), pltpu.VMEM((NB, R, wide_a), F32)], 32)
            v["a_got"] = exchange(v["a_send"], "batch", NB, 1)
            v["h_got"] = exchange(away, "seq", S, DH[0])
            token[0] = v["a_keep"]

        def halve(name, level):
            def run():
                got, keep = wait(name + "_got", name + "_keep")
                n = keep.shape[0]
                total = lambda lo, hi: (keep[lo:hi].astype(F32) + got[lo:hi].astype(F32)).astype(BF)
                if n > 1:
                    v[name + "_keep"], send = total(0, n // 2), total(n // 2, n)
                    v[name + "_got"] = exchange(send, "batch", NB, hops[name][level + 1])
                    token[0] = send
                    return
                mine = total(0, 1)[0]
                token[0] = mine
                if GATHER[name] is None:
                    v[name + "_all"] = gather_seq(mine, S)
                    v[name + "_ks"] = [[k] for k in range(S)]
                else:
                    first, second = GATHER[name]
                    v[name + "_all"] = [mine, exchange(mine, "seq", S, first)]
                    v[name + "_ks"] = [[0], [first], [second, first ^ second]]
            return run

        def spread(name):
            def run():
                if GATHER[name] is None:
                    return
                (parts,) = wait(name + "_all")
                pair = jnp.stack(parts)
                v[name + "_all"] = list(parts) + [exchange(pair, "seq", S, GATHER[name][1])]
                token[0] = pair
            return run

        def d_final():
            (parts,) = wait("d_all")
            v["o_wdn"], = kernel(
                functools.partial(down_final_kernel, v["d_ks"]), [sds((S * FJ, D), F32)], parts, "down_final")
            token[0] = v["o_wdn"]

        def u_final():
            (parts,) = wait("u_all")
            v["o_u"] = kernel(
                functools.partial(up_final_kernel, v["u_ks"]),
                [sds((R, FF), F32), sds((R, D), F32)] + [vec_out] * 4 + [sds((S * FJ,), F32)],
                parts, "up_final", [pltpu.VMEM((S, R, wide_u), F32)])
            token[0] = v["o_u"][0]

        def a_final():
            (parts,) = wait("a_all")
            v["o_a"] = kernel(
                functools.partial(att_final_kernel, v["a_ks"]),
                [sds((R, 3 * D), F32), vec_out, vec_out, sds((2 * R,), F32)],
                parts, "att_final", [pltpu.VMEM((S, R, wide_a), F32)])
            token[0] = v["o_a"][0]

        def h_first():
            (got,) = wait("h_got")
            beside = (v["beside"] + got[1].astype(F32)).astype(BF)
            v["own"] = v["own"] + got[0].astype(F32)
            v["h_got"] = exchange(beside, "seq", S, DH[1])
            token[0] = beside

        def h_last():
            (got,) = wait("h_got")
            unit1, scale1 = norm_parts(x_own.astype(F32))
            dh1 = v["own"] + got.astype(F32)
            v["d_tokens"] = v["dx1"] + norm_back(dh1, unit1, scale1, ln1_gain)
            token[0] = v["d_tokens"]

        def forward_out():
            x1, act = wait("x1", "act")
            v["out"], = kernel(out_kernel, [sds((t, D), BF)], [x1, act, w_down, bias_down], "out")
            token[0] = v["out"]

        v["xs"] = tuple(gather_seq(x_own, S))
        v["w_in"], v["w_down"], v["cot"] = w_in, w_down, cot_own
        steps = dict(
            pq=prep_qkv, af=attn_fwd, cs=cots_send, fs=fars_send, c1=cots(1), c2=cots(2), c3=cots(3), fa=fars, pm=prep_mlp, t1=turn("wdown_t", "w_down"), t2=turn("win_t", "w_in"), lo=local, up=up, bo=both,
            dn=down, bw=attn_bwd, d0=halve("d", 0), d1=halve("d", 1), d2=halve("d", 2), d3=spread("d"), d4=d_final,
            u0=halve("u", 0), u1=halve("u", 1), u2=halve("u", 2), u3=spread("u"), u4=u_final,
            a0=halve("a", 0), a1=halve("a", 1), a2=halve("a", 2), a3=spread("a"), a4=a_final,
            h1=h_first, h2=h_last, ou=forward_out)
        for name in ORDER:
            steps[name]()
        out, d_tokens, o_wdn = v["out"], v["d_tokens"].reshape(tokens.shape), v["o_wdn"]
        o_win, o_wout, o_bout, o_ln2g, o_ln2b, o_bdn, o_bin = v["o_u"]
        o_wqkv, o_ln1g, o_ln1b, o_bqv = v["o_a"]
        return (out.reshape(tokens.shape), d_tokens, o_ln1g, o_ln1b, o_wqkv, o_bqv, o_wout, o_bout,
                o_ln2g, o_ln2b, o_win, o_bin, o_wdn, o_bdn)
    return shards


def make_plain(S, NB):
    def shards(tokens, segments, ln1_gain, ln1_bias, w_qkv, bias_qv, w_out, bias_out,
               ln2_gain, ln2_bias, w_in, bias_in, w_down, bias_down, cotangent):
        rows, t, D = tokens.shape
        FF = w_in.shape[1]
        L = t * S
        hs = HEADS // S
        cs = hs * HEAD_DIM
        R = D // NB
        FJ = FF // (NB * S)
        scale = HEAD_DIM ** (-0.5)
        s = lax.axis_index("seq")
        b = lax.axis_index("batch")
        rel_s = jnp.arange(S, dtype=jnp.int32) ^ s
        rel_b = jnp.arange(NB, dtype=jnp.int32) ^ b

        x_own = tokens.reshape(t, D)
        cot_own = cotangent.reshape(t, D)
        wq_s = lax.dynamic_slice_in_dim(w_qkv.reshape(D, 3, S, cs), s, 1, 2).reshape(D, 3 * cs)
        bq_s = lax.dynamic_slice_in_dim(bias_qv.reshape(2, S, cs), s, 1, 1).reshape(2, cs)
        bqkv_s = jnp.concatenate([bq_s[0], jnp.zeros((cs,), F32), bq_s[1]])
        win_s = lax.dynamic_slice_in_dim(w_in.reshape(D, NB, S, FJ), s, 1, 2).reshape(D, NB * FJ)
        bin_s = lax.dynamic_slice_in_dim(bias_in.reshape(NB, S, FJ), s, 1, 1).reshape(NB * FJ)
        wdn_s = lax.dynamic_slice_in_dim(w_down.reshape(NB, S, FJ, D), s, 1, 1).reshape(NB * FJ, D)
        wout_rel = jnp.take(w_out.reshape(S, cs, D), rel_s, axis=0).reshape(D, D)
        seg_rel = jnp.take(segments.reshape(S, t), rel_s, axis=0).reshape(L)

        x_all = jnp.concatenate(gather_seq(x_own, S), 0)
        cot_in, x_all = lax.optimization_barrier((cot_own, x_all))
        cot_all = jnp.concatenate(gather_seq(cot_in, S), 0)

        x_f = x_all.astype(F32)
        unit1, scale1 = norm_parts(x_f)
        h1 = (unit1 * ln1_gain + ln1_bias).astype(BF)
        qkv = (dot(h1, wq_s) + bqkv_s).astype(BF)
        q = qkv[:, :cs].reshape(L, hs, HEAD_DIM)
        k = qkv[:, cs:2 * cs].reshape(L, hs, HEAD_DIM)
        v = qkv[:, 2 * cs:].reshape(L, hs, HEAD_DIM)
        mask = seg_rel[:, None] == seg_rel[None, :]
        scores = jnp.einsum("qhd,khd->hqk", q, k, preferred_element_type=F32) * scale
        scores = jnp.where(mask[None], scores, -1e30)
        top = jnp.max(scores, axis=-1, keepdims=True)
        expo = jnp.exp(scores - top)
        total = jnp.sum(expo, axis=-1, keepdims=True)
        probs = expo / total
        probs_low = probs.astype(BF)
        attn = jnp.einsum("hqk,khd->qhd", probs_low, v, preferred_element_type=F32).reshape(L, cs).astype(BF)

        got = gather_seq(attn, S)
        blocks = []
        for m, g in enumerate(got):
            g4 = g.reshape(S, t, cs)
            blocks.append(jnp.concatenate([g4[kk ^ m] for kk in range(S)], 0))
        attn_all = jnp.concatenate(blocks, 1)

        x1 = x_f + dot(attn_all, wout_rel) + bias_out
        unit2, scale2 = norm_parts(x1)
        h2 = (unit2 * ln2_gain + ln2_bias).astype(BF)

        u_s = dot(h2, win_s) + bin_s
        act_s, slope_s = gelu_both(u_s)
        act_s = act_s.astype(BF)
        dact_s = dot(cot_all, wdn_s, 1, 1)
        du_s = (dact_s * slope_s).astype(BF)
        g_win = dot(h2, du_s, 0, 0)
        g_wdn = dot(act_s, cot_all, 0, 0)
        g_bin = jnp.sum(du_s.astype(F32), 0)
        mlp = jnp.concatenate([g_win.reshape(NB, R, NB * FJ), g_wdn.reshape(NB, FJ, D)], 1).astype(BF)

        h2o = h2[:t]
        u = dot(h2o, w_in) + bias_in
        act, slope = gelu_both(u)
        act = act.astype(BF)
        activations = (x1[:t] + dot(act, w_down) + bias_down).astype(BF)
        dy = cot_own.astype(F32)
        du = (dot(cot_own, w_down, 1, 1) * slope).astype(BF)
        dh2 = dot(du, w_in, 1, 1)
        g_ln2g = jnp.sum(dh2 * unit2[:t], 0)
        g_ln2b = jnp.sum(dh2, 0)
        dx1 = dy + norm_back(dh2, unit2[:t], scale2[:t], ln2_gain)
        da = dx1.astype(BF)
        g_bout = jnp.sum(da.astype(F32), 0)
        g_bdn = jnp.sum(dy, 0)
        dattn = dot(da, wout_rel, 1, 1).astype(BF)
        da_rel = jnp.take(da.reshape(t, S, cs), rel_s, axis=1)
        both = [jnp.concatenate([dattn[:, kk * cs:(kk + 1) * cs], da_rel[:, kk]], 1) for kk in range(S)]
        both = jnp.concatenate([both[0]] + [exchange(both[kk], "seq", S, kk) for kk in range(1, S)], 0)
        dattn_all = both[:, :cs].reshape(L, hs, HEAD_DIM)
        da_s = both[:, cs:]

        log_total = top + jnp.log(total)
        p = jnp.exp(scores - log_total)
        p_low = p.astype(BF)
        dp = jnp.einsum("qhd,khd->hqk", dattn_all, v, preferred_element_type=F32)
        inner = jnp.sum(p * dp, axis=-1, keepdims=True)
        ds = (p * (dp - inner)).astype(BF)
        dq = jnp.einsum("hqk,khd->qhd", ds, k, preferred_element_type=F32) * scale
        dk = jnp.einsum("hqk,qhd->khd", ds, q, preferred_element_type=F32) * scale
        dv = jnp.einsum("hqk,qhd->khd", p_low, dattn_all, preferred_element_type=F32)
        dqkv = jnp.concatenate([dq.reshape(L, cs), dk.reshape(L, cs), dv.reshape(L, cs)], 1).astype(BF)

        dh1_part = dot(dqkv, wq_s, 1, 1)
        g_ln1g = jnp.sum(dh1_part * unit1, 0)
        g_ln1b = jnp.sum(dh1_part, 0)
        dh1_low = dh1_part.astype(BF)
        dh1 = dh1_part[:t]
        for kk in range(1, S):
            dh1 = dh1 + exchange(dh1_low[kk * t:(kk + 1) * t], "seq", S, kk).astype(F32)
        d_tokens = (dx1 + norm_back(dh1, unit1[:t], scale1[:t], ln1_gain)).reshape(tokens.shape)

        g_wqkv = dot(h1, dqkv, 0, 0)
        g_wout = dot(attn_all, da_s, 0, 0)
        g_wout = jnp.take(g_wout.reshape(S, cs, cs), rel_s, axis=0).reshape(D, cs)
        bsum = jnp.sum(dqkv.astype(F32), 0)
        g_bqv = jnp.zeros((2, S, cs), F32)
        g_bqv = lax.dynamic_update_slice(g_bqv, jnp.stack([bsum[:cs], bsum[2 * cs:]])[:, None], (0, s, 0))
        small = jnp.concatenate(
            [v_.reshape(NB, -1) for v_ in (g_ln1g, g_ln1b, g_bqv, g_bout, g_ln2g, g_ln2b, g_bdn, g_bin)], 1)
        small_n = small.shape[1]
        small_rows = -(-small_n // D)
        pad_rows = -(-small_rows // 16) * 16
        small = jnp.pad(small, ((0, 0), (0, pad_rows * D - small_n))).reshape(NB, pad_rows, D)
        att = jnp.concatenate(
            [jnp.concatenate([g_wqkv.reshape(NB, R, 3 * cs), g_wout.reshape(NB, R, cs)], 2), small], 1).astype(BF)

        def reduce_batch(buf):
            buf = jnp.take(buf, rel_b, axis=0).reshape((NB // 2, 2) + buf.shape[1:])
            buf = (buf[:, 0].astype(F32) + exchange(buf[:, 1], "batch", NB, 1).astype(F32)).astype(BF)
            n = NB // 2
            while n > 4:
                n //= 2
                buf = (buf[:n].astype(F32) + exchange(buf[n:], "batch", NB, 2 * n).astype(F32)).astype(BF)
            acc = buf[0].astype(F32)
            for m in range(1, n):
                acc = acc + exchange(buf[m], "batch", NB, 2 * m).astype(F32)
            parts = jnp.stack(gather_seq(acc.astype(BF), S))
            return jnp.take(parts, rel_s, axis=0).astype(F32)

        mlp = reduce_batch(mlp)
        att = reduce_batch(att)
        o_win = mlp[:, :R].reshape(S, R, NB, FJ).transpose(1, 2, 0, 3).reshape(R, FF)
        o_wdn = mlp[:, R:].reshape(S * FJ, D)
        o_wqkv = att[:, :R, :3 * cs].reshape(S, R, 3, cs).transpose(1, 2, 0, 3).reshape(R, 3 * D)
        o_wout = att[:, :R, 3 * cs:].transpose(1, 0, 2).reshape(R, D)
        flat = att[:, R:].reshape(S, -1)
        o_bin = flat[:, 8 * R:8 * R + FJ].reshape(S * FJ)
        tot = jnp.sum(flat[:, :8 * R], 0)
        o_ln1g, o_ln1b, o_bqv, o_bout, o_ln2g, o_ln2b, o_bdn = (
            tot[:R], tot[R:2 * R], tot[2 * R:4 * R], tot[4 * R:5 * R], tot[5 * R:6 * R], tot[6 * R:7 * R], tot[7 * R:])
        return (activations.reshape(tokens.shape), d_tokens, o_ln1g, o_ln1b, o_wqkv, o_bqv, o_wout, o_bout,
                o_ln2g, o_ln2b, o_win, o_bin, o_wdn, o_bdn)
    return shards


def solution(mesh):
    S, NB = mesh.shape["seq"], mesh.shape["batch"]
    shards = (make if BLOCK_ROWS // NB % 32 == 0 else make_plain)(S, NB)
    rowwise = P("batch", "seq", None)
    placed = (rowwise, P("batch", None)) + (P(),) * 12 + (rowwise,)
    b, bn = P("batch"), P("batch", None)
    return jax.shard_map(
        shards,
        mesh=mesh,
        in_specs=placed,
        out_specs=(rowwise, rowwise, b, b, bn, b, bn, b, b, b, bn, b, bn, b),
        check_vma=False,
    )
```

```python
import functools

import jax
import jax.numpy as jnp
from jax import lax
from jax.experimental import pallas as pl
from jax.experimental.pallas import tpu as pltpu
from jax.sharding import PartitionSpec as P

HEADS = 12
HEAD_DIM = 64
BLOCK_ROWS = HEADS * HEAD_DIM
BF = jnp.bfloat16
F32 = jnp.float32
MIB = 1 << 20


def dot(a, b, ca=1, cb=0):
    return lax.dot_general(a, b, (((ca,), (cb,)), ((), ())), preferred_element_type=F32)


def exchange(value, axis, size, step):
    return lax.ppermute(value, axis, [(j, j ^ step) for j in range(size)])


def gather_seq(value, size):
    return [value] + [exchange(value, "seq", size, k) for k in range(1, size)]


def norm_parts(values):
    mean = jnp.mean(values, axis=-1, keepdims=True)
    centred = values - mean
    var = jnp.mean(centred * centred, axis=-1, keepdims=True)
    scale = lax.rsqrt(var + 1e-06)
    return centred * scale, scale


def norm_back(grad, unit, scale, gain):
    grad = grad * gain
    mean = jnp.mean(grad, axis=-1, keepdims=True)
    along = jnp.mean(grad * unit, axis=-1, keepdims=True)
    return (grad - mean - unit * along) * scale


def gelu_both(v):
    c = 0.7978845608028654
    square = v * v
    t = jnp.tanh(c * v * (1.0 + 0.044715 * square))
    half = 0.5 * (1.0 + t)
    slope = half + (0.5 * c) * v * (1.0 - t * t) * (1.0 + 3.0 * 0.044715 * square)
    return v * half, slope


def call(kernel, outs, args, name, flops=0, limit=24):
    size = sum(a.size * a.dtype.itemsize for a in args) + sum(o.size * o.dtype.itemsize for o in outs)
    return pl.pallas_call(
        kernel,
        out_shape=outs,
        name=name,
        cost_estimate=pl.CostEstimate(flops=flops, bytes_accessed=size, transcendentals=0),
        compiler_params=pltpu.CompilerParams(vmem_limit_bytes=limit * MIB),
    )(*args)


def sds(shape, dtype):
    return jax.ShapeDtypeStruct(shape, dtype)


HOPS = {"d": "far", "u": "near", "a": "near"}
GATHER = {"d": None, "u": None, "a": None}
DH = (1, 2)
ORDER = "pq cs t2 t1 af fs c1 pm c2 c3 lo fa up dn d0 u0 bw ou d1 u1 a0 h1 d2 h2 a1 u2 d3 d4 a2 u3 u4 a3 a4".split()


def flat(ref):
    return ref[...].reshape(1, -1)


def make(S, NB):
    near_first = [2 ** i for i in range(NB.bit_length() - 1)]
    far_first = near_first[:1] + near_first[:0:-1]
    hops = {k: near_first if v == "near" else far_first for k, v in HOPS.items()}

    def rel_row(row, t):
        s = lax.axis_index("seq")
        parts = [row[:, i * t:(i + 1) * t] for i in range(S)]
        bit = 1
        while bit < S:
            on = (s & bit) != 0
            parts = [jnp.where(on, parts[i ^ bit], parts[i]) for i in range(S)]
            bit *= 2
        return jnp.concatenate(parts, 1)

    def prep_qkv_kernel(wqkv, wq_o):
        D = wqkv.shape[0]
        cs = D // S
        s = lax.axis_index("seq")
        for p in range(S):
            @pl.when(s == p)
            def _(p=p):
                for c in range(3):
                    wq_o[:, c * cs:(c + 1) * cs] = wqkv[:, c * D + p * cs:c * D + (p + 1) * cs]

    def prep_mlp_kernel(win, wout, wdown, bin_, win_o, wout_o, wdn_o, bin_o):
        D = wout.shape[0]
        FF = win.shape[1]
        cs = D // S
        FJ = FF // (NB * S)
        s = lax.axis_index("seq")
        vin = flat(bin_)
        for m in range(S):
            wout_o[m * cs:(m + 1) * cs, :] = wout[pl.ds(pl.multiple_of((s ^ m) * cs, 16), cs), :]
        for i in range(NB):
            wdn_o[i * FJ:(i + 1) * FJ, :] = wdown[pl.ds(pl.multiple_of((i * S + s) * FJ, 16), FJ), :]
        for p in range(S):
            @pl.when(s == p)
            def _(p=p):
                for i in range(NB):
                    at = (i * S + p) * FJ
                    win_o[:, i * FJ:(i + 1) * FJ] = win[:, at:at + FJ]
                    bin_o[:, i * FJ:(i + 1) * FJ] = vin[:, at:at + FJ]

    def turn_kernel(w, o):
        rows, cols = w.shape
        step = min(rows, cols)
        for i in range(0, rows, step):
            for j in range(0, cols, step):
                o[j:j + step, i:i + step] = jnp.transpose(w[i:i + step, j:j + step])

    def attn_fwd_kernel(*refs):
        xs, (seg_ref, g_ref, b_ref, bqv, wq_ref) = refs[:S], refs[S:S + 5]
        qkv_o, lse_o, row_o, col_o, attn_o = refs[S + 5:S + 10]
        near_o, far_o, bias_s = refs[S + 10:2 * S + 9], refs[2 * S + 9:3 * S + 8], refs[3 * S + 8]
        t, D = xs[0].shape
        L = S * t
        cs = D // S
        s = lax.axis_index("seq")
        gain, shift, bias = flat(g_ref), flat(b_ref), flat(bqv)
        for p in range(S):
            @pl.when(s == p)
            def _(p=p):
                zero = jnp.zeros((1, cs), F32)
                bias_s[...] = jnp.concatenate(
                    [bias[:, p * cs:(p + 1) * cs], zero, bias[:, D + p * cs:D + (p + 1) * cs]], 1)
        row = rel_row(seg_ref[...], t).astype(F32)
        row_o[...] = jnp.broadcast_to(row, row_o.shape)
        col_o[...] = jnp.transpose(jnp.broadcast_to(row, (128, L)))
        for k in range(S):
            unit, _ = norm_parts(xs[k][...].astype(F32))
            h1 = (unit * gain + shift).astype(BF)
            qkv_o[k * t:(k + 1) * t, :] = (dot(h1, wq_ref[...]) + bias_s[...]).astype(BF)
        heads = cs // HEAD_DIM
        outs = [[None] * heads for _ in range(S)]
        def part(c, h, rows=slice(None)):
            return qkv_o[rows, c * cs + h * HEAD_DIM:c * cs + (h + 1) * HEAD_DIM]
        def soft(sc, rows, h):
            sc = jnp.where(col_o[rows, :1] == row, sc, -1e30)
            top = jnp.max(sc, axis=-1, keepdims=True)
            ex = jnp.exp(sc - top)
            total = jnp.sum(ex, axis=-1, keepdims=True)
            lse_o[rows, h:h + 1] = top + jnp.log(total)
            return (ex * (1.0 / total)).astype(BF)
        def put(o, h, n):
            o = o.astype(BF)
            for r in range(o.shape[0] // t):
                outs[n + r][h] = o[r * t:(r + 1) * t]
        Q = 256
        todo = [(h, n) for h in range(heads) for n in range(L // Q)]
        def score(h, n):
            return dot(part(0, h, slice(n * Q, (n + 1) * Q)) * BF(HEAD_DIM ** -0.5), part(1, h), 1, 1)
        nxt = score(*todo[0])
        prev = None
        for i, (h, n) in enumerate(todo):
            cur = nxt
            if i + 1 < len(todo):
                nxt = score(*todo[i + 1])
            pr = soft(cur, slice(n * Q, (n + 1) * Q), h)
            if prev is not None:
                put(dot(prev[0], part(2, prev[1])), prev[1], prev[2])
            prev = (pr, h, n * Q // t)
        put(dot(prev[0], part(2, prev[1])), prev[1], prev[2])
        blocks = [jnp.concatenate(o, 1) for o in outs]
        for k in range(S):
            attn_o[k * t:(k + 1) * t, :] = blocks[k]
        for m in range(1, S):
            near_o[m - 1][...] = fold(blocks[m])
            far_o[m - 1][...] = fold(jnp.concatenate([blocks[k ^ m] for k in range(1, S)], 0))

    def fold(block):
        half = block.shape[0] // 2
        return jnp.concatenate([block[:half], block[half:]], 1)

    def unfold(block):
        half = block.shape[1] // 2
        return jnp.concatenate([block[:, :half], block[:, half:]], 0)

    def order(steps):
        ms = [0]
        for step in reversed(steps):
            ms = ms + [m ^ step for m in ms]
        return ms

    def store_blocks(scr, keep_o, send_o, b, steps):
        for p, m in enumerate(order(steps)):
            o, at = (keep_o, p) if p < NB // 2 else (send_o, p - NB // 2)
            o[at] = scr[b ^ m].astype(BF)

    def up_kernel(*refs):
        xs, (own,), nears, fars, cots = refs[:S], refs[S:S + 1], refs[S + 1:2 * S], refs[2 * S:3 * S - 1], refs[3 * S - 1:4 * S - 1]
        (wout, bout, g_ref, b_ref, win, bin_ref, attn_all, h2_o, slope_o, keep_o, send_o,
         act_s, cot_s, gw_s) = refs[4 * S - 1:]
        t, D = xs[0].shape
        cs = D // S
        FJ = win.shape[1] // NB
        b = lax.axis_index("batch")
        attn_all[:t, :] = jnp.concatenate([own[:t, :]] + [unfold(r[...]) for r in nears], 1)
        attn_all[t:, :] = jnp.concatenate([own[t:, :]] + [unfold(r[...]) for r in fars], 1)
        for k in range(S):
            cot_s[k * t:(k + 1) * t, :] = cots[k][...]
        x = jnp.concatenate([x[...].astype(F32) for x in xs], 0)
        x1 = x + dot(attn_all[...], wout[...]) + flat(bout)
        unit, _ = norm_parts(x1)
        h2 = (unit * flat(g_ref) + flat(b_ref)).astype(BF)
        h2_o[...] = h2
        act, slope = gelu_both(dot(h2, win[...]) + bin_ref[...])
        act_s[...] = act.astype(BF)
        slope_o[...] = slope
        gw_s[...] = dot(act_s[...], cot_s[...], 0, 0).reshape(NB, FJ, D)
        store_blocks(gw_s, keep_o, send_o, b, hops["d"])

    def down_kernel(*refs):
        cots, boths = refs[:S], refs[S:2 * S]
        h2, slope, wdn, attn_all, vec, keep_o, send_o, du_s, da_s, gw_s = refs[2 * S:]
        t, D = cots[0].shape
        R = D // NB
        cs = D // S
        NF = slope.shape[1]
        s = lax.axis_index("seq")
        b = lax.axis_index("batch")
        for k in range(S):
            da_s[k * t:(k + 1) * t, :] = boths[k][:, cs:]
        cot = jnp.concatenate([c[...] for c in cots], 0)
        du = (dot(cot, wdn[...], 1, 1) * slope[...]).astype(BF)
        du_s[...] = du
        gbin = jnp.sum(du.astype(F32), axis=0, keepdims=True)
        gw_s[:, :, :NF] = dot(h2[...], du_s[...], 0, 0).reshape(NB, R, NF)
        go = dot(attn_all[...], da_s[...], 0, 0)
        per = NB // S
        for m in range(S):
            for j in range(per):
                gw_s[(s ^ m) * per + j, :, NF:NF + cs] = go[m * cs + j * R:m * cs + (j + 1) * R, :]
        gw_s[:, :, NF + cs:] = columns([vec[:4, :], gbin], gw_s.shape[2] - NF - cs)
        store_blocks(gw_s, keep_o, send_o, b, hops["u"])

    def columns(rows, width):
        rows = jnp.concatenate(rows, 0)
        D = rows.shape[1]
        rows = jnp.concatenate([rows, jnp.zeros((128 - rows.shape[0], D), F32)], 0)
        return jnp.transpose(rows)[:, :width].reshape(NB, D // NB, width)

    def local_kernel(*refs):
        x_ref, own, nears, refs = refs[0], refs[1], refs[2:1 + S], refs[1 + S:]
        cot_ref, wout, bout, g_ref, b_ref, win, bin_ref, win_t, wdown_t = refs[:9]
        act_o, x1_o, dx1_o, vec_o = refs[9:13]
        both = refs[13:]
        t, D = x_ref.shape
        FF = win.shape[1]
        cs = D // S
        s = lax.axis_index("seq")
        heads = [wout[pl.ds(pl.multiple_of((s ^ m) * cs, 16), cs), :] for m in range(S)]
        attn = [own[:t, :]] + [unfold(r[...]) for r in nears]
        x1 = x_ref[...].astype(F32) + flat(bout)
        for m in range(S):
            x1 = x1 + dot(attn[m], heads[m])
        unit, scale = norm_parts(x1)
        h2 = (unit * flat(g_ref) + flat(b_ref)).astype(BF)
        cot = cot_ref[...]
        bias_in = flat(bin_ref)
        x1_o[...] = x1
        dh2 = jnp.zeros((t, D), F32)
        for c in range(FF // D):
            cols = slice(c * D, (c + 1) * D)
            act, slope = gelu_both(dot(h2, win[:, cols]) + bias_in[:, cols])
            act_o[:, cols] = act.astype(BF)
            du = (dot(cot, wdown_t[:, cols]) * slope).astype(BF)
            dh2 = dh2 + dot(du, win_t[cols, :])
        dy = cot.astype(F32)
        dx1 = dy + norm_back(dh2, unit, scale, flat(g_ref))
        dx1_o[...] = dx1
        da = dx1.astype(BF)
        vec_o[...] = jnp.concatenate([
            jnp.sum(da.astype(F32), axis=0, keepdims=True),
            jnp.sum(dh2 * unit, axis=0, keepdims=True),
            jnp.sum(dh2, axis=0, keepdims=True),
            jnp.sum(dy, axis=0, keepdims=True),
            jnp.zeros((4, D), F32)], 0)
        parts = [da[:, i * cs:(i + 1) * cs] for i in range(S)]
        bit = 1
        while bit < S:
            on = (s & bit) != 0
            parts = [jnp.where(on, parts[i ^ bit], parts[i]) for i in range(S)]
            bit *= 2
        for k in range(S):
            both[k][...] = jnp.concatenate([dot(da, heads[k], 1, 1).astype(BF), parts[k]], 1)

    def out_kernel(x1_ref, act, wdown, bdown, out_o):
        out_o[...] = (x1_ref[...] + dot(act[...], wdown[...]) + flat(bdown)).astype(BF)

    def attn_bwd_kernel(*refs):
        xs, boths = refs[:S], refs[S:2 * S]
        row_ref, col_ref, g_ref, b_ref, wq, qkv, lse = refs[2 * S:2 * S + 7]
        own_o, next_o, away_o, keep_o, send_o, h1_s, dqkv_s, gw_s = refs[2 * S + 7:]
        t, D = xs[0].shape
        L = S * t
        cs = D // S
        R = D // NB
        s = lax.axis_index("seq")
        b = lax.axis_index("batch")
        scale = HEAD_DIM ** -0.5
        row = row_ref[0:1, :]
        dattn = jnp.concatenate([r[:, :cs] for r in boths], 0)
        dattn_t = jnp.transpose(dattn)
        q_t = jnp.transpose(qkv[:, :cs] * BF(scale))
        Q = 512
        heads = cs // HEAD_DIM
        todo = [(h, n) for h in range(heads) for n in range(L // Q)]

        def part(c, h, rows=slice(None)):
            return qkv[rows, c * cs + h * HEAD_DIM:c * cs + (h + 1) * HEAD_DIM]

        def products(h, n):
            rows = slice(n * Q, (n + 1) * Q)
            return (dot(part(0, h, rows) * BF(scale), part(1, h), 1, 1),
                    dot(dattn[rows, h * HEAD_DIM:(h + 1) * HEAD_DIM], part(2, h), 1, 1))

        def slopes(sc, dp, h, n):
            rows = slice(n * Q, (n + 1) * Q)
            sc = jnp.where(col_ref[rows, :1] == row, sc, -1e30)
            p = jnp.exp(sc - lse[rows, h:h + 1])
            inner = jnp.sum(p * dp, axis=-1, keepdims=True)
            return p.astype(BF), (p * (dp - inner)).astype(BF)

        dk = [jnp.zeros((HEAD_DIM, L), F32) for _ in range(heads)]
        dv = [jnp.zeros((HEAD_DIM, L), F32) for _ in range(heads)]

        def gradients(p, ds, h, n):
            rows = slice(n * Q, (n + 1) * Q)
            at = h * HEAD_DIM
            dqkv_s[rows, at:at + HEAD_DIM] = dot(ds, part(1, h) * BF(scale)).astype(BF)
            dk[h] = dk[h] + dot(q_t[at:at + HEAD_DIM, rows], ds)
            dv[h] = dv[h] + dot(dattn_t[at:at + HEAD_DIM, rows], p)
            if n == L // Q - 1:
                dqkv_s[:, cs + at:cs + at + HEAD_DIM] = jnp.transpose(dk[h].astype(BF))
                dqkv_s[:, 2 * cs + at:2 * cs + at + HEAD_DIM] = jnp.transpose(dv[h].astype(BF))

        ahead = products(*todo[0])
        behind = None
        for i, at in enumerate(todo):
            now = ahead
            if i + 1 < len(todo):
                ahead = products(*todo[i + 1])
            p, ds = slopes(*now, *at)
            if behind is not None:
                gradients(*behind)
            behind = (p, ds) + at
        gradients(*behind)
        bsum = jnp.sum(dqkv_s[...].astype(F32), axis=0, keepdims=True)
        gg = jnp.zeros((1, D), F32)
        gb = jnp.zeros((1, D), F32)
        for k in range(S):
            rows = slice(k * t, (k + 1) * t)
            unit, _ = norm_parts(xs[k][...].astype(F32))
            h1_s[rows, :] = (unit * flat(g_ref) + flat(b_ref)).astype(BF)
            dh1 = dot(dqkv_s[rows, :], wq[...], 1, 1)
            gg = gg + jnp.sum(dh1 * unit, axis=0, keepdims=True)
            gb = gb + jnp.sum(dh1, axis=0, keepdims=True)
            if k == 0:
                own_o[...] = dh1
            elif k == DH[1]:
                next_o[...] = dh1
            else:
                away_o[int(k != DH[0])] = dh1.astype(BF)
        gw = dot(h1_s[...], dqkv_s[...], 0, 0)
        gw_s[:, :, :3 * cs] = gw.reshape(NB, R, 3 * cs)
        zero = jnp.zeros((1, cs), F32)
        wide_q = jnp.concatenate([jnp.where(s == i, bsum[:, :cs], zero) for i in range(S)], 1)
        wide_v = jnp.concatenate([jnp.where(s == i, bsum[:, 2 * cs:], zero) for i in range(S)], 1)
        wide = jnp.concatenate([wide_q, wide_v], 1)
        first = jnp.concatenate([wide[:, 2 * i * R:(2 * i + 1) * R] for i in range(NB)], 1)
        second = jnp.concatenate([wide[:, (2 * i + 1) * R:(2 * i + 2) * R] for i in range(NB)], 1)
        gw_s[:, :, 3 * cs:] = columns([gg, gb, first, second], gw_s.shape[2] - 3 * cs)
        store_blocks(gw_s, keep_o, send_o, b, hops["a"])

    def down_final_kernel(ks, *refs):
        parts, (wdn_o,) = refs[:-1], refs[-1:]
        FJ = parts[0].shape[0]
        s = lax.axis_index("seq")
        for k, block in order_of(zip(parts, ks)):
            wdn_o[pl.ds(pl.multiple_of((s ^ k) * FJ, 8), FJ), :] = block.astype(F32)

    def order_of(refs):
        out = []
        for ref, ks in refs:
            out += [(k, ref[...] if len(ks) == 1 else ref[i]) for i, k in enumerate(ks)]
        return out

    def up_final_kernel(ks, *refs):
        parts = refs[:len(ks)]
        win_o, wo_o, bo_o, g2_o, b2_o, bd_o, bin_o, scr = refs[len(ks):]
        R, FF = win_o.shape
        D = wo_o.shape[1]
        cs = D // S
        FJ = FF // (NB * S)
        NF = NB * FJ
        s = lax.axis_index("seq")
        for k, block in order_of(zip(parts, ks)):
            scr[s ^ k] = block
        for i in range(NB):
            win_o[:, i * S * FJ:(i + 1) * S * FJ] = jnp.concatenate(
                [scr[p, :, i * FJ:(i + 1) * FJ] for p in range(S)], 1).astype(F32)
        wo_o[...] = jnp.concatenate([scr[p, :, NF:NF + cs] for p in range(S)], 1).astype(F32)
        vecs = [as_rows(scr[p, :, NF + cs:].astype(F32)) for p in range(S)]
        total = sum(vecs[1:], vecs[0])
        for i, o in enumerate((bo_o, g2_o, b2_o, bd_o)):
            o[...] = total[i:i + 1, :].reshape(R)
        bin_o[...] = jnp.concatenate([v[4:5, :] for v in vecs], 1).reshape(S * FJ)

    def as_rows(cols):
        R, width = cols.shape
        cols = jnp.concatenate([cols, jnp.zeros((R, 128 - width), F32)], 1)
        cols = jnp.concatenate([cols, jnp.zeros((128 - R, 128), F32)], 0)
        return jnp.transpose(cols)[:8, :R]

    def att_final_kernel(ks, *refs):
        parts = refs[:len(ks)]
        wq_o, g1_o, b1_o, bqv_o, scr = refs[len(ks):]
        R = wq_o.shape[0]
        D = wq_o.shape[1] // 3
        cs = D // S
        s = lax.axis_index("seq")
        for k, block in order_of(zip(parts, ks)):
            scr[s ^ k] = block
        for c in range(3):
            wq_o[:, c * D:(c + 1) * D] = jnp.concatenate(
                [scr[p, :, c * cs:(c + 1) * cs] for p in range(S)], 1).astype(F32)
        tails = [scr[p, :, 3 * cs:].astype(F32) for p in range(S)]
        total = as_rows(sum(tails[1:], tails[0]))
        g1_o[...] = total[0:1, :].reshape(R)
        b1_o[...] = total[1:2, :].reshape(R)
        bqv_o[...] = jnp.concatenate([total[2:3, :], total[3:4, :]], 1).reshape(2 * R)

    def shards(tokens, segments, ln1_gain, ln1_bias, w_qkv, bias_qv, w_out, bias_out,
               ln2_gain, ln2_bias, w_in, bias_in, w_down, bias_down, cotangent):
        _, t, D = tokens.shape
        FF = w_in.shape[1]
        L = t * S
        cs = D // S
        R = D // NB
        FJ = FF // (NB * S)
        NF = NB * FJ
        x_own = tokens.reshape(t, D)
        cot_own = cotangent.reshape(t, D)

        wide_u, wide_a = -(-(NF + cs + 8) // 128) * 128, -(-(3 * cs + 8) // 128) * 128
        vec_out = sds((R,), F32)
        v = {}
        token = [None]

        def wait(*names):
            vals = tuple(v[n] for n in names)
            if token[0] is not None:
                vals, _ = lax.optimization_barrier((vals, token[0]))
            return vals

        def kernel(body, outs, args, name, scratch=(), limit=24, us=1):
            return pl.pallas_call(
                body, out_shape=outs, scratch_shapes=list(scratch), name=name,
                cost_estimate=pl.CostEstimate(flops=us * 10**9, bytes_accessed=us * 2 * 10**6, transcendentals=0),
                compiler_params=pltpu.CompilerParams(vmem_limit_bytes=limit * MIB))(*args)

        def prep_qkv():
            v["wq"], = kernel(prep_qkv_kernel, [sds((D, 3 * cs), BF)], [w_qkv], "prep_qkv", us=8)
            token[0] = v["wq"]

        def attn_fwd():
            near, far = sds((t // 2, 2 * cs), BF), sds(((L - t) // 2, 2 * cs), BF)
            v["qkv"], v["lse"], v["row"], v["col"], v["attn"], *sends = kernel(
                attn_fwd_kernel,
                [sds((L, 3 * cs), BF), sds((L, 128), F32), sds((8, L), F32), sds((L, 128), F32), sds((L, cs), BF)]
                + [near] * (S - 1) + [far] * (S - 1),
                v["xs"] + (segments, ln1_gain, ln1_bias, bias_qv) + wait("wq"), "attn_fwd",
                [pltpu.VMEM((1, 3 * cs), F32)], us=6)
            v["nears"] = tuple(exchange(sends[m - 1], "seq", S, m) for m in range(1, S))
            v["far_sends"] = tuple(sends[S - 1:])
            token[0] = v["attn"]

        def cots_send():
            (cot,) = wait("cot")
            v["cots"] = tuple(gather_seq(cot, S))

        def fars_send():
            (sends,) = wait("far_sends")
            v["fars"] = tuple(exchange(sends[m - 1], "seq", S, m) for m in range(1, S))

        def cots(*ks):
            def run():
                got = list(v["cots"])
                vals, _ = lax.optimization_barrier((tuple(got[k] for k in ks), token[0]))
                for k, g in zip(ks, vals):
                    got[k] = g
                v["cots"] = tuple(got)
                token[0] = got[ks[-1]]
            return run

        def turn(name, source):
            def run():
                w = v[source]
                if token[0] is not None:
                    w, _ = lax.optimization_barrier((w, token[0]))
                v[name], = kernel(turn_kernel, [sds(w.shape[::-1], BF)], [w], name, us=2)
                token[0] = v[name]
            return run

        def prep_mlp():
            (w,) = wait("w_in")
            v["win_s"], v["wout_s"], v["wdn_s"], v["bin_s"] = kernel(
                prep_mlp_kernel, [sds((D, NF), BF), sds((D, D), BF), sds((NF, D), BF), sds((1, NF), F32)],
                [w, w_out, w_down, bias_in], "prep_mlp")
            token[0] = v["bin_s"]

        def local():
            (nears,) = wait("nears")
            v["act"], v["x1"], v["dx1"], v["vec"], *both = kernel(
                local_kernel,
                [sds((t, FF), BF), sds((t, D), F32), sds((t, D), F32), sds((8, D), F32)]
                + [sds((t, 2 * cs), BF)] * S,
                (x_own, v["attn"]) + nears + (cot_own, w_out, bias_out, ln2_gain, ln2_bias, w_in, bias_in, v["win_t"], v["wdown_t"]),
                "local", limit=20, us=5)
            v["nears"] = nears
            v["boths"] = (both[0],) + tuple(exchange(both[k], "seq", S, k) for k in range(1, S))
            token[0] = v["dx1"]

        def fars():
            (v["fars"],) = wait("fars")
            token[0] = v["fars"][0]

        def up():
            nears, fars, cots = wait("nears", "fars", "cots")
            v["cots"] = cots
            v["attn_all"], v["h2"], v["slope"], v["d_keep"], v["d_send"] = kernel(
                up_kernel,
                [sds((L, D), BF), sds((L, D), BF), sds((L, NF), F32),
                 sds((NB // 2, FJ, D), BF), sds((NB // 2, FJ, D), BF)],
                v["xs"] + (v["attn"],) + nears + fars + cots
                + (v["wout_s"], bias_out, ln2_gain, ln2_bias, v["win_s"], v["bin_s"]), "up",
                [pltpu.VMEM((L, NF), BF), pltpu.VMEM((L, D), BF), pltpu.VMEM((NB, FJ, D), F32)], 32)
            v["d_got"] = exchange(v["d_send"], "batch", NB, 1)
            token[0] = v["d_keep"]

        def both():
            (v["boths"],) = wait("boths")
            token[0] = v["boths"][1]

        def down():
            boths, h2 = wait("boths", "h2")
            v["u_keep"], v["u_send"] = kernel(
                down_kernel, [sds((NB // 2, R, wide_u), BF), sds((NB // 2, R, wide_u), BF)],
                v["cots"] + boths + (h2, v["slope"], v["wdn_s"], v["attn_all"], v["vec"]), "down",
                [pltpu.VMEM((L, NF), BF), pltpu.VMEM((L, cs), BF), pltpu.VMEM((NB, R, wide_u), F32)], 32)
            v["u_got"] = exchange(v["u_send"], "batch", NB, 1)
            token[0] = v["u_keep"]

        def attn_bwd():
            boths, qkv = wait("boths", "qkv")
            v["own"], v["beside"], away, v["a_keep"], v["a_send"] = kernel(
                attn_bwd_kernel,
                [sds((t, D), F32), sds((t, D), F32), sds((S - 2, t, D), BF),
                 sds((NB // 2, R, wide_a), BF), sds((NB // 2, R, wide_a), BF)],
                v["xs"] + boths + (v["row"], v["col"], ln1_gain, ln1_bias, v["wq"], qkv, v["lse"]), "attn_bwd",
                [pltpu.VMEM((L, D), BF), pltpu.VMEM((L, 3 * cs), BF), pltpu.VMEM((NB, R, wide_a), F32)], 32)
            v["a_got"] = exchange(v["a_send"], "batch", NB, 1)
            v["h_got"] = exchange(away, "seq", S, DH[0])
            token[0] = v["a_keep"]

        def halve(name, level):
            def run():
                got, keep = wait(name + "_got", name + "_keep")
                n = keep.shape[0]
                total = lambda lo, hi: (keep[lo:hi].astype(F32) + got[lo:hi].astype(F32)).astype(BF)
                if n > 1:
                    v[name + "_keep"], send = total(0, n // 2), total(n // 2, n)
                    v[name + "_got"] = exchange(send, "batch", NB, hops[name][level + 1])
                    token[0] = send
                    return
                mine = total(0, 1)[0]
                token[0] = mine
                if GATHER[name] is None:
                    v[name + "_all"] = gather_seq(mine, S)
                    v[name + "_ks"] = [[k] for k in range(S)]
                else:
                    first, second = GATHER[name]
                    v[name + "_all"] = [mine, exchange(mine, "seq", S, first)]
                    v[name + "_ks"] = [[0], [first], [second, first ^ second]]
            return run

        def spread(name):
            def run():
                if GATHER[name] is None:
                    return
                (parts,) = wait(name + "_all")
                pair = jnp.stack(parts)
                v[name + "_all"] = list(parts) + [exchange(pair, "seq", S, GATHER[name][1])]
                token[0] = pair
            return run

        def d_final():
            (parts,) = wait("d_all")
            v["o_wdn"], = kernel(
                functools.partial(down_final_kernel, v["d_ks"]), [sds((S * FJ, D), F32)], parts, "down_final")
            token[0] = v["o_wdn"]

        def u_final():
            (parts,) = wait("u_all")
            v["o_u"] = kernel(
                functools.partial(up_final_kernel, v["u_ks"]),
                [sds((R, FF), F32), sds((R, D), F32)] + [vec_out] * 4 + [sds((S * FJ,), F32)],
                parts, "up_final", [pltpu.VMEM((S, R, wide_u), BF)])
            token[0] = v["o_u"][0]

        def a_final():
            (parts,) = wait("a_all")
            v["o_a"] = kernel(
                functools.partial(att_final_kernel, v["a_ks"]),
                [sds((R, 3 * D), F32), vec_out, vec_out, sds((2 * R,), F32)],
                parts, "att_final", [pltpu.VMEM((S, R, wide_a), BF)])
            token[0] = v["o_a"][0]

        def h_first():
            (got,) = wait("h_got")
            beside = (v["beside"] + got[1].astype(F32)).astype(BF)
            v["own"] = v["own"] + got[0].astype(F32)
            v["h_got"] = exchange(beside, "seq", S, DH[1])
            token[0] = beside

        def h_last():
            (got,) = wait("h_got")
            unit1, scale1 = norm_parts(x_own.astype(F32))
            dh1 = v["own"] + got.astype(F32)
            v["d_tokens"] = v["dx1"] + norm_back(dh1, unit1, scale1, ln1_gain)
            token[0] = v["d_tokens"]

        def forward_out():
            x1, act = wait("x1", "act")
            v["out"], = kernel(out_kernel, [sds((t, D), BF)], [x1, act, w_down, bias_down], "out")
            token[0] = v["out"]

        v["xs"] = tuple(gather_seq(x_own, S))
        v["w_in"], v["w_down"], v["cot"] = w_in, w_down, cot_own
        steps = dict(
            pq=prep_qkv, af=attn_fwd, cs=cots_send, fs=fars_send, c1=cots(1), c2=cots(2), c3=cots(3), fa=fars, pm=prep_mlp, t1=turn("wdown_t", "w_down"), t2=turn("win_t", "w_in"), lo=local, up=up, bo=both,
            dn=down, bw=attn_bwd, d0=halve("d", 0), d1=halve("d", 1), d2=halve("d", 2), d3=spread("d"), d4=d_final,
            u0=halve("u", 0), u1=halve("u", 1), u2=halve("u", 2), u3=spread("u"), u4=u_final,
            a0=halve("a", 0), a1=halve("a", 1), a2=halve("a", 2), a3=spread("a"), a4=a_final,
            h1=h_first, h2=h_last, ou=forward_out)
        for name in ORDER:
            steps[name]()
        out, d_tokens, o_wdn = v["out"], v["d_tokens"].reshape(tokens.shape), v["o_wdn"]
        o_win, o_wout, o_bout, o_ln2g, o_ln2b, o_bdn, o_bin = v["o_u"]
        o_wqkv, o_ln1g, o_ln1b, o_bqv = v["o_a"]
        return (out.reshape(tokens.shape), d_tokens, o_ln1g, o_ln1b, o_wqkv, o_bqv, o_wout, o_bout,
                o_ln2g, o_ln2b, o_win, o_bin, o_wdn, o_bdn)
    return shards


def make_plain(S, NB):
    def shards(tokens, segments, ln1_gain, ln1_bias, w_qkv, bias_qv, w_out, bias_out,
               ln2_gain, ln2_bias, w_in, bias_in, w_down, bias_down, cotangent):
        rows, t, D = tokens.shape
        FF = w_in.shape[1]
        L = t * S
        hs = HEADS // S
        cs = hs * HEAD_DIM
        R = D // NB
        FJ = FF // (NB * S)
        scale = HEAD_DIM ** (-0.5)
        s = lax.axis_index("seq")
        b = lax.axis_index("batch")
        rel_s = jnp.arange(S, dtype=jnp.int32) ^ s
        rel_b = jnp.arange(NB, dtype=jnp.int32) ^ b

        x_own = tokens.reshape(t, D)
        cot_own = cotangent.reshape(t, D)
        wq_s = lax.dynamic_slice_in_dim(w_qkv.reshape(D, 3, S, cs), s, 1, 2).reshape(D, 3 * cs)
        bq_s = lax.dynamic_slice_in_dim(bias_qv.reshape(2, S, cs), s, 1, 1).reshape(2, cs)
        bqkv_s = jnp.concatenate([bq_s[0], jnp.zeros((cs,), F32), bq_s[1]])
        win_s = lax.dynamic_slice_in_dim(w_in.reshape(D, NB, S, FJ), s, 1, 2).reshape(D, NB * FJ)
        bin_s = lax.dynamic_slice_in_dim(bias_in.reshape(NB, S, FJ), s, 1, 1).reshape(NB * FJ)
        wdn_s = lax.dynamic_slice_in_dim(w_down.reshape(NB, S, FJ, D), s, 1, 1).reshape(NB * FJ, D)
        wout_rel = jnp.take(w_out.reshape(S, cs, D), rel_s, axis=0).reshape(D, D)
        seg_rel = jnp.take(segments.reshape(S, t), rel_s, axis=0).reshape(L)

        x_all = jnp.concatenate(gather_seq(x_own, S), 0)
        cot_in, x_all = lax.optimization_barrier((cot_own, x_all))
        cot_all = jnp.concatenate(gather_seq(cot_in, S), 0)

        x_f = x_all.astype(F32)
        unit1, scale1 = norm_parts(x_f)
        h1 = (unit1 * ln1_gain + ln1_bias).astype(BF)
        qkv = (dot(h1, wq_s) + bqkv_s).astype(BF)
        q = qkv[:, :cs].reshape(L, hs, HEAD_DIM)
        k = qkv[:, cs:2 * cs].reshape(L, hs, HEAD_DIM)
        v = qkv[:, 2 * cs:].reshape(L, hs, HEAD_DIM)
        mask = seg_rel[:, None] == seg_rel[None, :]
        scores = jnp.einsum("qhd,khd->hqk", q, k, preferred_element_type=F32) * scale
        scores = jnp.where(mask[None], scores, -1e30)
        top = jnp.max(scores, axis=-1, keepdims=True)
        expo = jnp.exp(scores - top)
        total = jnp.sum(expo, axis=-1, keepdims=True)
        probs = expo / total
        probs_low = probs.astype(BF)
        attn = jnp.einsum("hqk,khd->qhd", probs_low, v, preferred_element_type=F32).reshape(L, cs).astype(BF)

        got = gather_seq(attn, S)
        blocks = []
        for m, g in enumerate(got):
            g4 = g.reshape(S, t, cs)
            blocks.append(jnp.concatenate([g4[kk ^ m] for kk in range(S)], 0))
        attn_all = jnp.concatenate(blocks, 1)

        x1 = x_f + dot(attn_all, wout_rel) + bias_out
        unit2, scale2 = norm_parts(x1)
        h2 = (unit2 * ln2_gain + ln2_bias).astype(BF)

        u_s = dot(h2, win_s) + bin_s
        act_s, slope_s = gelu_both(u_s)
        act_s = act_s.astype(BF)
        dact_s = dot(cot_all, wdn_s, 1, 1)
        du_s = (dact_s * slope_s).astype(BF)
        g_win = dot(h2, du_s, 0, 0)
        g_wdn = dot(act_s, cot_all, 0, 0)
        g_bin = jnp.sum(du_s.astype(F32), 0)
        mlp = jnp.concatenate([g_win.reshape(NB, R, NB * FJ), g_wdn.reshape(NB, FJ, D)], 1).astype(BF)

        h2o = h2[:t]
        u = dot(h2o, w_in) + bias_in
        act, slope = gelu_both(u)
        act = act.astype(BF)
        activations = (x1[:t] + dot(act, w_down) + bias_down).astype(BF)
        dy = cot_own.astype(F32)
        du = (dot(cot_own, w_down, 1, 1) * slope).astype(BF)
        dh2 = dot(du, w_in, 1, 1)
        g_ln2g = jnp.sum(dh2 * unit2[:t], 0)
        g_ln2b = jnp.sum(dh2, 0)
        dx1 = dy + norm_back(dh2, unit2[:t], scale2[:t], ln2_gain)
        da = dx1.astype(BF)
        g_bout = jnp.sum(da.astype(F32), 0)
        g_bdn = jnp.sum(dy, 0)
        dattn = dot(da, wout_rel, 1, 1).astype(BF)
        da_rel = jnp.take(da.reshape(t, S, cs), rel_s, axis=1)
        both = [jnp.concatenate([dattn[:, kk * cs:(kk + 1) * cs], da_rel[:, kk]], 1) for kk in range(S)]
        both = jnp.concatenate([both[0]] + [exchange(both[kk], "seq", S, kk) for kk in range(1, S)], 0)
        dattn_all = both[:, :cs].reshape(L, hs, HEAD_DIM)
        da_s = both[:, cs:]

        log_total = top + jnp.log(total)
        p = jnp.exp(scores - log_total)
        p_low = p.astype(BF)
        dp = jnp.einsum("qhd,khd->hqk", dattn_all, v, preferred_element_type=F32)
        inner = jnp.sum(p * dp, axis=-1, keepdims=True)
        ds = (p * (dp - inner)).astype(BF)
        dq = jnp.einsum("hqk,khd->qhd", ds, k, preferred_element_type=F32) * scale
        dk = jnp.einsum("hqk,qhd->khd", ds, q, preferred_element_type=F32) * scale
        dv = jnp.einsum("hqk,qhd->khd", p_low, dattn_all, preferred_element_type=F32)
        dqkv = jnp.concatenate([dq.reshape(L, cs), dk.reshape(L, cs), dv.reshape(L, cs)], 1).astype(BF)

        dh1_part = dot(dqkv, wq_s, 1, 1)
        g_ln1g = jnp.sum(dh1_part * unit1, 0)
        g_ln1b = jnp.sum(dh1_part, 0)
        dh1_low = dh1_part.astype(BF)
        dh1 = dh1_part[:t]
        for kk in range(1, S):
            dh1 = dh1 + exchange(dh1_low[kk * t:(kk + 1) * t], "seq", S, kk).astype(F32)
        d_tokens = (dx1 + norm_back(dh1, unit1[:t], scale1[:t], ln1_gain)).reshape(tokens.shape)

        g_wqkv = dot(h1, dqkv, 0, 0)
        g_wout = dot(attn_all, da_s, 0, 0)
        g_wout = jnp.take(g_wout.reshape(S, cs, cs), rel_s, axis=0).reshape(D, cs)
        bsum = jnp.sum(dqkv.astype(F32), 0)
        g_bqv = jnp.zeros((2, S, cs), F32)
        g_bqv = lax.dynamic_update_slice(g_bqv, jnp.stack([bsum[:cs], bsum[2 * cs:]])[:, None], (0, s, 0))
        small = jnp.concatenate(
            [v_.reshape(NB, -1) for v_ in (g_ln1g, g_ln1b, g_bqv, g_bout, g_ln2g, g_ln2b, g_bdn, g_bin)], 1)
        small_n = small.shape[1]
        small_rows = -(-small_n // D)
        pad_rows = -(-small_rows // 16) * 16
        small = jnp.pad(small, ((0, 0), (0, pad_rows * D - small_n))).reshape(NB, pad_rows, D)
        att = jnp.concatenate(
            [jnp.concatenate([g_wqkv.reshape(NB, R, 3 * cs), g_wout.reshape(NB, R, cs)], 2), small], 1).astype(BF)

        def reduce_batch(buf):
            buf = jnp.take(buf, rel_b, axis=0).reshape((NB // 2, 2) + buf.shape[1:])
            buf = (buf[:, 0].astype(F32) + exchange(buf[:, 1], "batch", NB, 1).astype(F32)).astype(BF)
            n = NB // 2
            while n > 4:
                n //= 2
                buf = (buf[:n].astype(F32) + exchange(buf[n:], "batch", NB, 2 * n).astype(F32)).astype(BF)
            acc = buf[0].astype(F32)
            for m in range(1, n):
                acc = acc + exchange(buf[m], "batch", NB, 2 * m).astype(F32)
            parts = jnp.stack(gather_seq(acc.astype(BF), S))
            return jnp.take(parts, rel_s, axis=0).astype(F32)

        mlp = reduce_batch(mlp)
        att = reduce_batch(att)
        o_win = mlp[:, :R].reshape(S, R, NB, FJ).transpose(1, 2, 0, 3).reshape(R, FF)
        o_wdn = mlp[:, R:].reshape(S * FJ, D)
        o_wqkv = att[:, :R, :3 * cs].reshape(S, R, 3, cs).transpose(1, 2, 0, 3).reshape(R, 3 * D)
        o_wout = att[:, :R, 3 * cs:].transpose(1, 0, 2).reshape(R, D)
        flat = att[:, R:].reshape(S, -1)
        o_bin = flat[:, 8 * R:8 * R + FJ].reshape(S * FJ)
        tot = jnp.sum(flat[:, :8 * R], 0)
        o_ln1g, o_ln1b, o_bqv, o_bout, o_ln2g, o_ln2b, o_bdn = (
            tot[:R], tot[R:2 * R], tot[2 * R:4 * R], tot[4 * R:5 * R], tot[5 * R:6 * R], tot[6 * R:7 * R], tot[7 * R:])
        return (activations.reshape(tokens.shape), d_tokens, o_ln1g, o_ln1b, o_wqkv, o_bqv, o_wout, o_bout,
                o_ln2g, o_ln2b, o_win, o_bin, o_wdn, o_bdn)
    return shards


def solution(mesh):
    S, NB = mesh.shape["seq"], mesh.shape["batch"]
    shards = (make if BLOCK_ROWS // NB % 32 == 0 else make_plain)(S, NB)
    rowwise = P("batch", "seq", None)
    placed = (rowwise, P("batch", None)) + (P(),) * 12 + (rowwise,)
    b, bn = P("batch"), P("batch", None)
    return jax.shard_map(
        shards,
        mesh=mesh,
        in_specs=placed,
        out_specs=(rowwise, rowwise, b, b, bn, b, bn, b, b, b, bn, b, bn, b),
        check_vma=False,
    )
```

```python
import functools

import jax
import jax.numpy as jnp
from jax import lax
from jax.experimental import pallas as pl
from jax.experimental.pallas import tpu as pltpu
from jax.sharding import PartitionSpec as P

HEADS = 12
HEAD_DIM = 64
BLOCK_ROWS = HEADS * HEAD_DIM
BF = jnp.bfloat16
F32 = jnp.float32
MIB = 1 << 20


def dot(a, b, ca=1, cb=0):
    return lax.dot_general(a, b, (((ca,), (cb,)), ((), ())), preferred_element_type=F32)


def exchange(value, axis, size, step):
    return lax.ppermute(value, axis, [(j, j ^ step) for j in range(size)])


def gather_seq(value, size):
    return [value] + [exchange(value, "seq", size, k) for k in range(1, size)]


def norm_parts(values):
    mean = jnp.mean(values, axis=-1, keepdims=True)
    centred = values - mean
    var = jnp.mean(centred * centred, axis=-1, keepdims=True)
    scale = lax.rsqrt(var + 1e-06)
    return centred * scale, scale


def norm_back(grad, unit, scale, gain):
    grad = grad * gain
    mean = jnp.mean(grad, axis=-1, keepdims=True)
    along = jnp.mean(grad * unit, axis=-1, keepdims=True)
    return (grad - mean - unit * along) * scale


def gelu_both(v):
    c = 0.7978845608028654
    square = v * v
    t = jnp.tanh(c * v * (1.0 + 0.044715 * square))
    half = 0.5 * (1.0 + t)
    slope = half + (0.5 * c) * v * (1.0 - t * t) * (1.0 + 3.0 * 0.044715 * square)
    return v * half, slope


def call(kernel, outs, args, name, flops=0, limit=24):
    size = sum(a.size * a.dtype.itemsize for a in args) + sum(o.size * o.dtype.itemsize for o in outs)
    return pl.pallas_call(
        kernel,
        out_shape=outs,
        name=name,
        cost_estimate=pl.CostEstimate(flops=flops, bytes_accessed=size, transcendentals=0),
        compiler_params=pltpu.CompilerParams(vmem_limit_bytes=limit * MIB),
    )(*args)


def sds(shape, dtype):
    return jax.ShapeDtypeStruct(shape, dtype)


HOPS = {"d": "far", "u": "near", "a": "near"}
GATHER = {"d": None, "u": None, "a": None}
DH = (2, 1)
ORDER = "pq cs t2 t1 af fs c1 pm c2 c3 lo fa up dn d0 u0 bw ou d1 u1 h1 a0 h2 d2 a1 u2 d3 d4 a2 h3 u3 u4 a3 a4".split()


def flat(ref):
    return ref[...].reshape(1, -1)


def make(S, NB):
    near_first = [2 ** i for i in range(NB.bit_length() - 1)]
    far_first = near_first[:1] + near_first[:0:-1]
    hops = {k: near_first if v == "near" else far_first for k, v in HOPS.items()}

    def rel_row(row, t):
        s = lax.axis_index("seq")
        parts = [row[:, i * t:(i + 1) * t] for i in range(S)]
        bit = 1
        while bit < S:
            on = (s & bit) != 0
            parts = [jnp.where(on, parts[i ^ bit], parts[i]) for i in range(S)]
            bit *= 2
        return jnp.concatenate(parts, 1)

    def prep_qkv_kernel(wqkv, wq_o):
        D = wqkv.shape[0]
        cs = D // S
        s = lax.axis_index("seq")
        for p in range(S):
            @pl.when(s == p)
            def _(p=p):
                for c in range(3):
                    wq_o[:, c * cs:(c + 1) * cs] = wqkv[:, c * D + p * cs:c * D + (p + 1) * cs]

    def prep_mlp_kernel(win, wout, wdown, bin_, win_o, wout_o, wdn_o, bin_o):
        D = wout.shape[0]
        FF = win.shape[1]
        cs = D // S
        FJ = FF // (NB * S)
        s = lax.axis_index("seq")
        vin = flat(bin_)
        for m in range(S):
            wout_o[m * cs:(m + 1) * cs, :] = wout[pl.ds(pl.multiple_of((s ^ m) * cs, 16), cs), :]
        for i in range(NB):
            wdn_o[i * FJ:(i + 1) * FJ, :] = wdown[pl.ds(pl.multiple_of((i * S + s) * FJ, 16), FJ), :]
        for p in range(S):
            @pl.when(s == p)
            def _(p=p):
                for i in range(NB):
                    at = (i * S + p) * FJ
                    win_o[:, i * FJ:(i + 1) * FJ] = win[:, at:at + FJ]
                    bin_o[:, i * FJ:(i + 1) * FJ] = vin[:, at:at + FJ]

    def turn_kernel(w, o):
        rows, cols = w.shape
        step = min(rows, cols)
        for i in range(0, rows, step):
            for j in range(0, cols, step):
                o[j:j + step, i:i + step] = jnp.transpose(w[i:i + step, j:j + step])

    def attn_fwd_kernel(*refs):
        xs, (seg_ref, g_ref, b_ref, bqv, wq_ref) = refs[:S], refs[S:S + 5]
        qkv_o, lse_o, row_o, col_o, attn_o = refs[S + 5:S + 10]
        near_o, far_o, bias_s = refs[S + 10:2 * S + 9], refs[2 * S + 9:3 * S + 8], refs[3 * S + 8]
        t, D = xs[0].shape
        L = S * t
        cs = D // S
        s = lax.axis_index("seq")
        gain, shift, bias = flat(g_ref), flat(b_ref), flat(bqv)
        for p in range(S):
            @pl.when(s == p)
            def _(p=p):
                zero = jnp.zeros((1, cs), F32)
                bias_s[...] = jnp.concatenate(
                    [bias[:, p * cs:(p + 1) * cs], zero, bias[:, D + p * cs:D + (p + 1) * cs]], 1)
        row = rel_row(seg_ref[...], t).astype(F32)
        row_o[...] = jnp.broadcast_to(row, row_o.shape)
        col_o[...] = jnp.transpose(jnp.broadcast_to(row, (128, L)))
        for k in range(S):
            unit, _ = norm_parts(xs[k][...].astype(F32))
            h1 = (unit * gain + shift).astype(BF)
            qkv_o[k * t:(k + 1) * t, :] = (dot(h1, wq_ref[...]) + bias_s[...]).astype(BF)
        heads = cs // HEAD_DIM
        outs = [[None] * heads for _ in range(S)]
        def part(c, h, rows=slice(None)):
            return qkv_o[rows, c * cs + h * HEAD_DIM:c * cs + (h + 1) * HEAD_DIM]
        def soft(sc, rows, h):
            sc = jnp.where(col_o[rows, :1] == row, sc, -1e30)
            top = jnp.max(sc, axis=-1, keepdims=True)
            ex = jnp.exp(sc - top)
            total = jnp.sum(ex, axis=-1, keepdims=True)
            lse_o[rows, h:h + 1] = top + jnp.log(total)
            return (ex * (1.0 / total)).astype(BF)
        def put(o, h, n):
            o = o.astype(BF)
            for r in range(o.shape[0] // t):
                outs[n + r][h] = o[r * t:(r + 1) * t]
        Q = 256
        todo = [(h, n) for h in range(heads) for n in range(L // Q)]
        def score(h, n):
            return dot(part(0, h, slice(n * Q, (n + 1) * Q)) * BF(HEAD_DIM ** -0.5), part(1, h), 1, 1)
        nxt = score(*todo[0])
        prev = None
        for i, (h, n) in enumerate(todo):
            cur = nxt
            if i + 1 < len(todo):
                nxt = score(*todo[i + 1])
            pr = soft(cur, slice(n * Q, (n + 1) * Q), h)
            if prev is not None:
                put(dot(prev[0], part(2, prev[1])), prev[1], prev[2])
            prev = (pr, h, n * Q // t)
        put(dot(prev[0], part(2, prev[1])), prev[1], prev[2])
        blocks = [jnp.concatenate(o, 1) for o in outs]
        for k in range(S):
            attn_o[k * t:(k + 1) * t, :] = blocks[k]
        for m in range(1, S):
            near_o[m - 1][...] = fold(blocks[m])
            far_o[m - 1][...] = fold(jnp.concatenate([blocks[k ^ m] for k in range(1, S)], 0))

    def fold(block):
        half = block.shape[0] // 2
        return jnp.concatenate([block[:half], block[half:]], 1)

    def unfold(block):
        half = block.shape[1] // 2
        return jnp.concatenate([block[:, :half], block[:, half:]], 0)

    def order(steps):
        ms = [0]
        for step in reversed(steps):
            ms = ms + [m ^ step for m in ms]
        return ms

    def store_blocks(scr, keep_o, send_o, b, steps):
        for p, m in enumerate(order(steps)):
            o, at = (keep_o, p) if p < NB // 2 else (send_o, p - NB // 2)
            o[at] = scr[b ^ m].astype(BF)

    def up_kernel(*refs):
        xs, (own,), nears, fars, cots = refs[:S], refs[S:S + 1], refs[S + 1:2 * S], refs[2 * S:3 * S - 1], refs[3 * S - 1:4 * S - 1]
        (wout, bout, g_ref, b_ref, win, bin_ref, attn_all, h2_o, slope_o, keep_o, send_o,
         act_s, cot_s, gw_s) = refs[4 * S - 1:]
        t, D = xs[0].shape
        cs = D // S
        FJ = win.shape[1] // NB
        b = lax.axis_index("batch")
        attn_all[:t, :] = jnp.concatenate([own[:t, :]] + [unfold(r[...]) for r in nears], 1)
        attn_all[t:, :] = jnp.concatenate([own[t:, :]] + [unfold(r[...]) for r in fars], 1)
        for k in range(S):
            cot_s[k * t:(k + 1) * t, :] = cots[k][...]
        x = jnp.concatenate([x[...].astype(F32) for x in xs], 0)
        x1 = x + dot(attn_all[...], wout[...]) + flat(bout)
        unit, _ = norm_parts(x1)
        h2 = (unit * flat(g_ref) + flat(b_ref)).astype(BF)
        h2_o[...] = h2
        act, slope = gelu_both(dot(h2, win[...]) + bin_ref[...])
        act_s[...] = act.astype(BF)
        slope_o[...] = slope
        gw_s[...] = dot(act_s[...], cot_s[...], 0, 0).reshape(NB, FJ, D)
        store_blocks(gw_s, keep_o, send_o, b, hops["d"])

    def down_kernel(*refs):
        cots, boths = refs[:S], refs[S:2 * S]
        h2, slope, wdn, attn_all, vec, keep_o, send_o, du_s, da_s, gw_s = refs[2 * S:]
        t, D = cots[0].shape
        R = D // NB
        cs = D // S
        NF = slope.shape[1]
        s = lax.axis_index("seq")
        b = lax.axis_index("batch")
        for k in range(S):
            da_s[k * t:(k + 1) * t, :] = boths[k][:, cs:]
        cot = jnp.concatenate([c[...] for c in cots], 0)
        du = (dot(cot, wdn[...], 1, 1) * slope[...]).astype(BF)
        du_s[...] = du
        gbin = jnp.sum(du.astype(F32), axis=0, keepdims=True)
        gw_s[:, :, :NF] = dot(h2[...], du_s[...], 0, 0).reshape(NB, R, NF)
        go = dot(attn_all[...], da_s[...], 0, 0)
        per = NB // S
        for m in range(S):
            for j in range(per):
                gw_s[(s ^ m) * per + j, :, NF:NF + cs] = go[m * cs + j * R:m * cs + (j + 1) * R, :]
        gw_s[:, :, NF + cs:] = columns([vec[:4, :], gbin], gw_s.shape[2] - NF - cs)
        store_blocks(gw_s, keep_o, send_o, b, hops["u"])

    def columns(rows, width):
        rows = jnp.concatenate(rows, 0)
        D = rows.shape[1]
        rows = jnp.concatenate([rows, jnp.zeros((128 - rows.shape[0], D), F32)], 0)
        return jnp.transpose(rows)[:, :width].reshape(NB, D // NB, width)

    def local_kernel(*refs):
        x_ref, own, nears, refs = refs[0], refs[1], refs[2:1 + S], refs[1 + S:]
        cot_ref, wout, bout, g_ref, b_ref, win, bin_ref, win_t, wdown_t = refs[:9]
        act_o, x1_o, dx1_o, vec_o = refs[9:13]
        both = refs[13:]
        t, D = x_ref.shape
        FF = win.shape[1]
        cs = D // S
        s = lax.axis_index("seq")
        heads = [wout[pl.ds(pl.multiple_of((s ^ m) * cs, 16), cs), :] for m in range(S)]
        attn = [own[:t, :]] + [unfold(r[...]) for r in nears]
        x1 = x_ref[...].astype(F32) + flat(bout)
        for m in range(S):
            x1 = x1 + dot(attn[m], heads[m])
        unit, scale = norm_parts(x1)
        h2 = (unit * flat(g_ref) + flat(b_ref)).astype(BF)
        cot = cot_ref[...]
        bias_in = flat(bin_ref)
        x1_o[...] = x1
        dh2 = jnp.zeros((t, D), F32)
        for c in range(FF // D):
            cols = slice(c * D, (c + 1) * D)
            act, slope = gelu_both(dot(h2, win[:, cols]) + bias_in[:, cols])
            act_o[:, cols] = act.astype(BF)
            du = (dot(cot, wdown_t[:, cols]) * slope).astype(BF)
            dh2 = dh2 + dot(du, win_t[cols, :])
        dy = cot.astype(F32)
        dx1 = dy + norm_back(dh2, unit, scale, flat(g_ref))
        dx1_o[...] = dx1
        da = dx1.astype(BF)
        vec_o[...] = jnp.concatenate([
            jnp.sum(da.astype(F32), axis=0, keepdims=True),
            jnp.sum(dh2 * unit, axis=0, keepdims=True),
            jnp.sum(dh2, axis=0, keepdims=True),
            jnp.sum(dy, axis=0, keepdims=True),
            jnp.zeros((4, D), F32)], 0)
        parts = [da[:, i * cs:(i + 1) * cs] for i in range(S)]
        bit = 1
        while bit < S:
            on = (s & bit) != 0
            parts = [jnp.where(on, parts[i ^ bit], parts[i]) for i in range(S)]
            bit *= 2
        for k in range(S):
            both[k][...] = jnp.concatenate([dot(da, heads[k], 1, 1).astype(BF), parts[k]], 1)

    def out_kernel(x1_ref, act, wdown, bdown, out_o):
        out_o[...] = (x1_ref[...] + dot(act[...], wdown[...]) + flat(bdown)).astype(BF)

    def attn_bwd_kernel(*refs):
        xs, boths = refs[:S], refs[S:2 * S]
        row_ref, col_ref, g_ref, b_ref, wq, qkv, lse = refs[2 * S:2 * S + 7]
        own_o, next_o, away_o, keep_o, send_o, h1_s, dqkv_s, gw_s = refs[2 * S + 7:]
        t, D = xs[0].shape
        L = S * t
        cs = D // S
        R = D // NB
        s = lax.axis_index("seq")
        b = lax.axis_index("batch")
        scale = HEAD_DIM ** -0.5
        row = row_ref[0:1, :]
        dattn = jnp.concatenate([r[:, :cs] for r in boths], 0)
        dattn_t = jnp.transpose(dattn)
        q_t = jnp.transpose(qkv[:, :cs] * BF(scale))
        Q = 512
        heads = cs // HEAD_DIM
        todo = [(h, n) for h in range(heads) for n in range(L // Q)]

        def part(c, h, rows=slice(None)):
            return qkv[rows, c * cs + h * HEAD_DIM:c * cs + (h + 1) * HEAD_DIM]

        def products(h, n):
            rows = slice(n * Q, (n + 1) * Q)
            return (dot(part(0, h, rows) * BF(scale), part(1, h), 1, 1),
                    dot(dattn[rows, h * HEAD_DIM:(h + 1) * HEAD_DIM], part(2, h), 1, 1))

        def slopes(sc, dp, h, n):
            rows = slice(n * Q, (n + 1) * Q)
            sc = jnp.where(col_ref[rows, :1] == row, sc, -1e30)
            p = jnp.exp(sc - lse[rows, h:h + 1])
            inner = jnp.sum(p * dp, axis=-1, keepdims=True)
            return p.astype(BF), (p * (dp - inner)).astype(BF)

        dk = [jnp.zeros((HEAD_DIM, L), F32) for _ in range(heads)]
        dv = [jnp.zeros((HEAD_DIM, L), F32) for _ in range(heads)]

        def gradients(p, ds, h, n):
            rows = slice(n * Q, (n + 1) * Q)
            at = h * HEAD_DIM
            dqkv_s[rows, at:at + HEAD_DIM] = dot(ds, part(1, h) * BF(scale)).astype(BF)
            dk[h] = dk[h] + dot(q_t[at:at + HEAD_DIM, rows], ds)
            dv[h] = dv[h] + dot(dattn_t[at:at + HEAD_DIM, rows], p)
            if n == L // Q - 1:
                dqkv_s[:, cs + at:cs + at + HEAD_DIM] = jnp.transpose(dk[h].astype(BF))
                dqkv_s[:, 2 * cs + at:2 * cs + at + HEAD_DIM] = jnp.transpose(dv[h].astype(BF))

        ahead = products(*todo[0])
        behind = None
        for i, at in enumerate(todo):
            now = ahead
            if i + 1 < len(todo):
                ahead = products(*todo[i + 1])
            p, ds = slopes(*now, *at)
            if behind is not None:
                gradients(*behind)
            behind = (p, ds) + at
        gradients(*behind)
        bsum = jnp.sum(dqkv_s[...].astype(F32), axis=0, keepdims=True)
        gg = jnp.zeros((1, D), F32)
        gb = jnp.zeros((1, D), F32)
        for k in range(S):
            rows = slice(k * t, (k + 1) * t)
            unit, _ = norm_parts(xs[k][...].astype(F32))
            h1_s[rows, :] = (unit * flat(g_ref) + flat(b_ref)).astype(BF)
            dh1 = dot(dqkv_s[rows, :], wq[...], 1, 1)
            gg = gg + jnp.sum(dh1 * unit, axis=0, keepdims=True)
            gb = gb + jnp.sum(dh1, axis=0, keepdims=True)
            if k == 0:
                own_o[...] = dh1
            elif k == DH[1]:
                next_o[...] = dh1
            else:
                away_o[int(k != DH[0])] = dh1.astype(BF)
        gw = dot(h1_s[...], dqkv_s[...], 0, 0)
        gw_s[:, :, :3 * cs] = gw.reshape(NB, R, 3 * cs)
        zero = jnp.zeros((1, cs), F32)
        wide_q = jnp.concatenate([jnp.where(s == i, bsum[:, :cs], zero) for i in range(S)], 1)
        wide_v = jnp.concatenate([jnp.where(s == i, bsum[:, 2 * cs:], zero) for i in range(S)], 1)
        wide = jnp.concatenate([wide_q, wide_v], 1)
        first = jnp.concatenate([wide[:, 2 * i * R:(2 * i + 1) * R] for i in range(NB)], 1)
        second = jnp.concatenate([wide[:, (2 * i + 1) * R:(2 * i + 2) * R] for i in range(NB)], 1)
        gw_s[:, :, 3 * cs:] = columns([gg, gb, first, second], gw_s.shape[2] - 3 * cs)
        store_blocks(gw_s, keep_o, send_o, b, hops["a"])

    def down_final_kernel(ks, *refs):
        parts, (wdn_o,) = refs[:-1], refs[-1:]
        FJ = parts[0].shape[0]
        s = lax.axis_index("seq")
        for k, block in order_of(zip(parts, ks)):
            wdn_o[pl.ds(pl.multiple_of((s ^ k) * FJ, 8), FJ), :] = block.astype(F32)

    def order_of(refs):
        out = []
        for ref, ks in refs:
            out += [(k, ref[...] if len(ks) == 1 else ref[i]) for i, k in enumerate(ks)]
        return out

    def up_final_kernel(ks, *refs):
        parts = refs[:len(ks)]
        win_o, wo_o, bo_o, g2_o, b2_o, bd_o, bin_o, scr = refs[len(ks):]
        R, FF = win_o.shape
        D = wo_o.shape[1]
        cs = D // S
        FJ = FF // (NB * S)
        NF = NB * FJ
        s = lax.axis_index("seq")
        for k, block in order_of(zip(parts, ks)):
            scr[s ^ k] = block
        for i in range(NB):
            win_o[:, i * S * FJ:(i + 1) * S * FJ] = jnp.concatenate(
                [scr[p, :, i * FJ:(i + 1) * FJ] for p in range(S)], 1).astype(F32)
        wo_o[...] = jnp.concatenate([scr[p, :, NF:NF + cs] for p in range(S)], 1).astype(F32)
        vecs = [as_rows(scr[p, :, NF + cs:].astype(F32)) for p in range(S)]
        total = sum(vecs[1:], vecs[0])
        for i, o in enumerate((bo_o, g2_o, b2_o, bd_o)):
            o[...] = total[i:i + 1, :].reshape(R)
        bin_o[...] = jnp.concatenate([v[4:5, :] for v in vecs], 1).reshape(S * FJ)

    def as_rows(cols):
        R, width = cols.shape
        cols = jnp.concatenate([cols, jnp.zeros((R, 128 - width), F32)], 1)
        cols = jnp.concatenate([cols, jnp.zeros((128 - R, 128), F32)], 0)
        return jnp.transpose(cols)[:8, :R]

    def att_final_kernel(ks, *refs):
        parts = refs[:len(ks)]
        wq_o, g1_o, b1_o, bqv_o, scr = refs[len(ks):]
        R = wq_o.shape[0]
        D = wq_o.shape[1] // 3
        cs = D // S
        s = lax.axis_index("seq")
        for k, block in order_of(zip(parts, ks)):
            scr[s ^ k] = block
        for c in range(3):
            wq_o[:, c * D:(c + 1) * D] = jnp.concatenate(
                [scr[p, :, c * cs:(c + 1) * cs] for p in range(S)], 1).astype(F32)
        tails = [scr[p, :, 3 * cs:].astype(F32) for p in range(S)]
        total = as_rows(sum(tails[1:], tails[0]))
        g1_o[...] = total[0:1, :].reshape(R)
        b1_o[...] = total[1:2, :].reshape(R)
        bqv_o[...] = jnp.concatenate([total[2:3, :], total[3:4, :]], 1).reshape(2 * R)

    def shards(tokens, segments, ln1_gain, ln1_bias, w_qkv, bias_qv, w_out, bias_out,
               ln2_gain, ln2_bias, w_in, bias_in, w_down, bias_down, cotangent):
        _, t, D = tokens.shape
        FF = w_in.shape[1]
        L = t * S
        cs = D // S
        R = D // NB
        FJ = FF // (NB * S)
        NF = NB * FJ
        x_own = tokens.reshape(t, D)
        cot_own = cotangent.reshape(t, D)

        wide_u, wide_a = -(-(NF + cs + 8) // 128) * 128, -(-(3 * cs + 8) // 128) * 128
        vec_out = sds((R,), F32)
        v = {}
        token = [None]

        def wait(*names):
            vals = tuple(v[n] for n in names)
            if token[0] is not None:
                vals, _ = lax.optimization_barrier((vals, token[0]))
            return vals

        def kernel(body, outs, args, name, scratch=(), limit=24, us=1):
            return pl.pallas_call(
                body, out_shape=outs, scratch_shapes=list(scratch), name=name,
                cost_estimate=pl.CostEstimate(flops=us * 10**9, bytes_accessed=us * 2 * 10**6, transcendentals=0),
                compiler_params=pltpu.CompilerParams(vmem_limit_bytes=limit * MIB))(*args)

        def prep_qkv():
            v["wq"], = kernel(prep_qkv_kernel, [sds((D, 3 * cs), BF)], [w_qkv], "prep_qkv", us=8)
            token[0] = v["wq"]

        def attn_fwd():
            near, far = sds((t // 2, 2 * cs), BF), sds(((L - t) // 2, 2 * cs), BF)
            v["qkv"], v["lse"], v["row"], v["col"], v["attn"], *sends = kernel(
                attn_fwd_kernel,
                [sds((L, 3 * cs), BF), sds((L, 128), F32), sds((8, L), F32), sds((L, 128), F32), sds((L, cs), BF)]
                + [near] * (S - 1) + [far] * (S - 1),
                v["xs"] + (segments, ln1_gain, ln1_bias, bias_qv) + wait("wq"), "attn_fwd",
                [pltpu.VMEM((1, 3 * cs), F32)], us=6)
            v["nears"] = tuple(exchange(sends[m - 1], "seq", S, m) for m in range(1, S))
            v["far_sends"] = tuple(sends[S - 1:])
            token[0] = v["attn"]

        def cots_send():
            (cot,) = wait("cot")
            v["cots"] = tuple(gather_seq(cot, S))

        def fars_send():
            (sends,) = wait("far_sends")
            v["fars"] = tuple(exchange(sends[m - 1], "seq", S, m) for m in range(1, S))

        def cots(*ks):
            def run():
                got = list(v["cots"])
                vals, _ = lax.optimization_barrier((tuple(got[k] for k in ks), token[0]))
                for k, g in zip(ks, vals):
                    got[k] = g
                v["cots"] = tuple(got)
                token[0] = got[ks[-1]]
            return run

        def turn(name, source):
            def run():
                w = v[source]
                if token[0] is not None:
                    w, _ = lax.optimization_barrier((w, token[0]))
                v[name], = kernel(turn_kernel, [sds(w.shape[::-1], BF)], [w], name, us=2)
                token[0] = v[name]
            return run

        def prep_mlp():
            (w,) = wait("w_in")
            v["win_s"], v["wout_s"], v["wdn_s"], v["bin_s"] = kernel(
                prep_mlp_kernel, [sds((D, NF), BF), sds((D, D), BF), sds((NF, D), BF), sds((1, NF), F32)],
                [w, w_out, w_down, bias_in], "prep_mlp")
            token[0] = v["bin_s"]

        def local():
            (nears,) = wait("nears")
            v["act"], v["x1"], v["dx1"], v["vec"], *both = kernel(
                local_kernel,
                [sds((t, FF), BF), sds((t, D), F32), sds((t, D), F32), sds((8, D), F32)]
                + [sds((t, 2 * cs), BF)] * S,
                (x_own, v["attn"]) + nears + (cot_own, w_out, bias_out, ln2_gain, ln2_bias, w_in, bias_in, v["win_t"], v["wdown_t"]),
                "local", limit=20, us=5)
            v["nears"] = nears
            v["boths"] = (both[0],) + tuple(exchange(both[k], "seq", S, k) for k in range(1, S))
            token[0] = v["dx1"]

        def fars():
            (v["fars"],) = wait("fars")
            token[0] = v["fars"][0]

        def up():
            nears, fars, cots = wait("nears", "fars", "cots")
            v["cots"] = cots
            v["attn_all"], v["h2"], v["slope"], v["d_keep"], v["d_send"] = kernel(
                up_kernel,
                [sds((L, D), BF), sds((L, D), BF), sds((L, NF), F32),
                 sds((NB // 2, FJ, D), BF), sds((NB // 2, FJ, D), BF)],
                v["xs"] + (v["attn"],) + nears + fars + cots
                + (v["wout_s"], bias_out, ln2_gain, ln2_bias, v["win_s"], v["bin_s"]), "up",
                [pltpu.VMEM((L, NF), BF), pltpu.VMEM((L, D), BF), pltpu.VMEM((NB, FJ, D), F32)], 32)
            v["d_got"] = exchange(v["d_send"], "batch", NB, 1)
            token[0] = v["d_keep"]

        def both():
            (v["boths"],) = wait("boths")
            token[0] = v["boths"][1]

        def down():
            boths, h2 = wait("boths", "h2")
            v["u_keep"], v["u_send"] = kernel(
                down_kernel, [sds((NB // 2, R, wide_u), BF), sds((NB // 2, R, wide_u), BF)],
                v["cots"] + boths + (h2, v["slope"], v["wdn_s"], v["attn_all"], v["vec"]), "down",
                [pltpu.VMEM((L, NF), BF), pltpu.VMEM((L, cs), BF), pltpu.VMEM((NB, R, wide_u), F32)], 32)
            v["u_got"] = exchange(v["u_send"], "batch", NB, 1)
            token[0] = v["u_keep"]

        def attn_bwd():
            boths, qkv = wait("boths", "qkv")
            v["own"], v["beside"], away, v["a_keep"], v["a_send"] = kernel(
                attn_bwd_kernel,
                [sds((t, D), F32), sds((t, D), F32), sds((S - 2, t, D), BF),
                 sds((NB // 2, R, wide_a), BF), sds((NB // 2, R, wide_a), BF)],
                v["xs"] + boths + (v["row"], v["col"], ln1_gain, ln1_bias, v["wq"], qkv, v["lse"]), "attn_bwd",
                [pltpu.VMEM((L, D), BF), pltpu.VMEM((L, 3 * cs), BF), pltpu.VMEM((NB, R, wide_a), F32)], 32)
            v["a_got"] = exchange(v["a_send"], "batch", NB, 1)
            v["h_got"] = exchange(away, "seq", S, DH[0])
            token[0] = v["a_keep"]

        def halve(name, level):
            def run():
                got, keep = wait(name + "_got", name + "_keep")
                n = keep.shape[0]
                total = lambda lo, hi: (keep[lo:hi].astype(F32) + got[lo:hi].astype(F32)).astype(BF)
                if n > 1:
                    v[name + "_keep"], send = total(0, n // 2), total(n // 2, n)
                    v[name + "_got"] = exchange(send, "batch", NB, hops[name][level + 1])
                    token[0] = send
                    return
                mine = total(0, 1)[0]
                token[0] = mine
                if GATHER[name] is None:
                    v[name + "_all"] = gather_seq(mine, S)
                    v[name + "_ks"] = [[k] for k in range(S)]
                else:
                    first, second = GATHER[name]
                    v[name + "_all"] = [mine, exchange(mine, "seq", S, first)]
                    v[name + "_ks"] = [[0], [first], [second, first ^ second]]
            return run

        def spread(name):
            def run():
                if GATHER[name] is None:
                    return
                (parts,) = wait(name + "_all")
                pair = jnp.stack(parts)
                v[name + "_all"] = list(parts) + [exchange(pair, "seq", S, GATHER[name][1])]
                token[0] = pair
            return run

        def d_final():
            (parts,) = wait("d_all")
            v["o_wdn"], = kernel(
                functools.partial(down_final_kernel, v["d_ks"]), [sds((S * FJ, D), F32)], parts, "down_final")
            token[0] = v["o_wdn"]

        def u_final():
            (parts,) = wait("u_all")
            v["o_u"] = kernel(
                functools.partial(up_final_kernel, v["u_ks"]),
                [sds((R, FF), F32), sds((R, D), F32)] + [vec_out] * 4 + [sds((S * FJ,), F32)],
                parts, "up_final", [pltpu.VMEM((S, R, wide_u), BF)])
            token[0] = v["o_u"][0]

        def a_final():
            (parts,) = wait("a_all")
            v["o_a"] = kernel(
                functools.partial(att_final_kernel, v["a_ks"]),
                [sds((R, 3 * D), F32), vec_out, vec_out, sds((2 * R,), F32)],
                parts, "att_final", [pltpu.VMEM((S, R, wide_a), BF)])
            token[0] = v["o_a"][0]

        def h_first():
            (got,) = wait("h_got")
            beside = (v["beside"] + got[1].astype(F32)).astype(BF)
            v["own"] = v["own"] + got[0].astype(F32)
            v["h_got"] = exchange(beside, "seq", S, DH[1])
            token[0] = beside

        def h_last():
            (v["h_got"],) = wait("h_got")
            token[0] = v["h_got"]

        def token_grad():
            (got,) = wait("h_got")
            unit1, scale1 = norm_parts(x_own.astype(F32))
            dh1 = v["own"] + got.astype(F32)
            v["d_tokens"] = v["dx1"] + norm_back(dh1, unit1, scale1, ln1_gain)
            token[0] = v["d_tokens"]

        def forward_out():
            x1, act = wait("x1", "act")
            v["out"], = kernel(out_kernel, [sds((t, D), BF)], [x1, act, w_down, bias_down], "out")
            token[0] = v["out"]

        v["xs"] = tuple(gather_seq(x_own, S))
        v["w_in"], v["w_down"], v["cot"] = w_in, w_down, cot_own
        steps = dict(
            pq=prep_qkv, af=attn_fwd, cs=cots_send, fs=fars_send, c1=cots(1), c2=cots(2), c3=cots(3), fa=fars, pm=prep_mlp, t1=turn("wdown_t", "w_down"), t2=turn("win_t", "w_in"), lo=local, up=up, bo=both,
            dn=down, bw=attn_bwd, d0=halve("d", 0), d1=halve("d", 1), d2=halve("d", 2), d3=spread("d"), d4=d_final,
            u0=halve("u", 0), u1=halve("u", 1), u2=halve("u", 2), u3=spread("u"), u4=u_final,
            a0=halve("a", 0), a1=halve("a", 1), a2=halve("a", 2), a3=spread("a"), a4=a_final,
            h1=h_first, h2=h_last, h3=token_grad, ou=forward_out)
        for name in ORDER:
            steps[name]()
        out, d_tokens, o_wdn = v["out"], v["d_tokens"].reshape(tokens.shape), v["o_wdn"]
        o_win, o_wout, o_bout, o_ln2g, o_ln2b, o_bdn, o_bin = v["o_u"]
        o_wqkv, o_ln1g, o_ln1b, o_bqv = v["o_a"]
        return (out.reshape(tokens.shape), d_tokens, o_ln1g, o_ln1b, o_wqkv, o_bqv, o_wout, o_bout,
                o_ln2g, o_ln2b, o_win, o_bin, o_wdn, o_bdn)
    return shards


def make_plain(S, NB):
    def shards(tokens, segments, ln1_gain, ln1_bias, w_qkv, bias_qv, w_out, bias_out,
               ln2_gain, ln2_bias, w_in, bias_in, w_down, bias_down, cotangent):
        rows, t, D = tokens.shape
        FF = w_in.shape[1]
        L = t * S
        hs = HEADS // S
        cs = hs * HEAD_DIM
        R = D // NB
        FJ = FF // (NB * S)
        scale = HEAD_DIM ** (-0.5)
        s = lax.axis_index("seq")
        b = lax.axis_index("batch")
        rel_s = jnp.arange(S, dtype=jnp.int32) ^ s
        rel_b = jnp.arange(NB, dtype=jnp.int32) ^ b

        x_own = tokens.reshape(t, D)
        cot_own = cotangent.reshape(t, D)
        wq_s = lax.dynamic_slice_in_dim(w_qkv.reshape(D, 3, S, cs), s, 1, 2).reshape(D, 3 * cs)
        bq_s = lax.dynamic_slice_in_dim(bias_qv.reshape(2, S, cs), s, 1, 1).reshape(2, cs)
        bqkv_s = jnp.concatenate([bq_s[0], jnp.zeros((cs,), F32), bq_s[1]])
        win_s = lax.dynamic_slice_in_dim(w_in.reshape(D, NB, S, FJ), s, 1, 2).reshape(D, NB * FJ)
        bin_s = lax.dynamic_slice_in_dim(bias_in.reshape(NB, S, FJ), s, 1, 1).reshape(NB * FJ)
        wdn_s = lax.dynamic_slice_in_dim(w_down.reshape(NB, S, FJ, D), s, 1, 1).reshape(NB * FJ, D)
        wout_rel = jnp.take(w_out.reshape(S, cs, D), rel_s, axis=0).reshape(D, D)
        seg_rel = jnp.take(segments.reshape(S, t), rel_s, axis=0).reshape(L)

        x_all = jnp.concatenate(gather_seq(x_own, S), 0)
        cot_in, x_all = lax.optimization_barrier((cot_own, x_all))
        cot_all = jnp.concatenate(gather_seq(cot_in, S), 0)

        x_f = x_all.astype(F32)
        unit1, scale1 = norm_parts(x_f)
        h1 = (unit1 * ln1_gain + ln1_bias).astype(BF)
        qkv = (dot(h1, wq_s) + bqkv_s).astype(BF)
        q = qkv[:, :cs].reshape(L, hs, HEAD_DIM)
        k = qkv[:, cs:2 * cs].reshape(L, hs, HEAD_DIM)
        v = qkv[:, 2 * cs:].reshape(L, hs, HEAD_DIM)
        mask = seg_rel[:, None] == seg_rel[None, :]
        scores = jnp.einsum("qhd,khd->hqk", q, k, preferred_element_type=F32) * scale
        scores = jnp.where(mask[None], scores, -1e30)
        top = jnp.max(scores, axis=-1, keepdims=True)
        expo = jnp.exp(scores - top)
        total = jnp.sum(expo, axis=-1, keepdims=True)
        probs = expo / total
        probs_low = probs.astype(BF)
        attn = jnp.einsum("hqk,khd->qhd", probs_low, v, preferred_element_type=F32).reshape(L, cs).astype(BF)

        got = gather_seq(attn, S)
        blocks = []
        for m, g in enumerate(got):
            g4 = g.reshape(S, t, cs)
            blocks.append(jnp.concatenate([g4[kk ^ m] for kk in range(S)], 0))
        attn_all = jnp.concatenate(blocks, 1)

        x1 = x_f + dot(attn_all, wout_rel) + bias_out
        unit2, scale2 = norm_parts(x1)
        h2 = (unit2 * ln2_gain + ln2_bias).astype(BF)

        u_s = dot(h2, win_s) + bin_s
        act_s, slope_s = gelu_both(u_s)
        act_s = act_s.astype(BF)
        dact_s = dot(cot_all, wdn_s, 1, 1)
        du_s = (dact_s * slope_s).astype(BF)
        g_win = dot(h2, du_s, 0, 0)
        g_wdn = dot(act_s, cot_all, 0, 0)
        g_bin = jnp.sum(du_s.astype(F32), 0)
        mlp = jnp.concatenate([g_win.reshape(NB, R, NB * FJ), g_wdn.reshape(NB, FJ, D)], 1).astype(BF)

        h2o = h2[:t]
        u = dot(h2o, w_in) + bias_in
        act, slope = gelu_both(u)
        act = act.astype(BF)
        activations = (x1[:t] + dot(act, w_down) + bias_down).astype(BF)
        dy = cot_own.astype(F32)
        du = (dot(cot_own, w_down, 1, 1) * slope).astype(BF)
        dh2 = dot(du, w_in, 1, 1)
        g_ln2g = jnp.sum(dh2 * unit2[:t], 0)
        g_ln2b = jnp.sum(dh2, 0)
        dx1 = dy + norm_back(dh2, unit2[:t], scale2[:t], ln2_gain)
        da = dx1.astype(BF)
        g_bout = jnp.sum(da.astype(F32), 0)
        g_bdn = jnp.sum(dy, 0)
        dattn = dot(da, wout_rel, 1, 1).astype(BF)
        da_rel = jnp.take(da.reshape(t, S, cs), rel_s, axis=1)
        both = [jnp.concatenate([dattn[:, kk * cs:(kk + 1) * cs], da_rel[:, kk]], 1) for kk in range(S)]
        both = jnp.concatenate([both[0]] + [exchange(both[kk], "seq", S, kk) for kk in range(1, S)], 0)
        dattn_all = both[:, :cs].reshape(L, hs, HEAD_DIM)
        da_s = both[:, cs:]

        log_total = top + jnp.log(total)
        p = jnp.exp(scores - log_total)
        p_low = p.astype(BF)
        dp = jnp.einsum("qhd,khd->hqk", dattn_all, v, preferred_element_type=F32)
        inner = jnp.sum(p * dp, axis=-1, keepdims=True)
        ds = (p * (dp - inner)).astype(BF)
        dq = jnp.einsum("hqk,khd->qhd", ds, k, preferred_element_type=F32) * scale
        dk = jnp.einsum("hqk,qhd->khd", ds, q, preferred_element_type=F32) * scale
        dv = jnp.einsum("hqk,qhd->khd", p_low, dattn_all, preferred_element_type=F32)
        dqkv = jnp.concatenate([dq.reshape(L, cs), dk.reshape(L, cs), dv.reshape(L, cs)], 1).astype(BF)

        dh1_part = dot(dqkv, wq_s, 1, 1)
        g_ln1g = jnp.sum(dh1_part * unit1, 0)
        g_ln1b = jnp.sum(dh1_part, 0)
        dh1_low = dh1_part.astype(BF)
        dh1 = dh1_part[:t]
        for kk in range(1, S):
            dh1 = dh1 + exchange(dh1_low[kk * t:(kk + 1) * t], "seq", S, kk).astype(F32)
        d_tokens = (dx1 + norm_back(dh1, unit1[:t], scale1[:t], ln1_gain)).reshape(tokens.shape)

        g_wqkv = dot(h1, dqkv, 0, 0)
        g_wout = dot(attn_all, da_s, 0, 0)
        g_wout = jnp.take(g_wout.reshape(S, cs, cs), rel_s, axis=0).reshape(D, cs)
        bsum = jnp.sum(dqkv.astype(F32), 0)
        g_bqv = jnp.zeros((2, S, cs), F32)
        g_bqv = lax.dynamic_update_slice(g_bqv, jnp.stack([bsum[:cs], bsum[2 * cs:]])[:, None], (0, s, 0))
        small = jnp.concatenate(
            [v_.reshape(NB, -1) for v_ in (g_ln1g, g_ln1b, g_bqv, g_bout, g_ln2g, g_ln2b, g_bdn, g_bin)], 1)
        small_n = small.shape[1]
        small_rows = -(-small_n // D)
        pad_rows = -(-small_rows // 16) * 16
        small = jnp.pad(small, ((0, 0), (0, pad_rows * D - small_n))).reshape(NB, pad_rows, D)
        att = jnp.concatenate(
            [jnp.concatenate([g_wqkv.reshape(NB, R, 3 * cs), g_wout.reshape(NB, R, cs)], 2), small], 1).astype(BF)

        def reduce_batch(buf):
            buf = jnp.take(buf, rel_b, axis=0).reshape((NB // 2, 2) + buf.shape[1:])
            buf = (buf[:, 0].astype(F32) + exchange(buf[:, 1], "batch", NB, 1).astype(F32)).astype(BF)
            n = NB // 2
            while n > 4:
                n //= 2
                buf = (buf[:n].astype(F32) + exchange(buf[n:], "batch", NB, 2 * n).astype(F32)).astype(BF)
            acc = buf[0].astype(F32)
            for m in range(1, n):
                acc = acc + exchange(buf[m], "batch", NB, 2 * m).astype(F32)
            parts = jnp.stack(gather_seq(acc.astype(BF), S))
            return jnp.take(parts, rel_s, axis=0).astype(F32)

        mlp = reduce_batch(mlp)
        att = reduce_batch(att)
        o_win = mlp[:, :R].reshape(S, R, NB, FJ).transpose(1, 2, 0, 3).reshape(R, FF)
        o_wdn = mlp[:, R:].reshape(S * FJ, D)
        o_wqkv = att[:, :R, :3 * cs].reshape(S, R, 3, cs).transpose(1, 2, 0, 3).reshape(R, 3 * D)
        o_wout = att[:, :R, 3 * cs:].transpose(1, 0, 2).reshape(R, D)
        flat = att[:, R:].reshape(S, -1)
        o_bin = flat[:, 8 * R:8 * R + FJ].reshape(S * FJ)
        tot = jnp.sum(flat[:, :8 * R], 0)
        o_ln1g, o_ln1b, o_bqv, o_bout, o_ln2g, o_ln2b, o_bdn = (
            tot[:R], tot[R:2 * R], tot[2 * R:4 * R], tot[4 * R:5 * R], tot[5 * R:6 * R], tot[6 * R:7 * R], tot[7 * R:])
        return (activations.reshape(tokens.shape), d_tokens, o_ln1g, o_ln1b, o_wqkv, o_bqv, o_wout, o_bout,
                o_ln2g, o_ln2b, o_win, o_bin, o_wdn, o_bdn)
    return shards


def solution(mesh):
    S, NB = mesh.shape["seq"], mesh.shape["batch"]
    shards = (make if BLOCK_ROWS // NB % 32 == 0 else make_plain)(S, NB)
    rowwise = P("batch", "seq", None)
    placed = (rowwise, P("batch", None)) + (P(),) * 12 + (rowwise,)
    b, bn = P("batch"), P("batch", None)
    return jax.shard_map(
        shards,
        mesh=mesh,
        in_specs=placed,
        out_specs=(rowwise, rowwise, b, b, bn, b, bn, b, b, b, bn, b, bn, b),
        check_vma=False,
    )
```

```python
import functools

import jax
import jax.numpy as jnp
from jax import lax
from jax.experimental import pallas as pl
from jax.experimental.pallas import tpu as pltpu
from jax.sharding import PartitionSpec as P

HEADS = 12
HEAD_DIM = 64
BLOCK_ROWS = HEADS * HEAD_DIM
BF = jnp.bfloat16
F32 = jnp.float32
MIB = 1 << 20


def dot(a, b, ca=1, cb=0):
    return lax.dot_general(a, b, (((ca,), (cb,)), ((), ())), preferred_element_type=F32)


def exchange(value, axis, size, step):
    return lax.ppermute(value, axis, [(j, j ^ step) for j in range(size)])


def gather_seq(value, size):
    return [value] + [exchange(value, "seq", size, k) for k in range(1, size)]


def norm_parts(values):
    mean = jnp.mean(values, axis=-1, keepdims=True)
    centred = values - mean
    var = jnp.mean(centred * centred, axis=-1, keepdims=True)
    scale = lax.rsqrt(var + 1e-06)
    return centred * scale, scale


def norm_back(grad, unit, scale, gain):
    grad = grad * gain
    mean = jnp.mean(grad, axis=-1, keepdims=True)
    along = jnp.mean(grad * unit, axis=-1, keepdims=True)
    return (grad - mean - unit * along) * scale


def gelu_both(v):
    c = 0.7978845608028654
    square = v * v
    t = jnp.tanh(c * v * (1.0 + 0.044715 * square))
    half = 0.5 * (1.0 + t)
    slope = half + (0.5 * c) * v * (1.0 - t * t) * (1.0 + 3.0 * 0.044715 * square)
    return v * half, slope


def call(kernel, outs, args, name, flops=0, limit=24):
    size = sum(a.size * a.dtype.itemsize for a in args) + sum(o.size * o.dtype.itemsize for o in outs)
    return pl.pallas_call(
        kernel,
        out_shape=outs,
        name=name,
        cost_estimate=pl.CostEstimate(flops=flops, bytes_accessed=size, transcendentals=0),
        compiler_params=pltpu.CompilerParams(vmem_limit_bytes=limit * MIB),
    )(*args)


def sds(shape, dtype):
    return jax.ShapeDtypeStruct(shape, dtype)


HOPS = {"d": "far", "u": "near", "a": "near"}
GATHER = {"d": None, "u": None, "a": None}
DH = (2, 1)
ORDER = "pq cs t1 t2 af c1 fs pm c2 c3 lo fa up dn d0 u0 bw ou d1 u1 h1 a0 h2 d2 a1 u2 d3 d4 a2 h3 u3 u4 a3 a4".split()


def flat(ref):
    return ref[...].reshape(1, -1)


def make(S, NB):
    near_first = [2 ** i for i in range(NB.bit_length() - 1)]
    far_first = near_first[:1] + near_first[:0:-1]
    hops = {k: near_first if v == "near" else far_first for k, v in HOPS.items()}

    def rel_row(row, t):
        s = lax.axis_index("seq")
        parts = [row[:, i * t:(i + 1) * t] for i in range(S)]
        bit = 1
        while bit < S:
            on = (s & bit) != 0
            parts = [jnp.where(on, parts[i ^ bit], parts[i]) for i in range(S)]
            bit *= 2
        return jnp.concatenate(parts, 1)

    def prep_qkv_kernel(wqkv, wq_o):
        D = wqkv.shape[0]
        cs = D // S
        s = lax.axis_index("seq")
        for p in range(S):
            @pl.when(s == p)
            def _(p=p):
                for c in range(3):
                    wq_o[:, c * cs:(c + 1) * cs] = wqkv[:, c * D + p * cs:c * D + (p + 1) * cs]

    def prep_mlp_kernel(win, wout, wdown, bin_, win_o, wout_o, wdn_o, bin_o):
        D = wout.shape[0]
        FF = win.shape[1]
        cs = D // S
        FJ = FF // (NB * S)
        s = lax.axis_index("seq")
        vin = flat(bin_)
        for m in range(S):
            wout_o[m * cs:(m + 1) * cs, :] = wout[pl.ds(pl.multiple_of((s ^ m) * cs, 16), cs), :]
        for i in range(NB):
            wdn_o[i * FJ:(i + 1) * FJ, :] = wdown[pl.ds(pl.multiple_of((i * S + s) * FJ, 16), FJ), :]
        for p in range(S):
            @pl.when(s == p)
            def _(p=p):
                for i in range(NB):
                    at = (i * S + p) * FJ
                    win_o[:, i * FJ:(i + 1) * FJ] = win[:, at:at + FJ]
                    bin_o[:, i * FJ:(i + 1) * FJ] = vin[:, at:at + FJ]

    def turn_kernel(w, o):
        rows, cols = w.shape
        step = min(rows, cols)
        for i in range(0, rows, step):
            for j in range(0, cols, step):
                o[j:j + step, i:i + step] = jnp.transpose(w[i:i + step, j:j + step])

    def attn_fwd_kernel(*refs):
        xs, (seg_ref, g_ref, b_ref, bqv, wq_ref) = refs[:S], refs[S:S + 5]
        qkv_o, lse_o, row_o, col_o, attn_o = refs[S + 5:S + 10]
        near_o, far_o, bias_s = refs[S + 10:2 * S + 9], refs[2 * S + 9:3 * S + 8], refs[3 * S + 8]
        t, D = xs[0].shape
        L = S * t
        cs = D // S
        s = lax.axis_index("seq")
        gain, shift, bias = flat(g_ref), flat(b_ref), flat(bqv)
        for p in range(S):
            @pl.when(s == p)
            def _(p=p):
                zero = jnp.zeros((1, cs), F32)
                bias_s[...] = jnp.concatenate(
                    [bias[:, p * cs:(p + 1) * cs], zero, bias[:, D + p * cs:D + (p + 1) * cs]], 1)
        row = rel_row(seg_ref[...], t).astype(F32)
        row_o[...] = jnp.broadcast_to(row, row_o.shape)
        col_o[...] = jnp.transpose(jnp.broadcast_to(row, (128, L)))
        for k in range(S):
            unit, _ = norm_parts(xs[k][...].astype(F32))
            h1 = (unit * gain + shift).astype(BF)
            qkv_o[k * t:(k + 1) * t, :] = (dot(h1, wq_ref[...]) + bias_s[...]).astype(BF)
        heads = cs // HEAD_DIM
        outs = [[None] * heads for _ in range(S)]
        def part(c, h, rows=slice(None)):
            return qkv_o[rows, c * cs + h * HEAD_DIM:c * cs + (h + 1) * HEAD_DIM]
        def soft(sc, rows, h):
            sc = jnp.where(col_o[rows, :1] == row, sc, -1e30)
            top = jnp.max(sc, axis=-1, keepdims=True)
            ex = jnp.exp(sc - top)
            total = jnp.sum(ex, axis=-1, keepdims=True)
            lse_o[rows, h:h + 1] = top + jnp.log(total)
            return (ex * (1.0 / total)).astype(BF)
        def put(o, h, n):
            o = o.astype(BF)
            for r in range(o.shape[0] // t):
                outs[n + r][h] = o[r * t:(r + 1) * t]
        Q = 256
        todo = [(h, n) for h in range(heads) for n in range(L // Q)]
        def score(h, n):
            return dot(part(0, h, slice(n * Q, (n + 1) * Q)) * BF(HEAD_DIM ** -0.5), part(1, h), 1, 1)
        nxt = score(*todo[0])
        prev = None
        for i, (h, n) in enumerate(todo):
            cur = nxt
            if i + 1 < len(todo):
                nxt = score(*todo[i + 1])
            pr = soft(cur, slice(n * Q, (n + 1) * Q), h)
            if prev is not None:
                put(dot(prev[0], part(2, prev[1])), prev[1], prev[2])
            prev = (pr, h, n * Q // t)
        put(dot(prev[0], part(2, prev[1])), prev[1], prev[2])
        blocks = [jnp.concatenate(o, 1) for o in outs]
        for k in range(S):
            attn_o[k * t:(k + 1) * t, :] = blocks[k]
        for m in range(1, S):
            near_o[m - 1][...] = fold(blocks[m])
            far_o[m - 1][...] = fold(jnp.concatenate([blocks[k ^ m] for k in range(1, S)], 0))

    def fold(block):
        half = block.shape[0] // 2
        return jnp.concatenate([block[:half], block[half:]], 1)

    def unfold(block):
        half = block.shape[1] // 2
        return jnp.concatenate([block[:, :half], block[:, half:]], 0)

    def order(steps):
        ms = [0]
        for step in reversed(steps):
            ms = ms + [m ^ step for m in ms]
        return ms

    def store_blocks(scr, keep_o, send_o, b, steps):
        for p, m in enumerate(order(steps)):
            o, at = (keep_o, p) if p < NB // 2 else (send_o, p - NB // 2)
            o[at] = scr[b ^ m].astype(BF)

    def up_kernel(*refs):
        xs, (own,), nears, fars, cots = refs[:S], refs[S:S + 1], refs[S + 1:2 * S], refs[2 * S:3 * S - 1], refs[3 * S - 1:4 * S - 1]
        (wout, bout, g_ref, b_ref, win, bin_ref, attn_all, h2_o, slope_o, keep_o, send_o,
         act_s, cot_s, gw_s) = refs[4 * S - 1:]
        t, D = xs[0].shape
        cs = D // S
        FJ = win.shape[1] // NB
        b = lax.axis_index("batch")
        attn_all[:t, :] = jnp.concatenate([own[:t, :]] + [unfold(r[...]) for r in nears], 1)
        attn_all[t:, :] = jnp.concatenate([own[t:, :]] + [unfold(r[...]) for r in fars], 1)
        for k in range(S):
            cot_s[k * t:(k + 1) * t, :] = cots[k][...]
        x = jnp.concatenate([x[...].astype(F32) for x in xs], 0)
        x1 = x + dot(attn_all[...], wout[...]) + flat(bout)
        unit, _ = norm_parts(x1)
        h2 = (unit * flat(g_ref) + flat(b_ref)).astype(BF)
        h2_o[...] = h2
        act, slope = gelu_both(dot(h2, win[...]) + bin_ref[...])
        act_s[...] = act.astype(BF)
        slope_o[...] = slope
        gw_s[...] = dot(act_s[...], cot_s[...], 0, 0).reshape(NB, FJ, D)
        store_blocks(gw_s, keep_o, send_o, b, hops["d"])

    def down_kernel(*refs):
        cots, boths = refs[:S], refs[S:2 * S]
        h2, slope, wdn, attn_all, vec, keep_o, send_o, du_s, da_s, gw_s = refs[2 * S:]
        t, D = cots[0].shape
        R = D // NB
        cs = D // S
        NF = slope.shape[1]
        s = lax.axis_index("seq")
        b = lax.axis_index("batch")
        for k in range(S):
            da_s[k * t:(k + 1) * t, :] = boths[k][:, cs:]
        cot = jnp.concatenate([c[...] for c in cots], 0)
        du = (dot(cot, wdn[...], 1, 1) * slope[...]).astype(BF)
        du_s[...] = du
        gbin = jnp.sum(du.astype(F32), axis=0, keepdims=True)
        gw_s[:, :, :NF] = dot(h2[...], du_s[...], 0, 0).reshape(NB, R, NF)
        go = dot(attn_all[...], da_s[...], 0, 0)
        per = NB // S
        for m in range(S):
            for j in range(per):
                gw_s[(s ^ m) * per + j, :, NF:NF + cs] = go[m * cs + j * R:m * cs + (j + 1) * R, :]
        gw_s[:, :, NF + cs:] = columns([vec[:4, :], gbin], gw_s.shape[2] - NF - cs)
        store_blocks(gw_s, keep_o, send_o, b, hops["u"])

    def columns(rows, width):
        rows = jnp.concatenate(rows, 0)
        D = rows.shape[1]
        rows = jnp.concatenate([rows, jnp.zeros((128 - rows.shape[0], D), F32)], 0)
        return jnp.transpose(rows)[:, :width].reshape(NB, D // NB, width)

    def local_kernel(*refs):
        x_ref, own, nears, refs = refs[0], refs[1], refs[2:1 + S], refs[1 + S:]
        cot_ref, wout, bout, g_ref, b_ref, win, bin_ref, win_t, wdown_t = refs[:9]
        act_o, x1_o, dx1_o, vec_o = refs[9:13]
        both = refs[13:]
        t, D = x_ref.shape
        FF = win.shape[1]
        cs = D // S
        s = lax.axis_index("seq")
        heads = [wout[pl.ds(pl.multiple_of((s ^ m) * cs, 16), cs), :] for m in range(S)]
        attn = [own[:t, :]] + [unfold(r[...]) for r in nears]
        x1 = x_ref[...].astype(F32) + flat(bout)
        for m in range(S):
            x1 = x1 + dot(attn[m], heads[m])
        unit, scale = norm_parts(x1)
        h2 = (unit * flat(g_ref) + flat(b_ref)).astype(BF)
        cot = cot_ref[...]
        bias_in = flat(bin_ref)
        x1_o[...] = x1
        dh2 = jnp.zeros((t, D), F32)
        for c in range(FF // D):
            cols = slice(c * D, (c + 1) * D)
            act, slope = gelu_both(dot(h2, win[:, cols]) + bias_in[:, cols])
            act_o[:, cols] = act.astype(BF)
            du = (dot(cot, wdown_t[:, cols]) * slope).astype(BF)
            dh2 = dh2 + dot(du, win_t[cols, :])
        dy = cot.astype(F32)
        dx1 = dy + norm_back(dh2, unit, scale, flat(g_ref))
        dx1_o[...] = dx1
        da = dx1.astype(BF)
        vec_o[...] = jnp.concatenate([
            jnp.sum(da.astype(F32), axis=0, keepdims=True),
            jnp.sum(dh2 * unit, axis=0, keepdims=True),
            jnp.sum(dh2, axis=0, keepdims=True),
            jnp.sum(dy, axis=0, keepdims=True),
            jnp.zeros((4, D), F32)], 0)
        parts = [da[:, i * cs:(i + 1) * cs] for i in range(S)]
        bit = 1
        while bit < S:
            on = (s & bit) != 0
            parts = [jnp.where(on, parts[i ^ bit], parts[i]) for i in range(S)]
            bit *= 2
        for k in range(S):
            both[k][...] = jnp.concatenate([dot(da, heads[k], 1, 1).astype(BF), parts[k]], 1)

    def out_kernel(x1_ref, act, wdown, bdown, out_o):
        out_o[...] = (x1_ref[...] + dot(act[...], wdown[...]) + flat(bdown)).astype(BF)

    def attn_bwd_kernel(*refs):
        xs, boths = refs[:S], refs[S:2 * S]
        row_ref, col_ref, g_ref, b_ref, wq, qkv, lse = refs[2 * S:2 * S + 7]
        own_o, next_o, away_o, keep_o, send_o, h1_s, dqkv_s, gw_s = refs[2 * S + 7:]
        t, D = xs[0].shape
        L = S * t
        cs = D // S
        R = D // NB
        s = lax.axis_index("seq")
        b = lax.axis_index("batch")
        scale = HEAD_DIM ** -0.5
        row = row_ref[0:1, :]
        dattn = jnp.concatenate([r[:, :cs] for r in boths], 0)
        dattn_t = jnp.transpose(dattn)
        q_t = jnp.transpose(qkv[:, :cs] * BF(scale))
        Q = 512
        heads = cs // HEAD_DIM
        todo = [(h, n) for h in range(heads) for n in range(L // Q)]

        def part(c, h, rows=slice(None)):
            return qkv[rows, c * cs + h * HEAD_DIM:c * cs + (h + 1) * HEAD_DIM]

        def products(h, n):
            rows = slice(n * Q, (n + 1) * Q)
            return (dot(part(0, h, rows) * BF(scale), part(1, h), 1, 1),
                    dot(dattn[rows, h * HEAD_DIM:(h + 1) * HEAD_DIM], part(2, h), 1, 1))

        def slopes(sc, dp, h, n):
            rows = slice(n * Q, (n + 1) * Q)
            sc = jnp.where(col_ref[rows, :1] == row, sc, -1e30)
            p = jnp.exp(sc - lse[rows, h:h + 1])
            inner = jnp.sum(p * dp, axis=-1, keepdims=True)
            return p.astype(BF), (p * (dp - inner)).astype(BF)

        dk = [jnp.zeros((HEAD_DIM, L), F32) for _ in range(heads)]
        dv = [jnp.zeros((HEAD_DIM, L), F32) for _ in range(heads)]

        def gradients(p, ds, h, n):
            rows = slice(n * Q, (n + 1) * Q)
            at = h * HEAD_DIM
            dqkv_s[rows, at:at + HEAD_DIM] = dot(ds, part(1, h) * BF(scale)).astype(BF)
            dk[h] = dk[h] + dot(q_t[at:at + HEAD_DIM, rows], ds)
            dv[h] = dv[h] + dot(dattn_t[at:at + HEAD_DIM, rows], p)
            if n == L // Q - 1:
                dqkv_s[:, cs + at:cs + at + HEAD_DIM] = jnp.transpose(dk[h].astype(BF))
                dqkv_s[:, 2 * cs + at:2 * cs + at + HEAD_DIM] = jnp.transpose(dv[h].astype(BF))

        ahead = products(*todo[0])
        behind = None
        for i, at in enumerate(todo):
            now = ahead
            if i + 1 < len(todo):
                ahead = products(*todo[i + 1])
            p, ds = slopes(*now, *at)
            if behind is not None:
                gradients(*behind)
            behind = (p, ds) + at
        gradients(*behind)
        bsum = jnp.sum(dqkv_s[...].astype(F32), axis=0, keepdims=True)
        gg = jnp.zeros((1, D), F32)
        gb = jnp.zeros((1, D), F32)
        for k in range(S):
            rows = slice(k * t, (k + 1) * t)
            unit, _ = norm_parts(xs[k][...].astype(F32))
            h1_s[rows, :] = (unit * flat(g_ref) + flat(b_ref)).astype(BF)
            dh1 = dot(dqkv_s[rows, :], wq[...], 1, 1)
            gg = gg + jnp.sum(dh1 * unit, axis=0, keepdims=True)
            gb = gb + jnp.sum(dh1, axis=0, keepdims=True)
            if k == 0:
                own_o[...] = dh1
            elif k == DH[1]:
                next_o[...] = dh1
            else:
                away_o[int(k != DH[0])] = dh1.astype(BF)
        gw = dot(h1_s[...], dqkv_s[...], 0, 0)
        gw_s[:, :, :3 * cs] = gw.reshape(NB, R, 3 * cs)
        zero = jnp.zeros((1, cs), F32)
        wide_q = jnp.concatenate([jnp.where(s == i, bsum[:, :cs], zero) for i in range(S)], 1)
        wide_v = jnp.concatenate([jnp.where(s == i, bsum[:, 2 * cs:], zero) for i in range(S)], 1)
        wide = jnp.concatenate([wide_q, wide_v], 1)
        first = jnp.concatenate([wide[:, 2 * i * R:(2 * i + 1) * R] for i in range(NB)], 1)
        second = jnp.concatenate([wide[:, (2 * i + 1) * R:(2 * i + 2) * R] for i in range(NB)], 1)
        gw_s[:, :, 3 * cs:] = columns([gg, gb, first, second], gw_s.shape[2] - 3 * cs)
        store_blocks(gw_s, keep_o, send_o, b, hops["a"])

    def down_final_kernel(ks, *refs):
        parts, (wdn_o,) = refs[:-1], refs[-1:]
        FJ = parts[0].shape[0]
        s = lax.axis_index("seq")
        for k, block in order_of(zip(parts, ks)):
            wdn_o[pl.ds(pl.multiple_of((s ^ k) * FJ, 8), FJ), :] = block.astype(F32)

    def order_of(refs):
        out = []
        for ref, ks in refs:
            out += [(k, ref[...] if len(ks) == 1 else ref[i]) for i, k in enumerate(ks)]
        return out

    def up_final_kernel(ks, *refs):
        parts = refs[:len(ks)]
        win_o, wo_o, bo_o, g2_o, b2_o, bd_o, bin_o, scr = refs[len(ks):]
        R, FF = win_o.shape
        D = wo_o.shape[1]
        cs = D // S
        FJ = FF // (NB * S)
        NF = NB * FJ
        s = lax.axis_index("seq")
        for k, block in order_of(zip(parts, ks)):
            scr[s ^ k] = block
        for i in range(NB):
            win_o[:, i * S * FJ:(i + 1) * S * FJ] = jnp.concatenate(
                [scr[p, :, i * FJ:(i + 1) * FJ] for p in range(S)], 1).astype(F32)
        wo_o[...] = jnp.concatenate([scr[p, :, NF:NF + cs] for p in range(S)], 1).astype(F32)
        vecs = [as_rows(scr[p, :, NF + cs:].astype(F32)) for p in range(S)]
        total = sum(vecs[1:], vecs[0])
        for i, o in enumerate((bo_o, g2_o, b2_o, bd_o)):
            o[...] = total[i:i + 1, :].reshape(R)
        bin_o[...] = jnp.concatenate([v[4:5, :] for v in vecs], 1).reshape(S * FJ)

    def as_rows(cols):
        R, width = cols.shape
        cols = jnp.concatenate([cols, jnp.zeros((R, 128 - width), F32)], 1)
        cols = jnp.concatenate([cols, jnp.zeros((128 - R, 128), F32)], 0)
        return jnp.transpose(cols)[:8, :R]

    def att_final_kernel(ks, *refs):
        parts = refs[:len(ks)]
        wq_o, g1_o, b1_o, bqv_o, scr = refs[len(ks):]
        R = wq_o.shape[0]
        D = wq_o.shape[1] // 3
        cs = D // S
        s = lax.axis_index("seq")
        for k, block in order_of(zip(parts, ks)):
            scr[s ^ k] = block
        for c in range(3):
            wq_o[:, c * D:(c + 1) * D] = jnp.concatenate(
                [scr[p, :, c * cs:(c + 1) * cs] for p in range(S)], 1).astype(F32)
        tails = [scr[p, :, 3 * cs:].astype(F32) for p in range(S)]
        total = as_rows(sum(tails[1:], tails[0]))
        g1_o[...] = total[0:1, :].reshape(R)
        b1_o[...] = total[1:2, :].reshape(R)
        bqv_o[...] = jnp.concatenate([total[2:3, :], total[3:4, :]], 1).reshape(2 * R)

    def shards(tokens, segments, ln1_gain, ln1_bias, w_qkv, bias_qv, w_out, bias_out,
               ln2_gain, ln2_bias, w_in, bias_in, w_down, bias_down, cotangent):
        _, t, D = tokens.shape
        FF = w_in.shape[1]
        L = t * S
        cs = D // S
        R = D // NB
        FJ = FF // (NB * S)
        NF = NB * FJ
        x_own = tokens.reshape(t, D)
        cot_own = cotangent.reshape(t, D)

        wide_u, wide_a = -(-(NF + cs + 8) // 128) * 128, -(-(3 * cs + 8) // 128) * 128
        vec_out = sds((R,), F32)
        v = {}
        token = [None]

        def wait(*names):
            vals = tuple(v[n] for n in names)
            if token[0] is not None:
                vals, _ = lax.optimization_barrier((vals, token[0]))
            return vals

        def kernel(body, outs, args, name, scratch=(), limit=24, us=1):
            return pl.pallas_call(
                body, out_shape=outs, scratch_shapes=list(scratch), name=name,
                cost_estimate=pl.CostEstimate(flops=us * 10**9, bytes_accessed=us * 2 * 10**6, transcendentals=0),
                compiler_params=pltpu.CompilerParams(vmem_limit_bytes=limit * MIB))(*args)

        def prep_qkv():
            v["wq"], = kernel(prep_qkv_kernel, [sds((D, 3 * cs), BF)], [w_qkv], "prep_qkv", us=8)
            token[0] = v["wq"]

        def attn_fwd():
            near, far = sds((t // 2, 2 * cs), BF), sds(((L - t) // 2, 2 * cs), BF)
            v["qkv"], v["lse"], v["row"], v["col"], v["attn"], *sends = kernel(
                attn_fwd_kernel,
                [sds((L, 3 * cs), BF), sds((L, 128), F32), sds((8, L), F32), sds((L, 128), F32), sds((L, cs), BF)]
                + [near] * (S - 1) + [far] * (S - 1),
                v["xs"] + (segments, ln1_gain, ln1_bias, bias_qv) + wait("wq"), "attn_fwd",
                [pltpu.VMEM((1, 3 * cs), F32)], us=6)
            v["nears"] = tuple(exchange(sends[m - 1], "seq", S, m) for m in range(1, S))
            v["far_sends"] = tuple(sends[S - 1:])
            token[0] = v["attn"]

        def cots_send():
            (cot,) = wait("cot")
            v["cots"] = tuple(gather_seq(cot, S))

        def fars_send():
            (sends,) = wait("far_sends")
            v["fars"] = tuple(exchange(sends[m - 1], "seq", S, m) for m in range(1, S))

        def cots(*ks):
            def run():
                got = list(v["cots"])
                vals, _ = lax.optimization_barrier((tuple(got[k] for k in ks), token[0]))
                for k, g in zip(ks, vals):
                    got[k] = g
                v["cots"] = tuple(got)
                token[0] = got[ks[-1]]
            return run

        def turn(name, source):
            def run():
                w = v[source]
                if token[0] is not None:
                    w, _ = lax.optimization_barrier((w, token[0]))
                v[name], = kernel(turn_kernel, [sds(w.shape[::-1], BF)], [w], name, us=2)
                token[0] = v[name]
            return run

        def prep_mlp():
            (w,) = wait("w_in")
            v["win_s"], v["wout_s"], v["wdn_s"], v["bin_s"] = kernel(
                prep_mlp_kernel, [sds((D, NF), BF), sds((D, D), BF), sds((NF, D), BF), sds((1, NF), F32)],
                [w, w_out, w_down, bias_in], "prep_mlp")
            token[0] = v["bin_s"]

        def local():
            (nears,) = wait("nears")
            v["act"], v["x1"], v["dx1"], v["vec"], *both = kernel(
                local_kernel,
                [sds((t, FF), BF), sds((t, D), F32), sds((t, D), F32), sds((8, D), F32)]
                + [sds((t, 2 * cs), BF)] * S,
                (x_own, v["attn"]) + nears + (cot_own, w_out, bias_out, ln2_gain, ln2_bias, w_in, bias_in, v["win_t"], v["wdown_t"]),
                "local", limit=20, us=5)
            v["nears"] = nears
            v["boths"] = (both[0],) + tuple(exchange(both[k], "seq", S, k) for k in range(1, S))
            token[0] = v["dx1"]

        def fars():
            (v["fars"],) = wait("fars")
            token[0] = v["fars"][0]

        def up():
            nears, fars, cots = wait("nears", "fars", "cots")
            v["cots"] = cots
            v["attn_all"], v["h2"], v["slope"], v["d_keep"], v["d_send"] = kernel(
                up_kernel,
                [sds((L, D), BF), sds((L, D), BF), sds((L, NF), F32),
                 sds((NB // 2, FJ, D), BF), sds((NB // 2, FJ, D), BF)],
                v["xs"] + (v["attn"],) + nears + fars + cots
                + (v["wout_s"], bias_out, ln2_gain, ln2_bias, v["win_s"], v["bin_s"]), "up",
                [pltpu.VMEM((L, NF), BF), pltpu.VMEM((L, D), BF), pltpu.VMEM((NB, FJ, D), F32)], 32)
            v["d_got"] = exchange(v["d_send"], "batch", NB, 1)
            token[0] = v["d_keep"]

        def both():
            (v["boths"],) = wait("boths")
            token[0] = v["boths"][1]

        def down():
            boths, h2 = wait("boths", "h2")
            v["u_keep"], v["u_send"] = kernel(
                down_kernel, [sds((NB // 2, R, wide_u), BF), sds((NB // 2, R, wide_u), BF)],
                v["cots"] + boths + (h2, v["slope"], v["wdn_s"], v["attn_all"], v["vec"]), "down",
                [pltpu.VMEM((L, NF), BF), pltpu.VMEM((L, cs), BF), pltpu.VMEM((NB, R, wide_u), F32)], 32)
            v["u_got"] = exchange(v["u_send"], "batch", NB, 1)
            token[0] = v["u_keep"]

        def attn_bwd():
            boths, qkv = wait("boths", "qkv")
            v["own"], v["beside"], away, v["a_keep"], v["a_send"] = kernel(
                attn_bwd_kernel,
                [sds((t, D), F32), sds((t, D), F32), sds((S - 2, t, D), BF),
                 sds((NB // 2, R, wide_a), BF), sds((NB // 2, R, wide_a), BF)],
                v["xs"] + boths + (v["row"], v["col"], ln1_gain, ln1_bias, v["wq"], qkv, v["lse"]), "attn_bwd",
                [pltpu.VMEM((L, D), BF), pltpu.VMEM((L, 3 * cs), BF), pltpu.VMEM((NB, R, wide_a), F32)], 32)
            v["a_got"] = exchange(v["a_send"], "batch", NB, 1)
            v["h_got"] = exchange(away, "seq", S, DH[0])
            token[0] = v["a_keep"]

        def halve(name, level):
            def run():
                got, keep = wait(name + "_got", name + "_keep")
                n = keep.shape[0]
                total = lambda lo, hi: (keep[lo:hi].astype(F32) + got[lo:hi].astype(F32)).astype(BF)
                if n > 1:
                    v[name + "_keep"], send = total(0, n // 2), total(n // 2, n)
                    v[name + "_got"] = exchange(send, "batch", NB, hops[name][level + 1])
                    token[0] = send
                    return
                mine = total(0, 1)[0]
                token[0] = mine
                if GATHER[name] is None:
                    v[name + "_all"] = gather_seq(mine, S)
                    v[name + "_ks"] = [[k] for k in range(S)]
                else:
                    first, second = GATHER[name]
                    v[name + "_all"] = [mine, exchange(mine, "seq", S, first)]
                    v[name + "_ks"] = [[0], [first], [second, first ^ second]]
            return run

        def spread(name):
            def run():
                if GATHER[name] is None:
                    return
                (parts,) = wait(name + "_all")
                pair = jnp.stack(parts)
                v[name + "_all"] = list(parts) + [exchange(pair, "seq", S, GATHER[name][1])]
                token[0] = pair
            return run

        def d_final():
            (parts,) = wait("d_all")
            v["o_wdn"], = kernel(
                functools.partial(down_final_kernel, v["d_ks"]), [sds((S * FJ, D), F32)], parts, "down_final")
            token[0] = v["o_wdn"]

        def u_final():
            (parts,) = wait("u_all")
            v["o_u"] = kernel(
                functools.partial(up_final_kernel, v["u_ks"]),
                [sds((R, FF), F32), sds((R, D), F32)] + [vec_out] * 4 + [sds((S * FJ,), F32)],
                parts, "up_final", [pltpu.VMEM((S, R, wide_u), BF)])
            token[0] = v["o_u"][0]

        def a_final():
            (parts,) = wait("a_all")
            v["o_a"] = kernel(
                functools.partial(att_final_kernel, v["a_ks"]),
                [sds((R, 3 * D), F32), vec_out, vec_out, sds((2 * R,), F32)],
                parts, "att_final", [pltpu.VMEM((S, R, wide_a), BF)])
            token[0] = v["o_a"][0]

        def h_first():
            (got,) = wait("h_got")
            beside = (v["beside"] + got[1].astype(F32)).astype(BF)
            v["own"] = v["own"] + got[0].astype(F32)
            v["h_got"] = exchange(beside, "seq", S, DH[1])
            token[0] = beside

        def h_last():
            (v["h_got"],) = wait("h_got")
            token[0] = v["h_got"]

        def token_grad():
            (got,) = wait("h_got")
            unit1, scale1 = norm_parts(x_own.astype(F32))
            dh1 = v["own"] + got.astype(F32)
            v["d_tokens"] = v["dx1"] + norm_back(dh1, unit1, scale1, ln1_gain)
            token[0] = v["d_tokens"]

        def forward_out():
            x1, act = wait("x1", "act")
            v["out"], = kernel(out_kernel, [sds((t, D), BF)], [x1, act, w_down, bias_down], "out")
            token[0] = v["out"]

        v["xs"] = tuple(gather_seq(x_own, S))
        v["w_in"], v["w_down"], v["cot"] = w_in, w_down, cot_own
        steps = dict(
            pq=prep_qkv, af=attn_fwd, cs=cots_send, fs=fars_send, c1=cots(1), c2=cots(2), c3=cots(3), fa=fars, pm=prep_mlp, t1=turn("wdown_t", "w_down"), t2=turn("win_t", "w_in"), lo=local, up=up, bo=both,
            dn=down, bw=attn_bwd, d0=halve("d", 0), d1=halve("d", 1), d2=halve("d", 2), d3=spread("d"), d4=d_final,
            u0=halve("u", 0), u1=halve("u", 1), u2=halve("u", 2), u3=spread("u"), u4=u_final,
            a0=halve("a", 0), a1=halve("a", 1), a2=halve("a", 2), a3=spread("a"), a4=a_final,
            h1=h_first, h2=h_last, h3=token_grad, ou=forward_out)
        for name in ORDER:
            steps[name]()
        out, d_tokens, o_wdn = v["out"], v["d_tokens"].reshape(tokens.shape), v["o_wdn"]
        o_win, o_wout, o_bout, o_ln2g, o_ln2b, o_bdn, o_bin = v["o_u"]
        o_wqkv, o_ln1g, o_ln1b, o_bqv = v["o_a"]
        return (out.reshape(tokens.shape), d_tokens, o_ln1g, o_ln1b, o_wqkv, o_bqv, o_wout, o_bout,
                o_ln2g, o_ln2b, o_win, o_bin, o_wdn, o_bdn)
    return shards


def make_plain(S, NB):
    def shards(tokens, segments, ln1_gain, ln1_bias, w_qkv, bias_qv, w_out, bias_out,
               ln2_gain, ln2_bias, w_in, bias_in, w_down, bias_down, cotangent):
        rows, t, D = tokens.shape
        FF = w_in.shape[1]
        L = t * S
        hs = HEADS // S
        cs = hs * HEAD_DIM
        R = D // NB
        FJ = FF // (NB * S)
        scale = HEAD_DIM ** (-0.5)
        s = lax.axis_index("seq")
        b = lax.axis_index("batch")
        rel_s = jnp.arange(S, dtype=jnp.int32) ^ s
        rel_b = jnp.arange(NB, dtype=jnp.int32) ^ b

        x_own = tokens.reshape(t, D)
        cot_own = cotangent.reshape(t, D)
        wq_s = lax.dynamic_slice_in_dim(w_qkv.reshape(D, 3, S, cs), s, 1, 2).reshape(D, 3 * cs)
        bq_s = lax.dynamic_slice_in_dim(bias_qv.reshape(2, S, cs), s, 1, 1).reshape(2, cs)
        bqkv_s = jnp.concatenate([bq_s[0], jnp.zeros((cs,), F32), bq_s[1]])
        win_s = lax.dynamic_slice_in_dim(w_in.reshape(D, NB, S, FJ), s, 1, 2).reshape(D, NB * FJ)
        bin_s = lax.dynamic_slice_in_dim(bias_in.reshape(NB, S, FJ), s, 1, 1).reshape(NB * FJ)
        wdn_s = lax.dynamic_slice_in_dim(w_down.reshape(NB, S, FJ, D), s, 1, 1).reshape(NB * FJ, D)
        wout_rel = jnp.take(w_out.reshape(S, cs, D), rel_s, axis=0).reshape(D, D)
        seg_rel = jnp.take(segments.reshape(S, t), rel_s, axis=0).reshape(L)

        x_all = jnp.concatenate(gather_seq(x_own, S), 0)
        cot_in, x_all = lax.optimization_barrier((cot_own, x_all))
        cot_all = jnp.concatenate(gather_seq(cot_in, S), 0)

        x_f = x_all.astype(F32)
        unit1, scale1 = norm_parts(x_f)
        h1 = (unit1 * ln1_gain + ln1_bias).astype(BF)
        qkv = (dot(h1, wq_s) + bqkv_s).astype(BF)
        q = qkv[:, :cs].reshape(L, hs, HEAD_DIM)
        k = qkv[:, cs:2 * cs].reshape(L, hs, HEAD_DIM)
        v = qkv[:, 2 * cs:].reshape(L, hs, HEAD_DIM)
        mask = seg_rel[:, None] == seg_rel[None, :]
        scores = jnp.einsum("qhd,khd->hqk", q, k, preferred_element_type=F32) * scale
        scores = jnp.where(mask[None], scores, -1e30)
        top = jnp.max(scores, axis=-1, keepdims=True)
        expo = jnp.exp(scores - top)
        total = jnp.sum(expo, axis=-1, keepdims=True)
        probs = expo / total
        probs_low = probs.astype(BF)
        attn = jnp.einsum("hqk,khd->qhd", probs_low, v, preferred_element_type=F32).reshape(L, cs).astype(BF)

        got = gather_seq(attn, S)
        blocks = []
        for m, g in enumerate(got):
            g4 = g.reshape(S, t, cs)
            blocks.append(jnp.concatenate([g4[kk ^ m] for kk in range(S)], 0))
        attn_all = jnp.concatenate(blocks, 1)

        x1 = x_f + dot(attn_all, wout_rel) + bias_out
        unit2, scale2 = norm_parts(x1)
        h2 = (unit2 * ln2_gain + ln2_bias).astype(BF)

        u_s = dot(h2, win_s) + bin_s
        act_s, slope_s = gelu_both(u_s)
        act_s = act_s.astype(BF)
        dact_s = dot(cot_all, wdn_s, 1, 1)
        du_s = (dact_s * slope_s).astype(BF)
        g_win = dot(h2, du_s, 0, 0)
        g_wdn = dot(act_s, cot_all, 0, 0)
        g_bin = jnp.sum(du_s.astype(F32), 0)
        mlp = jnp.concatenate([g_win.reshape(NB, R, NB * FJ), g_wdn.reshape(NB, FJ, D)], 1).astype(BF)

        h2o = h2[:t]
        u = dot(h2o, w_in) + bias_in
        act, slope = gelu_both(u)
        act = act.astype(BF)
        activations = (x1[:t] + dot(act, w_down) + bias_down).astype(BF)
        dy = cot_own.astype(F32)
        du = (dot(cot_own, w_down, 1, 1) * slope).astype(BF)
        dh2 = dot(du, w_in, 1, 1)
        g_ln2g = jnp.sum(dh2 * unit2[:t], 0)
        g_ln2b = jnp.sum(dh2, 0)
        dx1 = dy + norm_back(dh2, unit2[:t], scale2[:t], ln2_gain)
        da = dx1.astype(BF)
        g_bout = jnp.sum(da.astype(F32), 0)
        g_bdn = jnp.sum(dy, 0)
        dattn = dot(da, wout_rel, 1, 1).astype(BF)
        da_rel = jnp.take(da.reshape(t, S, cs), rel_s, axis=1)
        both = [jnp.concatenate([dattn[:, kk * cs:(kk + 1) * cs], da_rel[:, kk]], 1) for kk in range(S)]
        both = jnp.concatenate([both[0]] + [exchange(both[kk], "seq", S, kk) for kk in range(1, S)], 0)
        dattn_all = both[:, :cs].reshape(L, hs, HEAD_DIM)
        da_s = both[:, cs:]

        log_total = top + jnp.log(total)
        p = jnp.exp(scores - log_total)
        p_low = p.astype(BF)
        dp = jnp.einsum("qhd,khd->hqk", dattn_all, v, preferred_element_type=F32)
        inner = jnp.sum(p * dp, axis=-1, keepdims=True)
        ds = (p * (dp - inner)).astype(BF)
        dq = jnp.einsum("hqk,khd->qhd", ds, k, preferred_element_type=F32) * scale
        dk = jnp.einsum("hqk,qhd->khd", ds, q, preferred_element_type=F32) * scale
        dv = jnp.einsum("hqk,qhd->khd", p_low, dattn_all, preferred_element_type=F32)
        dqkv = jnp.concatenate([dq.reshape(L, cs), dk.reshape(L, cs), dv.reshape(L, cs)], 1).astype(BF)

        dh1_part = dot(dqkv, wq_s, 1, 1)
        g_ln1g = jnp.sum(dh1_part * unit1, 0)
        g_ln1b = jnp.sum(dh1_part, 0)
        dh1_low = dh1_part.astype(BF)
        dh1 = dh1_part[:t]
        for kk in range(1, S):
            dh1 = dh1 + exchange(dh1_low[kk * t:(kk + 1) * t], "seq", S, kk).astype(F32)
        d_tokens = (dx1 + norm_back(dh1, unit1[:t], scale1[:t], ln1_gain)).reshape(tokens.shape)

        g_wqkv = dot(h1, dqkv, 0, 0)
        g_wout = dot(attn_all, da_s, 0, 0)
        g_wout = jnp.take(g_wout.reshape(S, cs, cs), rel_s, axis=0).reshape(D, cs)
        bsum = jnp.sum(dqkv.astype(F32), 0)
        g_bqv = jnp.zeros((2, S, cs), F32)
        g_bqv = lax.dynamic_update_slice(g_bqv, jnp.stack([bsum[:cs], bsum[2 * cs:]])[:, None], (0, s, 0))
        small = jnp.concatenate(
            [v_.reshape(NB, -1) for v_ in (g_ln1g, g_ln1b, g_bqv, g_bout, g_ln2g, g_ln2b, g_bdn, g_bin)], 1)
        small_n = small.shape[1]
        small_rows = -(-small_n // D)
        pad_rows = -(-small_rows // 16) * 16
        small = jnp.pad(small, ((0, 0), (0, pad_rows * D - small_n))).reshape(NB, pad_rows, D)
        att = jnp.concatenate(
            [jnp.concatenate([g_wqkv.reshape(NB, R, 3 * cs), g_wout.reshape(NB, R, cs)], 2), small], 1).astype(BF)

        def reduce_batch(buf):
            buf = jnp.take(buf, rel_b, axis=0).reshape((NB // 2, 2) + buf.shape[1:])
            buf = (buf[:, 0].astype(F32) + exchange(buf[:, 1], "batch", NB, 1).astype(F32)).astype(BF)
            n = NB // 2
            while n > 4:
                n //= 2
                buf = (buf[:n].astype(F32) + exchange(buf[n:], "batch", NB, 2 * n).astype(F32)).astype(BF)
            acc = buf[0].astype(F32)
            for m in range(1, n):
                acc = acc + exchange(buf[m], "batch", NB, 2 * m).astype(F32)
            parts = jnp.stack(gather_seq(acc.astype(BF), S))
            return jnp.take(parts, rel_s, axis=0).astype(F32)

        mlp = reduce_batch(mlp)
        att = reduce_batch(att)
        o_win = mlp[:, :R].reshape(S, R, NB, FJ).transpose(1, 2, 0, 3).reshape(R, FF)
        o_wdn = mlp[:, R:].reshape(S * FJ, D)
        o_wqkv = att[:, :R, :3 * cs].reshape(S, R, 3, cs).transpose(1, 2, 0, 3).reshape(R, 3 * D)
        o_wout = att[:, :R, 3 * cs:].transpose(1, 0, 2).reshape(R, D)
        flat = att[:, R:].reshape(S, -1)
        o_bin = flat[:, 8 * R:8 * R + FJ].reshape(S * FJ)
        tot = jnp.sum(flat[:, :8 * R], 0)
        o_ln1g, o_ln1b, o_bqv, o_bout, o_ln2g, o_ln2b, o_bdn = (
            tot[:R], tot[R:2 * R], tot[2 * R:4 * R], tot[4 * R:5 * R], tot[5 * R:6 * R], tot[6 * R:7 * R], tot[7 * R:])
        return (activations.reshape(tokens.shape), d_tokens, o_ln1g, o_ln1b, o_wqkv, o_bqv, o_wout, o_bout,
                o_ln2g, o_ln2b, o_win, o_bin, o_wdn, o_bdn)
    return shards


def solution(mesh):
    S, NB = mesh.shape["seq"], mesh.shape["batch"]
    shards = (make if BLOCK_ROWS // NB % 32 == 0 else make_plain)(S, NB)
    rowwise = P("batch", "seq", None)
    placed = (rowwise, P("batch", None)) + (P(),) * 12 + (rowwise,)
    b, bn = P("batch"), P("batch", None)
    return jax.shard_map(
        shards,
        mesh=mesh,
        in_specs=placed,
        out_specs=(rowwise, rowwise, b, b, bn, b, bn, b, b, b, bn, b, bn, b),
        check_vma=False,
    )
```

```python
import functools

import jax
import jax.numpy as jnp
from jax import lax
from jax.experimental import pallas as pl
from jax.experimental.pallas import tpu as pltpu
from jax.sharding import PartitionSpec as P

HEADS = 12
HEAD_DIM = 64
BLOCK_ROWS = HEADS * HEAD_DIM
BF = jnp.bfloat16
F32 = jnp.float32
MIB = 1 << 20


def dot(a, b, ca=1, cb=0):
    return lax.dot_general(a, b, (((ca,), (cb,)), ((), ())), preferred_element_type=F32)


def exchange(value, axis, size, step):
    return lax.ppermute(value, axis, [(j, j ^ step) for j in range(size)])


def gather_seq(value, size):
    return [value] + [exchange(value, "seq", size, k) for k in range(1, size)]


def norm_parts(values):
    mean = jnp.mean(values, axis=-1, keepdims=True)
    centred = values - mean
    var = jnp.mean(centred * centred, axis=-1, keepdims=True)
    scale = lax.rsqrt(var + 1e-06)
    return centred * scale, scale


def norm_back(grad, unit, scale, gain):
    grad = grad * gain
    mean = jnp.mean(grad, axis=-1, keepdims=True)
    along = jnp.mean(grad * unit, axis=-1, keepdims=True)
    return (grad - mean - unit * along) * scale


def gelu_both(v):
    c = 0.7978845608028654
    square = v * v
    t = jnp.tanh(c * v * (1.0 + 0.044715 * square))
    half = 0.5 * (1.0 + t)
    slope = half + (0.5 * c) * v * (1.0 - t * t) * (1.0 + 3.0 * 0.044715 * square)
    return v * half, slope


def call(kernel, outs, args, name, flops=0, limit=24):
    size = sum(a.size * a.dtype.itemsize for a in args) + sum(o.size * o.dtype.itemsize for o in outs)
    return pl.pallas_call(
        kernel,
        out_shape=outs,
        name=name,
        cost_estimate=pl.CostEstimate(flops=flops, bytes_accessed=size, transcendentals=0),
        compiler_params=pltpu.CompilerParams(vmem_limit_bytes=limit * MIB),
    )(*args)


def sds(shape, dtype):
    return jax.ShapeDtypeStruct(shape, dtype)


HOPS = {"d": "far", "u": "near", "a": "near"}
GATHER = {"d": None, "u": None, "a": None}
DH = (2, 1)
ORDER = (
    "pq", "cs", "t1", "t2", "af", "c1", "fs", "pm", "c2", "c3", "lo", "fa",
    "up", "dn", "d0", "u0", "bw", "ou", "d1", "u1", "h1", "a0", "h2", "d2",
    "a1", "u2", "d3", "d4", "a2", "h3", "u3", "u4", "a3", "a4",
)


def flat(ref):
    return ref[...].reshape(1, -1)


def make(S, NB):
    near_first = [2 ** i for i in range(NB.bit_length() - 1)]
    far_first = near_first[:1] + near_first[:0:-1]
    hops = {k: near_first if v == "near" else far_first for k, v in HOPS.items()}

    def rel_row(row, t):
        s = lax.axis_index("seq")
        parts = [row[:, i * t:(i + 1) * t] for i in range(S)]
        bit = 1
        while bit < S:
            on = (s & bit) != 0
            parts = [jnp.where(on, parts[i ^ bit], parts[i]) for i in range(S)]
            bit *= 2
        return jnp.concatenate(parts, 1)

    def prep_qkv_kernel(wqkv, wq_o):
        D = wqkv.shape[0]
        cs = D // S
        s = lax.axis_index("seq")
        for p in range(S):
            @pl.when(s == p)
            def _(p=p):
                for c in range(3):
                    wq_o[:, c * cs:(c + 1) * cs] = wqkv[:, c * D + p * cs:c * D + (p + 1) * cs]

    def prep_mlp_kernel(win, wout, wdown, bin_, win_o, wout_o, wdn_o, bin_o):
        D = wout.shape[0]
        FF = win.shape[1]
        cs = D // S
        FJ = FF // (NB * S)
        s = lax.axis_index("seq")
        vin = flat(bin_)
        for m in range(S):
            wout_o[m * cs:(m + 1) * cs, :] = wout[pl.ds(pl.multiple_of((s ^ m) * cs, 16), cs), :]
        for i in range(NB):
            wdn_o[i * FJ:(i + 1) * FJ, :] = wdown[pl.ds(pl.multiple_of((i * S + s) * FJ, 16), FJ), :]
        for p in range(S):
            @pl.when(s == p)
            def _(p=p):
                for i in range(NB):
                    at = (i * S + p) * FJ
                    win_o[:, i * FJ:(i + 1) * FJ] = win[:, at:at + FJ]
                    bin_o[:, i * FJ:(i + 1) * FJ] = vin[:, at:at + FJ]

    def turn_kernel(w, o):
        rows, cols = w.shape
        step = min(rows, cols)
        for i in range(0, rows, step):
            for j in range(0, cols, step):
                o[j:j + step, i:i + step] = jnp.transpose(w[i:i + step, j:j + step])

    def attn_fwd_kernel(*refs):
        xs, (seg_ref, g_ref, b_ref, bqv, wq_ref) = refs[:S], refs[S:S + 5]
        qkv_o, lse_o, row_o, col_o, attn_o = refs[S + 5:S + 10]
        near_o, far_o, bias_s = refs[S + 10:2 * S + 9], refs[2 * S + 9:3 * S + 8], refs[3 * S + 8]
        t, D = xs[0].shape
        L = S * t
        cs = D // S
        s = lax.axis_index("seq")
        gain, shift, bias = flat(g_ref), flat(b_ref), flat(bqv)
        for p in range(S):
            @pl.when(s == p)
            def _(p=p):
                zero = jnp.zeros((1, cs), F32)
                bias_s[...] = jnp.concatenate(
                    [bias[:, p * cs:(p + 1) * cs], zero, bias[:, D + p * cs:D + (p + 1) * cs]], 1)
        row = rel_row(seg_ref[...], t).astype(F32)
        row_o[...] = jnp.broadcast_to(row, row_o.shape)
        col_o[...] = jnp.transpose(jnp.broadcast_to(row, (128, L)))
        for k in range(S):
            unit, _ = norm_parts(xs[k][...].astype(F32))
            h1 = (unit * gain + shift).astype(BF)
            qkv_o[k * t:(k + 1) * t, :] = (dot(h1, wq_ref[...]) + bias_s[...]).astype(BF)
        heads = cs // HEAD_DIM
        outs = [[None] * heads for _ in range(S)]
        def part(c, h, rows=slice(None)):
            return qkv_o[rows, c * cs + h * HEAD_DIM:c * cs + (h + 1) * HEAD_DIM]
        def soft(sc, rows, h):
            sc = jnp.where(col_o[rows, :1] == row, sc, -1e30)
            top = jnp.max(sc, axis=-1, keepdims=True)
            ex = jnp.exp(sc - top)
            total = jnp.sum(ex, axis=-1, keepdims=True)
            lse_o[rows, h:h + 1] = top + jnp.log(total)
            return (ex * (1.0 / total)).astype(BF)
        def put(o, h, n):
            o = o.astype(BF)
            for r in range(o.shape[0] // t):
                outs[n + r][h] = o[r * t:(r + 1) * t]
        Q = 256
        todo = [(h, n) for h in range(heads) for n in range(L // Q)]
        def score(h, n):
            return dot(part(0, h, slice(n * Q, (n + 1) * Q)) * BF(HEAD_DIM ** -0.5), part(1, h), 1, 1)
        nxt = score(*todo[0])
        prev = None
        for i, (h, n) in enumerate(todo):
            cur = nxt
            if i + 1 < len(todo):
                nxt = score(*todo[i + 1])
            pr = soft(cur, slice(n * Q, (n + 1) * Q), h)
            if prev is not None:
                put(dot(prev[0], part(2, prev[1])), prev[1], prev[2])
            prev = (pr, h, n * Q // t)
        put(dot(prev[0], part(2, prev[1])), prev[1], prev[2])
        blocks = [jnp.concatenate(o, 1) for o in outs]
        for k in range(S):
            attn_o[k * t:(k + 1) * t, :] = blocks[k]
        for m in range(1, S):
            near_o[m - 1][...] = fold(blocks[m])
            far_o[m - 1][...] = fold(jnp.concatenate([blocks[k ^ m] for k in range(1, S)], 0))

    def fold(block):
        half = block.shape[0] // 2
        return jnp.concatenate([block[:half], block[half:]], 1)

    def unfold(block):
        half = block.shape[1] // 2
        return jnp.concatenate([block[:, :half], block[:, half:]], 0)

    def order(steps):
        ms = [0]
        for step in reversed(steps):
            ms = ms + [m ^ step for m in ms]
        return ms

    def store_blocks(scr, keep_o, send_o, b, steps):
        for p, m in enumerate(order(steps)):
            o, at = (keep_o, p) if p < NB // 2 else (send_o, p - NB // 2)
            o[at] = scr[b ^ m].astype(BF)

    def up_kernel(*refs):
        xs, (own,), nears, fars, cots = refs[:S], refs[S:S + 1], refs[S + 1:2 * S], refs[2 * S:3 * S - 1], refs[3 * S - 1:4 * S - 1]
        (wout, bout, g_ref, b_ref, win, bin_ref, attn_all, h2_o, slope_o, keep_o, send_o,
         act_s, cot_s, gw_s) = refs[4 * S - 1:]
        t, D = xs[0].shape
        cs = D // S
        FJ = win.shape[1] // NB
        b = lax.axis_index("batch")
        attn_all[:t, :] = jnp.concatenate([own[:t, :]] + [unfold(r[...]) for r in nears], 1)
        attn_all[t:, :] = jnp.concatenate([own[t:, :]] + [unfold(r[...]) for r in fars], 1)
        for k in range(S):
            cot_s[k * t:(k + 1) * t, :] = cots[k][...]
        x = jnp.concatenate([x[...].astype(F32) for x in xs], 0)
        x1 = x + dot(attn_all[...], wout[...]) + flat(bout)
        unit, _ = norm_parts(x1)
        h2 = (unit * flat(g_ref) + flat(b_ref)).astype(BF)
        h2_o[...] = h2
        act, slope = gelu_both(dot(h2, win[...]) + bin_ref[...])
        act_s[...] = act.astype(BF)
        slope_o[...] = slope
        gw_s[...] = dot(act_s[...], cot_s[...], 0, 0).reshape(NB, FJ, D)
        store_blocks(gw_s, keep_o, send_o, b, hops["d"])

    def down_kernel(*refs):
        cots, boths = refs[:S], refs[S:2 * S]
        h2, slope, wdn, attn_all, vec, keep_o, send_o, du_s, da_s, gw_s = refs[2 * S:]
        t, D = cots[0].shape
        R = D // NB
        cs = D // S
        NF = slope.shape[1]
        s = lax.axis_index("seq")
        b = lax.axis_index("batch")
        for k in range(S):
            da_s[k * t:(k + 1) * t, :] = boths[k][:, cs:]
        cot = jnp.concatenate([c[...] for c in cots], 0)
        du = (dot(cot, wdn[...], 1, 1) * slope[...]).astype(BF)
        du_s[...] = du
        gbin = jnp.sum(du.astype(F32), axis=0, keepdims=True)
        gw_s[:, :, :NF] = dot(h2[...], du_s[...], 0, 0).reshape(NB, R, NF)
        go = dot(attn_all[...], da_s[...], 0, 0)
        per = NB // S
        for m in range(S):
            for j in range(per):
                gw_s[(s ^ m) * per + j, :, NF:NF + cs] = go[m * cs + j * R:m * cs + (j + 1) * R, :]
        gw_s[:, :, NF + cs:] = columns([vec[:4, :], gbin], gw_s.shape[2] - NF - cs)
        store_blocks(gw_s, keep_o, send_o, b, hops["u"])

    def columns(rows, width):
        rows = jnp.concatenate(rows, 0)
        D = rows.shape[1]
        rows = jnp.concatenate([rows, jnp.zeros((128 - rows.shape[0], D), F32)], 0)
        return jnp.transpose(rows)[:, :width].reshape(NB, D // NB, width)

    def local_kernel(*refs):
        x_ref, own, nears, refs = refs[0], refs[1], refs[2:1 + S], refs[1 + S:]
        cot_ref, wout, bout, g_ref, b_ref, win, bin_ref, win_t, wdown_t = refs[:9]
        act_o, x1_o, dx1_o, vec_o = refs[9:13]
        both = refs[13:]
        t, D = x_ref.shape
        FF = win.shape[1]
        cs = D // S
        s = lax.axis_index("seq")
        heads = [wout[pl.ds(pl.multiple_of((s ^ m) * cs, 16), cs), :] for m in range(S)]
        attn = [own[:t, :]] + [unfold(r[...]) for r in nears]
        x1 = x_ref[...].astype(F32) + flat(bout)
        for m in range(S):
            x1 = x1 + dot(attn[m], heads[m])
        unit, scale = norm_parts(x1)
        h2 = (unit * flat(g_ref) + flat(b_ref)).astype(BF)
        cot = cot_ref[...]
        bias_in = flat(bin_ref)
        x1_o[...] = x1
        dh2 = jnp.zeros((t, D), F32)
        for c in range(FF // D):
            cols = slice(c * D, (c + 1) * D)
            act, slope = gelu_both(dot(h2, win[:, cols]) + bias_in[:, cols])
            act_o[:, cols] = act.astype(BF)
            du = (dot(cot, wdown_t[:, cols]) * slope).astype(BF)
            dh2 = dh2 + dot(du, win_t[cols, :])
        dy = cot.astype(F32)
        dx1 = dy + norm_back(dh2, unit, scale, flat(g_ref))
        dx1_o[...] = dx1
        da = dx1.astype(BF)
        vec_o[...] = jnp.concatenate([
            jnp.sum(da.astype(F32), axis=0, keepdims=True),
            jnp.sum(dh2 * unit, axis=0, keepdims=True),
            jnp.sum(dh2, axis=0, keepdims=True),
            jnp.sum(dy, axis=0, keepdims=True),
            jnp.zeros((4, D), F32)], 0)
        parts = [da[:, i * cs:(i + 1) * cs] for i in range(S)]
        bit = 1
        while bit < S:
            on = (s & bit) != 0
            parts = [jnp.where(on, parts[i ^ bit], parts[i]) for i in range(S)]
            bit *= 2
        for k in range(S):
            both[k][...] = jnp.concatenate([dot(da, heads[k], 1, 1).astype(BF), parts[k]], 1)

    def out_kernel(x1_ref, act, wdown, bdown, out_o):
        out_o[...] = (x1_ref[...] + dot(act[...], wdown[...]) + flat(bdown)).astype(BF)

    def attn_bwd_kernel(*refs):
        xs, boths = refs[:S], refs[S:2 * S]
        row_ref, col_ref, g_ref, b_ref, wq, qkv, lse = refs[2 * S:2 * S + 7]
        own_o, next_o, away_o, keep_o, send_o, h1_s, dqkv_s, gw_s = refs[2 * S + 7:]
        t, D = xs[0].shape
        L = S * t
        cs = D // S
        R = D // NB
        s = lax.axis_index("seq")
        b = lax.axis_index("batch")
        scale = HEAD_DIM ** -0.5
        row = row_ref[0:1, :]
        dattn = jnp.concatenate([r[:, :cs] for r in boths], 0)
        dattn_t = jnp.transpose(dattn)
        q_t = jnp.transpose(qkv[:, :cs] * BF(scale))
        Q = 512
        heads = cs // HEAD_DIM
        todo = [(h, n) for h in range(heads) for n in range(L // Q)]

        def part(c, h, rows=slice(None)):
            return qkv[rows, c * cs + h * HEAD_DIM:c * cs + (h + 1) * HEAD_DIM]

        def products(h, n):
            rows = slice(n * Q, (n + 1) * Q)
            return (dot(part(0, h, rows) * BF(scale), part(1, h), 1, 1),
                    dot(dattn[rows, h * HEAD_DIM:(h + 1) * HEAD_DIM], part(2, h), 1, 1))

        def slopes(sc, dp, h, n):
            rows = slice(n * Q, (n + 1) * Q)
            sc = jnp.where(col_ref[rows, :1] == row, sc, -1e30)
            p = jnp.exp(sc - lse[rows, h:h + 1])
            inner = jnp.sum(p * dp, axis=-1, keepdims=True)
            return p.astype(BF), (p * (dp - inner)).astype(BF)

        dk = [jnp.zeros((HEAD_DIM, L), F32) for _ in range(heads)]
        dv = [jnp.zeros((HEAD_DIM, L), F32) for _ in range(heads)]

        def gradients(p, ds, h, n):
            rows = slice(n * Q, (n + 1) * Q)
            at = h * HEAD_DIM
            dqkv_s[rows, at:at + HEAD_DIM] = dot(ds, part(1, h) * BF(scale)).astype(BF)
            dk[h] = dk[h] + dot(q_t[at:at + HEAD_DIM, rows], ds)
            dv[h] = dv[h] + dot(dattn_t[at:at + HEAD_DIM, rows], p)
            if n == L // Q - 1:
                dqkv_s[:, cs + at:cs + at + HEAD_DIM] = jnp.transpose(dk[h].astype(BF))
                dqkv_s[:, 2 * cs + at:2 * cs + at + HEAD_DIM] = jnp.transpose(dv[h].astype(BF))

        ahead = products(*todo[0])
        behind = None
        for i, at in enumerate(todo):
            now = ahead
            if i + 1 < len(todo):
                ahead = products(*todo[i + 1])
            p, ds = slopes(*now, *at)
            if behind is not None:
                gradients(*behind)
            behind = (p, ds) + at
        gradients(*behind)
        bsum = jnp.sum(dqkv_s[...].astype(F32), axis=0, keepdims=True)
        gg = jnp.zeros((1, D), F32)
        gb = jnp.zeros((1, D), F32)
        for k in range(S):
            rows = slice(k * t, (k + 1) * t)
            unit, _ = norm_parts(xs[k][...].astype(F32))
            h1_s[rows, :] = (unit * flat(g_ref) + flat(b_ref)).astype(BF)
            dh1 = dot(dqkv_s[rows, :], wq[...], 1, 1)
            gg = gg + jnp.sum(dh1 * unit, axis=0, keepdims=True)
            gb = gb + jnp.sum(dh1, axis=0, keepdims=True)
            if k == 0:
                own_o[...] = dh1
            elif k == DH[1]:
                next_o[...] = dh1
            else:
                away_o[int(k != DH[0])] = dh1.astype(BF)
        gw = dot(h1_s[...], dqkv_s[...], 0, 0)
        gw_s[:, :, :3 * cs] = gw.reshape(NB, R, 3 * cs)
        zero = jnp.zeros((1, cs), F32)
        wide_q = jnp.concatenate([jnp.where(s == i, bsum[:, :cs], zero) for i in range(S)], 1)
        wide_v = jnp.concatenate([jnp.where(s == i, bsum[:, 2 * cs:], zero) for i in range(S)], 1)
        wide = jnp.concatenate([wide_q, wide_v], 1)
        first = jnp.concatenate([wide[:, 2 * i * R:(2 * i + 1) * R] for i in range(NB)], 1)
        second = jnp.concatenate([wide[:, (2 * i + 1) * R:(2 * i + 2) * R] for i in range(NB)], 1)
        gw_s[:, :, 3 * cs:] = columns([gg, gb, first, second], gw_s.shape[2] - 3 * cs)
        store_blocks(gw_s, keep_o, send_o, b, hops["a"])

    def down_final_kernel(ks, *refs):
        parts, (wdn_o,) = refs[:-1], refs[-1:]
        FJ = parts[0].shape[0]
        s = lax.axis_index("seq")
        for k, block in order_of(zip(parts, ks)):
            wdn_o[pl.ds(pl.multiple_of((s ^ k) * FJ, 8), FJ), :] = block.astype(F32)

    def order_of(refs):
        out = []
        for ref, ks in refs:
            out += [(k, ref[...] if len(ks) == 1 else ref[i]) for i, k in enumerate(ks)]
        return out

    def up_final_kernel(ks, *refs):
        parts = refs[:len(ks)]
        win_o, wo_o, bo_o, g2_o, b2_o, bd_o, bin_o, scr = refs[len(ks):]
        R, FF = win_o.shape
        D = wo_o.shape[1]
        cs = D // S
        FJ = FF // (NB * S)
        NF = NB * FJ
        s = lax.axis_index("seq")
        for k, block in order_of(zip(parts, ks)):
            scr[s ^ k] = block
        for i in range(NB):
            win_o[:, i * S * FJ:(i + 1) * S * FJ] = jnp.concatenate(
                [scr[p, :, i * FJ:(i + 1) * FJ] for p in range(S)], 1).astype(F32)
        wo_o[...] = jnp.concatenate([scr[p, :, NF:NF + cs] for p in range(S)], 1).astype(F32)
        vecs = [as_rows(scr[p, :, NF + cs:].astype(F32)) for p in range(S)]
        total = sum(vecs[1:], vecs[0])
        for i, o in enumerate((bo_o, g2_o, b2_o, bd_o)):
            o[...] = total[i:i + 1, :].reshape(R)
        bin_o[...] = jnp.concatenate([v[4:5, :] for v in vecs], 1).reshape(S * FJ)

    def as_rows(cols):
        R, width = cols.shape
        cols = jnp.concatenate([cols, jnp.zeros((R, 128 - width), F32)], 1)
        cols = jnp.concatenate([cols, jnp.zeros((128 - R, 128), F32)], 0)
        return jnp.transpose(cols)[:8, :R]

    def att_final_kernel(ks, *refs):
        parts = refs[:len(ks)]
        wq_o, g1_o, b1_o, bqv_o, scr = refs[len(ks):]
        R = wq_o.shape[0]
        D = wq_o.shape[1] // 3
        cs = D // S
        s = lax.axis_index("seq")
        for k, block in order_of(zip(parts, ks)):
            scr[s ^ k] = block
        for c in range(3):
            wq_o[:, c * D:(c + 1) * D] = jnp.concatenate(
                [scr[p, :, c * cs:(c + 1) * cs] for p in range(S)], 1).astype(F32)
        tails = [scr[p, :, 3 * cs:].astype(F32) for p in range(S)]
        total = as_rows(sum(tails[1:], tails[0]))
        g1_o[...] = total[0:1, :].reshape(R)
        b1_o[...] = total[1:2, :].reshape(R)
        bqv_o[...] = jnp.concatenate([total[2:3, :], total[3:4, :]], 1).reshape(2 * R)

    def shards(tokens, segments, ln1_gain, ln1_bias, w_qkv, bias_qv, w_out, bias_out,
               ln2_gain, ln2_bias, w_in, bias_in, w_down, bias_down, cotangent):
        _, t, D = tokens.shape
        FF = w_in.shape[1]
        L = t * S
        cs = D // S
        R = D // NB
        FJ = FF // (NB * S)
        NF = NB * FJ
        x_own = tokens.reshape(t, D)
        cot_own = cotangent.reshape(t, D)

        wide_u, wide_a = -(-(NF + cs + 8) // 128) * 128, -(-(3 * cs + 8) // 128) * 128
        vec_out = sds((R,), F32)
        v = {}
        token = [None]

        def wait(*names):
            vals = tuple(v[n] for n in names)
            if token[0] is not None:
                vals, _ = lax.optimization_barrier((vals, token[0]))
            return vals

        def kernel(body, outs, args, name, scratch=(), limit=24, us=1):
            return pl.pallas_call(
                body, out_shape=outs, scratch_shapes=list(scratch), name=name,
                cost_estimate=pl.CostEstimate(flops=us * 10**9, bytes_accessed=us * 2 * 10**6, transcendentals=0),
                compiler_params=pltpu.CompilerParams(vmem_limit_bytes=limit * MIB))(*args)

        def prep_qkv():
            v["wq"], = kernel(prep_qkv_kernel, [sds((D, 3 * cs), BF)], [w_qkv], "prep_qkv", us=8)
            token[0] = v["wq"]

        def attn_fwd():
            near, far = sds((t // 2, 2 * cs), BF), sds(((L - t) // 2, 2 * cs), BF)
            v["qkv"], v["lse"], v["row"], v["col"], v["attn"], *sends = kernel(
                attn_fwd_kernel,
                [sds((L, 3 * cs), BF), sds((L, 128), F32), sds((8, L), F32), sds((L, 128), F32), sds((L, cs), BF)]
                + [near] * (S - 1) + [far] * (S - 1),
                v["xs"] + (segments, ln1_gain, ln1_bias, bias_qv) + wait("wq"), "attn_fwd",
                [pltpu.VMEM((1, 3 * cs), F32)], us=6)
            v["nears"] = tuple(exchange(sends[m - 1], "seq", S, m) for m in range(1, S))
            v["far_sends"] = tuple(sends[S - 1:])
            token[0] = v["attn"]

        def cots_send():
            (cot,) = wait("cot")
            v["cots"] = tuple(gather_seq(cot, S))

        def fars_send():
            (sends,) = wait("far_sends")
            v["fars"] = tuple(exchange(sends[m - 1], "seq", S, m) for m in range(1, S))

        def cots(*ks):
            def run():
                got = list(v["cots"])
                vals, _ = lax.optimization_barrier((tuple(got[k] for k in ks), token[0]))
                for k, g in zip(ks, vals):
                    got[k] = g
                v["cots"] = tuple(got)
                token[0] = got[ks[-1]]
            return run

        def turn(name, source):
            def run():
                w = v[source]
                if token[0] is not None:
                    w, _ = lax.optimization_barrier((w, token[0]))
                v[name], = kernel(turn_kernel, [sds(w.shape[::-1], BF)], [w], name, us=2)
                token[0] = v[name]
            return run

        def prep_mlp():
            (w,) = wait("w_in")
            v["win_s"], v["wout_s"], v["wdn_s"], v["bin_s"] = kernel(
                prep_mlp_kernel, [sds((D, NF), BF), sds((D, D), BF), sds((NF, D), BF), sds((1, NF), F32)],
                [w, w_out, w_down, bias_in], "prep_mlp")
            token[0] = v["bin_s"]

        def local():
            (nears,) = wait("nears")
            v["act"], v["x1"], v["dx1"], v["vec"], *both = kernel(
                local_kernel,
                [sds((t, FF), BF), sds((t, D), F32), sds((t, D), F32), sds((8, D), F32)]
                + [sds((t, 2 * cs), BF)] * S,
                (x_own, v["attn"]) + nears + (cot_own, w_out, bias_out, ln2_gain, ln2_bias, w_in, bias_in, v["win_t"], v["wdown_t"]),
                "local", limit=20, us=5)
            v["nears"] = nears
            v["boths"] = (both[0],) + tuple(exchange(both[k], "seq", S, k) for k in range(1, S))
            token[0] = v["dx1"]

        def fars():
            (v["fars"],) = wait("fars")
            token[0] = v["fars"][0]

        def up():
            nears, fars, cots = wait("nears", "fars", "cots")
            v["cots"] = cots
            v["attn_all"], v["h2"], v["slope"], v["d_keep"], v["d_send"] = kernel(
                up_kernel,
                [sds((L, D), BF), sds((L, D), BF), sds((L, NF), F32),
                 sds((NB // 2, FJ, D), BF), sds((NB // 2, FJ, D), BF)],
                v["xs"] + (v["attn"],) + nears + fars + cots
                + (v["wout_s"], bias_out, ln2_gain, ln2_bias, v["win_s"], v["bin_s"]), "up",
                [pltpu.VMEM((L, NF), BF), pltpu.VMEM((L, D), BF), pltpu.VMEM((NB, FJ, D), F32)], 32)
            v["d_got"] = exchange(v["d_send"], "batch", NB, 1)
            token[0] = v["d_keep"]

        def both():
            (v["boths"],) = wait("boths")
            token[0] = v["boths"][1]

        def down():
            boths, h2 = wait("boths", "h2")
            v["u_keep"], v["u_send"] = kernel(
                down_kernel, [sds((NB // 2, R, wide_u), BF), sds((NB // 2, R, wide_u), BF)],
                v["cots"] + boths + (h2, v["slope"], v["wdn_s"], v["attn_all"], v["vec"]), "down",
                [pltpu.VMEM((L, NF), BF), pltpu.VMEM((L, cs), BF), pltpu.VMEM((NB, R, wide_u), F32)], 32)
            v["u_got"] = exchange(v["u_send"], "batch", NB, 1)
            token[0] = v["u_keep"]

        def attn_bwd():
            boths, qkv = wait("boths", "qkv")
            v["own"], v["beside"], away, v["a_keep"], v["a_send"] = kernel(
                attn_bwd_kernel,
                [sds((t, D), F32), sds((t, D), F32), sds((S - 2, t, D), BF),
                 sds((NB // 2, R, wide_a), BF), sds((NB // 2, R, wide_a), BF)],
                v["xs"] + boths + (v["row"], v["col"], ln1_gain, ln1_bias, v["wq"], qkv, v["lse"]), "attn_bwd",
                [pltpu.VMEM((L, D), BF), pltpu.VMEM((L, 3 * cs), BF), pltpu.VMEM((NB, R, wide_a), F32)], 32)
            v["a_got"] = exchange(v["a_send"], "batch", NB, 1)
            v["h_got"] = exchange(away, "seq", S, DH[0])
            token[0] = v["a_keep"]

        def halve(name, level):
            def run():
                got, keep = wait(name + "_got", name + "_keep")
                n = keep.shape[0]
                total = lambda lo, hi: (keep[lo:hi].astype(F32) + got[lo:hi].astype(F32)).astype(BF)
                if n > 1:
                    v[name + "_keep"], send = total(0, n // 2), total(n // 2, n)
                    v[name + "_got"] = exchange(send, "batch", NB, hops[name][level + 1])
                    token[0] = send
                    return
                mine = total(0, 1)[0]
                token[0] = mine
                if GATHER[name] is None:
                    v[name + "_all"] = gather_seq(mine, S)
                    v[name + "_ks"] = [[k] for k in range(S)]
                else:
                    first, second = GATHER[name]
                    v[name + "_all"] = [mine, exchange(mine, "seq", S, first)]
                    v[name + "_ks"] = [[0], [first], [second, first ^ second]]
            return run

        def spread(name):
            def run():
                if GATHER[name] is None:
                    return
                (parts,) = wait(name + "_all")
                pair = jnp.stack(parts)
                v[name + "_all"] = list(parts) + [exchange(pair, "seq", S, GATHER[name][1])]
                token[0] = pair
            return run

        def d_final():
            (parts,) = wait("d_all")
            v["o_wdn"], = kernel(
                functools.partial(down_final_kernel, v["d_ks"]), [sds((S * FJ, D), F32)], parts, "down_final")
            token[0] = v["o_wdn"]

        def u_final():
            (parts,) = wait("u_all")
            v["o_u"] = kernel(
                functools.partial(up_final_kernel, v["u_ks"]),
                [sds((R, FF), F32), sds((R, D), F32)] + [vec_out] * 4 + [sds((S * FJ,), F32)],
                parts, "up_final", [pltpu.VMEM((S, R, wide_u), BF)])
            token[0] = v["o_u"][0]

        def a_final():
            (parts,) = wait("a_all")
            v["o_a"] = kernel(
                functools.partial(att_final_kernel, v["a_ks"]),
                [sds((R, 3 * D), F32), vec_out, vec_out, sds((2 * R,), F32)],
                parts, "att_final", [pltpu.VMEM((S, R, wide_a), BF)])
            token[0] = v["o_a"][0]

        def h_first():
            (got,) = wait("h_got")
            beside = (v["beside"] + got[1].astype(F32)).astype(BF)
            v["own"] = v["own"] + got[0].astype(F32)
            v["h_got"] = exchange(beside, "seq", S, DH[1])
            token[0] = beside

        def h_last():
            (v["h_got"],) = wait("h_got")
            token[0] = v["h_got"]

        def token_grad():
            (got,) = wait("h_got")
            unit1, scale1 = norm_parts(x_own.astype(F32))
            dh1 = v["own"] + got.astype(F32)
            v["d_tokens"] = v["dx1"] + norm_back(dh1, unit1, scale1, ln1_gain)
            token[0] = v["d_tokens"]

        def forward_out():
            x1, act = wait("x1", "act")
            v["out"], = kernel(out_kernel, [sds((t, D), BF)], [x1, act, w_down, bias_down], "out")
            token[0] = v["out"]

        v["xs"] = tuple(gather_seq(x_own, S))
        v["w_in"], v["w_down"], v["cot"] = w_in, w_down, cot_own
        steps = dict(
            pq=prep_qkv, af=attn_fwd, cs=cots_send, fs=fars_send, c1=cots(1), c2=cots(2), c3=cots(3), fa=fars, pm=prep_mlp, t1=turn("wdown_t", "w_down"), t2=turn("win_t", "w_in"), lo=local, up=up, bo=both,
            dn=down, bw=attn_bwd, d0=halve("d", 0), d1=halve("d", 1), d2=halve("d", 2), d3=spread("d"), d4=d_final,
            u0=halve("u", 0), u1=halve("u", 1), u2=halve("u", 2), u3=spread("u"), u4=u_final,
            a0=halve("a", 0), a1=halve("a", 1), a2=halve("a", 2), a3=spread("a"), a4=a_final,
            h1=h_first, h2=h_last, h3=token_grad, ou=forward_out)
        for name in ORDER:
            steps[name]()
        out, d_tokens, o_wdn = v["out"], v["d_tokens"].reshape(tokens.shape), v["o_wdn"]
        o_win, o_wout, o_bout, o_ln2g, o_ln2b, o_bdn, o_bin = v["o_u"]
        o_wqkv, o_ln1g, o_ln1b, o_bqv = v["o_a"]
        return (out.reshape(tokens.shape), d_tokens, o_ln1g, o_ln1b, o_wqkv, o_bqv, o_wout, o_bout,
                o_ln2g, o_ln2b, o_win, o_bin, o_wdn, o_bdn)
    return shards


def make_plain(S, NB):
    def shards(tokens, segments, ln1_gain, ln1_bias, w_qkv, bias_qv, w_out, bias_out,
               ln2_gain, ln2_bias, w_in, bias_in, w_down, bias_down, cotangent):
        rows, t, D = tokens.shape
        FF = w_in.shape[1]
        L = t * S
        hs = HEADS // S
        cs = hs * HEAD_DIM
        R = D // NB
        FJ = FF // (NB * S)
        scale = HEAD_DIM ** (-0.5)
        s = lax.axis_index("seq")
        b = lax.axis_index("batch")
        rel_s = jnp.arange(S, dtype=jnp.int32) ^ s
        rel_b = jnp.arange(NB, dtype=jnp.int32) ^ b

        x_own = tokens.reshape(t, D)
        cot_own = cotangent.reshape(t, D)
        wq_s = lax.dynamic_slice_in_dim(w_qkv.reshape(D, 3, S, cs), s, 1, 2).reshape(D, 3 * cs)
        bq_s = lax.dynamic_slice_in_dim(bias_qv.reshape(2, S, cs), s, 1, 1).reshape(2, cs)
        bqkv_s = jnp.concatenate([bq_s[0], jnp.zeros((cs,), F32), bq_s[1]])
        win_s = lax.dynamic_slice_in_dim(w_in.reshape(D, NB, S, FJ), s, 1, 2).reshape(D, NB * FJ)
        bin_s = lax.dynamic_slice_in_dim(bias_in.reshape(NB, S, FJ), s, 1, 1).reshape(NB * FJ)
        wdn_s = lax.dynamic_slice_in_dim(w_down.reshape(NB, S, FJ, D), s, 1, 1).reshape(NB * FJ, D)
        wout_rel = jnp.take(w_out.reshape(S, cs, D), rel_s, axis=0).reshape(D, D)
        seg_rel = jnp.take(segments.reshape(S, t), rel_s, axis=0).reshape(L)

        x_all = jnp.concatenate(gather_seq(x_own, S), 0)
        cot_in, x_all = lax.optimization_barrier((cot_own, x_all))
        cot_all = jnp.concatenate(gather_seq(cot_in, S), 0)

        x_f = x_all.astype(F32)
        unit1, scale1 = norm_parts(x_f)
        h1 = (unit1 * ln1_gain + ln1_bias).astype(BF)
        qkv = (dot(h1, wq_s) + bqkv_s).astype(BF)
        q = qkv[:, :cs].reshape(L, hs, HEAD_DIM)
        k = qkv[:, cs:2 * cs].reshape(L, hs, HEAD_DIM)
        v = qkv[:, 2 * cs:].reshape(L, hs, HEAD_DIM)
        mask = seg_rel[:, None] == seg_rel[None, :]
        scores = jnp.einsum("qhd,khd->hqk", q, k, preferred_element_type=F32) * scale
        scores = jnp.where(mask[None], scores, -1e30)
        top = jnp.max(scores, axis=-1, keepdims=True)
        expo = jnp.exp(scores - top)
        total = jnp.sum(expo, axis=-1, keepdims=True)
        probs = expo / total
        probs_low = probs.astype(BF)
        attn = jnp.einsum("hqk,khd->qhd", probs_low, v, preferred_element_type=F32).reshape(L, cs).astype(BF)

        got = gather_seq(attn, S)
        blocks = []
        for m, g in enumerate(got):
            g4 = g.reshape(S, t, cs)
            blocks.append(jnp.concatenate([g4[kk ^ m] for kk in range(S)], 0))
        attn_all = jnp.concatenate(blocks, 1)

        x1 = x_f + dot(attn_all, wout_rel) + bias_out
        unit2, scale2 = norm_parts(x1)
        h2 = (unit2 * ln2_gain + ln2_bias).astype(BF)

        u_s = dot(h2, win_s) + bin_s
        act_s, slope_s = gelu_both(u_s)
        act_s = act_s.astype(BF)
        dact_s = dot(cot_all, wdn_s, 1, 1)
        du_s = (dact_s * slope_s).astype(BF)
        g_win = dot(h2, du_s, 0, 0)
        g_wdn = dot(act_s, cot_all, 0, 0)
        g_bin = jnp.sum(du_s.astype(F32), 0)
        mlp = jnp.concatenate([g_win.reshape(NB, R, NB * FJ), g_wdn.reshape(NB, FJ, D)], 1).astype(BF)

        h2o = h2[:t]
        u = dot(h2o, w_in) + bias_in
        act, slope = gelu_both(u)
        act = act.astype(BF)
        activations = (x1[:t] + dot(act, w_down) + bias_down).astype(BF)
        dy = cot_own.astype(F32)
        du = (dot(cot_own, w_down, 1, 1) * slope).astype(BF)
        dh2 = dot(du, w_in, 1, 1)
        g_ln2g = jnp.sum(dh2 * unit2[:t], 0)
        g_ln2b = jnp.sum(dh2, 0)
        dx1 = dy + norm_back(dh2, unit2[:t], scale2[:t], ln2_gain)
        da = dx1.astype(BF)
        g_bout = jnp.sum(da.astype(F32), 0)
        g_bdn = jnp.sum(dy, 0)
        dattn = dot(da, wout_rel, 1, 1).astype(BF)
        da_rel = jnp.take(da.reshape(t, S, cs), rel_s, axis=1)
        both = [jnp.concatenate([dattn[:, kk * cs:(kk + 1) * cs], da_rel[:, kk]], 1) for kk in range(S)]
        both = jnp.concatenate([both[0]] + [exchange(both[kk], "seq", S, kk) for kk in range(1, S)], 0)
        dattn_all = both[:, :cs].reshape(L, hs, HEAD_DIM)
        da_s = both[:, cs:]

        log_total = top + jnp.log(total)
        p = jnp.exp(scores - log_total)
        p_low = p.astype(BF)
        dp = jnp.einsum("qhd,khd->hqk", dattn_all, v, preferred_element_type=F32)
        inner = jnp.sum(p * dp, axis=-1, keepdims=True)
        ds = (p * (dp - inner)).astype(BF)
        dq = jnp.einsum("hqk,khd->qhd", ds, k, preferred_element_type=F32) * scale
        dk = jnp.einsum("hqk,qhd->khd", ds, q, preferred_element_type=F32) * scale
        dv = jnp.einsum("hqk,qhd->khd", p_low, dattn_all, preferred_element_type=F32)
        dqkv = jnp.concatenate([dq.reshape(L, cs), dk.reshape(L, cs), dv.reshape(L, cs)], 1).astype(BF)

        dh1_part = dot(dqkv, wq_s, 1, 1)
        g_ln1g = jnp.sum(dh1_part * unit1, 0)
        g_ln1b = jnp.sum(dh1_part, 0)
        dh1_low = dh1_part.astype(BF)
        dh1 = dh1_part[:t]
        for kk in range(1, S):
            dh1 = dh1 + exchange(dh1_low[kk * t:(kk + 1) * t], "seq", S, kk).astype(F32)
        d_tokens = (dx1 + norm_back(dh1, unit1[:t], scale1[:t], ln1_gain)).reshape(tokens.shape)

        g_wqkv = dot(h1, dqkv, 0, 0)
        g_wout = dot(attn_all, da_s, 0, 0)
        g_wout = jnp.take(g_wout.reshape(S, cs, cs), rel_s, axis=0).reshape(D, cs)
        bsum = jnp.sum(dqkv.astype(F32), 0)
        g_bqv = jnp.zeros((2, S, cs), F32)
        g_bqv = lax.dynamic_update_slice(g_bqv, jnp.stack([bsum[:cs], bsum[2 * cs:]])[:, None], (0, s, 0))
        small = jnp.concatenate(
            [v_.reshape(NB, -1) for v_ in (g_ln1g, g_ln1b, g_bqv, g_bout, g_ln2g, g_ln2b, g_bdn, g_bin)], 1)
        small_n = small.shape[1]
        small_rows = -(-small_n // D)
        pad_rows = -(-small_rows // 16) * 16
        small = jnp.pad(small, ((0, 0), (0, pad_rows * D - small_n))).reshape(NB, pad_rows, D)
        att = jnp.concatenate(
            [jnp.concatenate([g_wqkv.reshape(NB, R, 3 * cs), g_wout.reshape(NB, R, cs)], 2), small], 1).astype(BF)

        def reduce_batch(buf):
            buf = jnp.take(buf, rel_b, axis=0).reshape((NB // 2, 2) + buf.shape[1:])
            buf = (buf[:, 0].astype(F32) + exchange(buf[:, 1], "batch", NB, 1).astype(F32)).astype(BF)
            n = NB // 2
            while n > 4:
                n //= 2
                buf = (buf[:n].astype(F32) + exchange(buf[n:], "batch", NB, 2 * n).astype(F32)).astype(BF)
            acc = buf[0].astype(F32)
            for m in range(1, n):
                acc = acc + exchange(buf[m], "batch", NB, 2 * m).astype(F32)
            parts = jnp.stack(gather_seq(acc.astype(BF), S))
            return jnp.take(parts, rel_s, axis=0).astype(F32)

        mlp = reduce_batch(mlp)
        att = reduce_batch(att)
        o_win = mlp[:, :R].reshape(S, R, NB, FJ).transpose(1, 2, 0, 3).reshape(R, FF)
        o_wdn = mlp[:, R:].reshape(S * FJ, D)
        o_wqkv = att[:, :R, :3 * cs].reshape(S, R, 3, cs).transpose(1, 2, 0, 3).reshape(R, 3 * D)
        o_wout = att[:, :R, 3 * cs:].transpose(1, 0, 2).reshape(R, D)
        flat = att[:, R:].reshape(S, -1)
        o_bin = flat[:, 8 * R:8 * R + FJ].reshape(S * FJ)
        tot = jnp.sum(flat[:, :8 * R], 0)
        o_ln1g, o_ln1b, o_bqv, o_bout, o_ln2g, o_ln2b, o_bdn = (
            tot[:R], tot[R:2 * R], tot[2 * R:4 * R], tot[4 * R:5 * R], tot[5 * R:6 * R], tot[6 * R:7 * R], tot[7 * R:])
        return (activations.reshape(tokens.shape), d_tokens, o_ln1g, o_ln1b, o_wqkv, o_bqv, o_wout, o_bout,
                o_ln2g, o_ln2b, o_win, o_bin, o_wdn, o_bdn)
    return shards


def solution(mesh):
    S, NB = mesh.shape["seq"], mesh.shape["batch"]
    shards = (make if BLOCK_ROWS // NB % 32 == 0 else make_plain)(S, NB)
    rowwise = P("batch", "seq", None)
    placed = (rowwise, P("batch", None)) + (P(),) * 12 + (rowwise,)
    b, bn = P("batch"), P("batch", None)
    return jax.shard_map(
        shards,
        mesh=mesh,
        in_specs=placed,
        out_specs=(rowwise, rowwise, b, b, bn, b, bn, b, b, b, bn, b, bn, b),
        check_vma=False,
    )
```
